32 devices in a mesh: rows: 16 (over z, y, x), seq: 2 (over core).
Axes of the slice: x: 2, y: 2, z: 4, core: 2. Of those that a mesh axis runs over, the one named last changes fastest.
Arguments:
- tokens_a: bfloat16 [64, 512, 768], P('rows', 'seq'), may hold values from -6 to 6
- lengths_a: int32 [64], P('rows'), may hold values from 128 to 512, as said below
- cotangent_a: bfloat16 [64, 512, 768], P('rows', 'seq'), may hold values from -6 to 6
- tokens_b: bfloat16 [128, 256, 768], P('rows', 'seq'), may hold values from -6 to 6
- lengths_b: int32 [128], P('rows'), may hold values from 64 to 256, as said below
- cotangent_b: bfloat16 [128, 256, 768], P('rows', 'seq'), may hold values from -6 to 6
- gain_attn: float32 [768], replicated, may hold values from 0.25 to 1.75
- w_query: bfloat16 [768, 768], replicated, may hold values from -0.0546875 to 0.0546875
- w_key: bfloat16 [768, 768], replicated, may hold values from -0.21875 to 0.21875
- w_value: bfloat16 [768, 768], replicated, may hold values from -0.21875 to 0.21875
- w_out: bfloat16 [768, 768], replicated, may hold values from -0.875 to 0.875
- relative_bias_table: float32 [32, 12], replicated, may hold values from -4 to 4
- gain_ffn: float32 [768], replicated, may hold values from 0.25 to 1.75
- w_in: bfloat16 [768, 3072], replicated, may hold values from -0.21875 to 0.21875
- w_back: bfloat16 [3072, 768], replicated, may hold values from -0.15625 to 0.15625
Outputs:
- out_a: bfloat16 [64, 512, 768], P('rows', 'seq')
- out_b: bfloat16 [128, 256, 768], P('rows', 'seq')
- grad_tokens_a: bfloat16 [64, 512, 768], P('rows', 'seq')
- grad_tokens_b: bfloat16 [128, 256, 768], P('rows', 'seq')
- grad_gain_attn: float32 [768], replicated
- grad_query: float32 [768, 768], P('rows', 'seq')
- grad_key: float32 [768, 768], P('rows', 'seq')
- grad_value: float32 [768, 768], P('rows', 'seq')
- grad_out: float32 [768, 768], P('rows', 'seq')
- grad_table: float32 [32, 12], replicated
- grad_gain_ffn: float32 [768], replicated
- grad_in: float32 [768, 3072], P('rows', 'seq')
- grad_back: float32 [3072, 768], P('rows', 'seq')
The draws below stay inside these ranges and needn't reach their ends.
Inputs may be any that keep to these rules, and one draw needn't show every extreme that they name: `lengths_a`: real tokens of each sequence; keys at positions at or beyond it are padding. In every draw some sequence has exactly 512. `lengths_b`: real tokens of each sequence; keys at positions at or beyond it are padding. In every draw some sequence has exactly 256.
All inputs are finite; a program needn't handle non-finite values.
Results may differ from the reference program's by a relative error of at most 0.015.
Values may be sent and summed in bfloat16 or wider, within the bound.
No kernel may reach another device: no remote copies, remote signals or barrier semaphores. Data moves between devices by JAX's collectives and lax.ppermute only.
A program may use at most 384 MiB of HBM per device.

```python
import jax
import jax.numpy as jnp
from jax import lax

D = 768
HEADS = 12
FF = 3072
BUCKETS = 32
LEN_A = 512
LEN_B = 256
ROWS_A = 64
ROWS_B = 128


def draw_lengths(key, total_rows, longest):
    first_key, second_key = jax.random.split(key)
    drawn = jax.random.randint(first_key, (total_rows,), longest // 4, longest + 1, dtype=jnp.int32)
    chosen = jax.random.randint(second_key, (), 0, total_rows, dtype=jnp.int32)
    return drawn.at[chosen].set(longest)


def draw_lengths_a(key, part):
    return draw_lengths(jax.random.fold_in(key, 11), ROWS_A, LEN_A)


def draw_lengths_b(key, part):
    return draw_lengths(jax.random.fold_in(key, 23), ROWS_B, LEN_B)


def raised(values, own_key, source, target, shards_of, factor):
    def block_of(position):
        return (jnp.arange(values.shape[position]) // (values.shape[position] // shards_of)).reshape((-1,) + (1,) * (values.ndim - 1 - position))

    one_side = jax.random.permutation(own_key, shards_of)[block_of(target)]
    far = (block_of(target) + shards_of // 2) % shards_of
    return jnp.where((block_of(source) == one_side) | (block_of(source) == far), factor * values, values)


def levels(key, dims, cuts, least, high):
    def one(axis_at, parts):
        draws = jax.random.uniform(jax.random.fold_in(jax.random.fold_in(key, 6), axis_at), (parts,), jnp.float32, least / len(cuts), high / len(cuts))
        return jnp.repeat(jnp.exp(draws), dims[axis_at] // parts).reshape((-1,) + (1,) * (len(dims) - axis_at - 1))

    loudness = one(*cuts[0])
    for cut in cuts[1:]:
        loudness = loudness * one(*cut)
    return loudness


def bell_draw(stream_key, shape, scale, limit, cuts=(), kind=jnp.bfloat16):
    values = jax.random.normal(stream_key, shape, jnp.float32) * scale
    if len(cuts) > 0:
        values = levels(stream_key, shape, cuts, -0.22, 0.18) * values
    return jnp.clip(values, min=-limit, max=limit).astype(kind)


def heavy_noise(stream_key, extent, deviation, most, shards, heavy, held_as=jnp.bfloat16):
    values = deviation * jax.random.normal(stream_key, extent, jnp.float32)
    if shards:
        values = values * levels(stream_key, extent, shards, -0.22, 0.18)
    return jnp.clip(raised(values, jax.random.fold_in(stream_key, 3), *heavy), -most, most).astype(held_as)


def setup_inputs(seed: int = 0) -> dict:
    streams_of = jax.random.split(jax.random.key(seed), 16)
    return {
        "tokens_a": bell_draw(streams_of[0], (ROWS_A, LEN_A, D), 1.0, 6.0, ((0, 16), (1, 2))),
        "lengths_a": draw_lengths_a(jax.random.fold_in(streams_of[15], 71), 0),
        "cotangent_a": heavy_noise(streams_of[2], (ROWS_A, LEN_A, D), 1.0, 6.0, ((0, 16), (1, 2)), (0, 2, 16, 2.0)),
        "tokens_b": bell_draw(streams_of[3], (ROWS_B, LEN_B, D), 1.0, 6.0, ((0, 16), (1, 2))),
        "lengths_b": draw_lengths_b(jax.random.fold_in(streams_of[15], 71), 0),
        "cotangent_b": heavy_noise(streams_of[5], (ROWS_B, LEN_B, D), 1.0, 6.0, ((0, 16), (1, 2)), (0, 2, 16, 2.0)),
        "gain_attn": jnp.clip(1.0 + 0.15 * jax.random.normal(streams_of[6], (D,), jnp.float32), 0.25, 1.75),
        "w_query": bell_draw(streams_of[7], (D, D), (16 * D) ** -0.5, 0.0546875),
        "w_key": bell_draw(streams_of[8], (D, D), D ** -0.5, 0.21875),
        "w_value": bell_draw(streams_of[9], (D, D), D ** -0.5, 0.21875),
        "w_out": bell_draw(streams_of[10], (D, D), (D // 16) ** -0.5, 0.875),
        "relative_bias_table": bell_draw(streams_of[11], (BUCKETS, HEADS), 1.0, 4.0, (), jnp.float32),
        "gain_ffn": jnp.clip(1.0 + 0.15 * jax.random.normal(streams_of[12], (D,), jnp.float32), 0.25, 1.75),
        "w_in": bell_draw(streams_of[13], (D, FF), D ** -0.5, 0.21875),
        "w_back": bell_draw(streams_of[14], (FF, D), (FF // 2) ** -0.5, 0.15625),
    }


epsilon = 1e-06
topmost_precision = lax.Precision.HIGHEST
bucket_edges = (12, 16, 23, 32, 46, 64, 91)
masked_score = -1e+30
gelu_coef = 0.7978845608
cubic_coef = 0.044715

@jax.custom_vjp
def low(v):
    return lax.optimization_barrier(v.astype(jnp.bfloat16)).astype(jnp.float32)

@jax.custom_vjp
def low_back(v):
    return v

def low_keep(v):
    return (low(v), None)

def low_pass(kept, grad):
    return (grad,)

def back_keep(v):
    return (v, None)

def back_low(kept, grad):
    return (low(grad),)
low.defvjp(low_keep, low_pass)
low_back.defvjp(back_keep, back_low)

def gelu_tanh(value_in):
    return 0.5 * value_in * (1.0 + jnp.tanh(gelu_coef * (value_in + cubic_coef * value_in * value_in * value_in)))

def bucket_ids(query_pos, key_pos, buckets):
    offset = key_pos[None, :].astype(jnp.int32) - query_pos[:, None].astype(jnp.int32)
    distance = jnp.abs(offset)
    far_part = jnp.full(offset.shape, 8, dtype=jnp.int32)
    for edge_value in bucket_edges:
        far_part = far_part + (distance >= edge_value).astype(jnp.int32)
    near_or_far = jnp.where(distance < 8, distance, far_part).astype(jnp.int32)
    return near_or_far + buckets // 2 * (offset > 0).astype(jnp.int32)

def inv_rms(array_in):
    return lax.rsqrt(lax.optimization_barrier(jnp.mean(array_in * array_in, axis=-1, keepdims=True)) + epsilon)

def exact_einsum(form, left, right, float_type):
    return jnp.einsum(form, left.astype(float_type), right.astype(float_type), precision=topmost_precision)

def layer(tokens_in, params, length_one, bucket_indicator):
    gain_attn, w_query, w_key, w_value, w_out, relative_bias_table, gain_ffn, w_in, w_back = params
    float_type = tokens_in.dtype
    length_now, feature_width = tokens_in.shape
    head_count = relative_bias_table.shape[1]
    head_size = feature_width // head_count
    normed = low(tokens_in * inv_rms(tokens_in) * gain_attn)

    def project(weight_matrix):
        return low(low_back(exact_einsum('ld,de->le', normed, weight_matrix, float_type)))
    query_heads = project(w_query).reshape(length_now, head_count, head_size)
    key_heads = project(w_key).reshape(length_now, head_count, head_size)
    value_heads = project(w_value).reshape(length_now, head_count, head_size)
    raw_scores = low_back(exact_einsum('qhe,khe->hqk', query_heads, key_heads, float_type))
    relative_position_bias = exact_einsum('mfi,mz->zfi', bucket_indicator, relative_bias_table, float_type)
    key_pos = jnp.arange(length_now, dtype=jnp.int32)
    key_live = (key_pos < length_one.astype(jnp.int32))[None, None, :]
    masked_fill = jnp.full(raw_scores.shape, masked_score, dtype=float_type)
    scores = jnp.where(key_live, raw_scores + relative_position_bias, masked_fill)
    row_max = lax.optimization_barrier(jnp.max(scores, axis=-1, keepdims=True))
    exp_scores = jnp.exp(scores - row_max)
    attn_probs = low(exp_scores / lax.optimization_barrier(jnp.sum(exp_scores, axis=-1, keepdims=True)))
    attn_mixed = exact_einsum('hqk,khe->qhe', attn_probs, value_heads, float_type)
    attn_mixed = low(low_back(attn_mixed.reshape(length_now, feature_width)))
    hidden = tokens_in + low_back(exact_einsum('ld,de->le', attn_mixed, w_out, float_type))
    normed_two = low(hidden * inv_rms(hidden) * gain_ffn)
    inner_pre = low_back(exact_einsum('ld,df->lf', normed_two, w_in, float_type))
    inner_low = low(gelu_tanh(inner_pre))
    return hidden + exact_einsum('lf,fd->ld', inner_low, w_back, float_type)

def run_bucket(tokens, lengths, cotangent, params):
    length_now = tokens.shape[1]
    float_type = params[0].dtype
    positions = jnp.arange(length_now, dtype=jnp.int32)
    bucket_range = jnp.arange(BUCKETS, dtype=jnp.int32)[:, None, None]
    bucket_indicator = (bucket_ids(positions, positions, BUCKETS)[None] == bucket_range).astype(float_type)

    def step_one(carried, pieces):
        tok_one, len_one, cot_one = pieces

        def forward(tokens_in, weights_in):
            return layer(tokens_in, weights_in, len_one, bucket_indicator)
        layer_out, pullback = jax.vjp(forward, tok_one.astype(float_type), params)
        grad_tok, grad_weights = pullback(cot_one.astype(float_type))
        carried = jax.tree.map(jnp.add, carried, grad_weights)
        return (carried, (layer_out.astype(jnp.bfloat16), grad_tok.astype(jnp.bfloat16)))
    start_grads = jax.tree.map(jnp.zeros_like, params)
    grad_total, (outs_all, grads_all) = lax.scan(step_one, start_grads, (tokens, lengths.astype(jnp.int32), cotangent))
    return (outs_all, grads_all, grad_total)

def reference(tokens_a, lengths_a, cotangent_a, tokens_b, lengths_b, cotangent_b, gain_attn, w_query, w_key, w_value, w_out, relative_bias_table, gain_ffn, w_in, w_back):
    params = tuple((weight_arg.astype(jnp.float32) for weight_arg in (gain_attn, w_query, w_key, w_value, w_out, relative_bias_table, gain_ffn, w_in, w_back)))
    out_a, grad_a, sums_a = run_bucket(tokens_a, lengths_a, cotangent_a, params)
    out_b, grad_b, sums_b = run_bucket(tokens_b, lengths_b, cotangent_b, params)
    grads = jax.tree.map(jnp.add, sums_a, sums_b)
    return (out_a, out_b, grad_a, grad_b, grads[0], grads[1], grads[2], grads[3], grads[4], grads[5], grads[6], grads[7], grads[8])
```

```python
import functools

import jax
import jax.numpy as jnp
from jax import lax
from jax.experimental import pallas as pl
from jax.experimental.pallas import tpu as pltpu
from jax.sharding import PartitionSpec as P

EPS = 1e-06
EDGES = (12, 16, 23, 32, 46, 64, 91)
MASKED = -1e30
C1 = 0.7978845608
C3 = 0.044715
BF = jnp.bfloat16
F32 = jnp.float32
HEAD = 64
PAIR = 2 * HEAD
MIB = 1 << 20


def dot(a, b, ca, cb):
    return lax.dot_general(a, b, (((ca,), (cb,)), ((), ())), preferred_element_type=F32)


def exact(a, b):
    return lax.dot_general(
        a, b, (((1,), (0,)), ((), ())), precision=lax.Precision.HIGHEST, preferred_element_type=F32
    )


def sds(shape, dtype):
    return jax.ShapeDtypeStruct(shape, dtype)


def call(kernel, grid, in_specs, out_specs, out_shape, scratch=(), flops=0, nbytes=0, vmem=60):
    return pl.pallas_call(
        kernel,
        grid_spec=pltpu.PrefetchScalarGridSpec(
            num_scalar_prefetch=1,
            grid=grid,
            in_specs=in_specs,
            out_specs=out_specs,
            scratch_shapes=list(scratch),
        ),
        out_shape=out_shape,
        compiler_params=pltpu.CompilerParams(vmem_limit_bytes=vmem * MIB),
        cost_estimate=pl.CostEstimate(flops=int(flops), bytes_accessed=int(nbytes), transcendentals=0),
    )


def whole(shape):
    return pl.BlockSpec(shape, lambda *_: (0,) * len(shape))


def bucket_of(rel, buckets):
    n = jnp.abs(rel)
    far = jnp.full(rel.shape, 8, jnp.int32)
    for edge in EDGES:
        far = far + (n >= edge).astype(jnp.int32)
    return jnp.where(n < 8, n, far) + jnp.where(rel > 0, buckets // 2, 0)


def strip_kernel(meta, table, strip, *, base, buckets, head_count):
    rows = strip.shape[1]
    rel = lax.broadcasted_iota(jnp.int32, (rows, 128), 0) - base - lax.broadcasted_iota(jnp.int32, (rows, 128), 1)
    ids = bucket_of(rel, buckets)
    h = pl.program_id(0)
    acc = jnp.zeros((rows, 128), F32)
    for b in range(buckets):
        acc = jnp.where(ids == b, table[b, h], acc)
    strip[0] = acc


def qkv_kernel(meta, x_ref, gain, wq, wk, wv, normed, q, k, v):
    x = x_ref[0].astype(F32)
    r = lax.rsqrt(jnp.mean(x * x, axis=-1, keepdims=True) + EPS)
    n = (x * r * gain[...]).astype(BF)
    normed[0] = n
    q[0] = dot(n, wq[...], 1, 0).astype(BF)
    k[0] = dot(n, wk[...], 1, 0).astype(BF)
    v[0] = dot(n, wv[...], 1, 0).astype(BF)


def units_of(na, la, nb, lb):
    out = [(0, s, la, s * la // 2) for s in range(na)]
    return out + [(1, s, lb, na * la // 2 + s * lb // 2) for s in range(nb)]


def joined(ref, off, half):
    return jnp.concatenate([ref[0, off : off + half, :], ref[1, off : off + half, :]], axis=0)


def strip_rows(flip, base, size, cb, kh):
    half = size // 2
    plain = base - 128 * cb + half * kh
    if flip is None:
        return plain
    moved = (128 * cb + half) % size
    return pl.multiple_of(jnp.where(flip == 0, plain, base - moved + half * (1 - kh)), 128)


def lanes_of(shape, high):
    lane = lax.broadcasted_iota(jnp.int32, shape, len(shape) - 1)
    return (lane >= HEAD) == high


def half_mask(high):
    return jnp.where(lanes_of((1, PAIR), high), 1.0, 0.0).astype(BF)


def attn_kernel(meta, q, k, v, strip, pa, pb, attn, kaug, *, dims, base):
    na, la, nb, lb = dims
    flip = meta[0]

    @pl.when(pl.program_id(0) == 0)
    def _():
        for kind, s, size, off in units_of(*dims):
            half = size // 2
            for kh in range(2):
                row = lax.broadcasted_iota(jnp.int32, (half, 128), 0)
                start = jnp.where(flip == 0, half * kh, half * (1 - kh))
                length = meta[2 + (s if kind == 0 else na + s)]
                lane = lax.broadcasted_iota(jnp.int32, (half, 128), 1)
                gone = jnp.logical_and(row + start >= length, lane == 0)
                kaug[kh, off : off + half, :] = jnp.where(gone, MASKED, 0.0).astype(BF)

    for kind, s, size, off in units_of(*dims):
        half = size // 2
        pref = pa if kind == 0 else pb
        q2, k2, v2 = joined(q, off, half), joined(k, off, half), joined(v, off, half)
        v2t = v2.T
        ones = jnp.where(lax.broadcasted_iota(jnp.int32, (size, 128), 1) == 0, 1.0, 0.0).astype(BF)
        qa = jnp.concatenate([q2, ones], axis=1)
        ka = joined(kaug, off, half)
        mixed = []
        for h in range(2):
            kk = jnp.concatenate([k2 * half_mask(h == 1), ka], axis=1)
            for c2 in range(size // 256):
                scores = dot(kk, qa[256 * c2 : 256 * c2 + 256], 1, 1)
                for sub in range(2):
                    cb = 2 * c2 + sub
                    bias = jnp.concatenate(
                        [strip[h, pl.ds(strip_rows(flip, base, size, cb, kh), half), :] for kh in range(2)], axis=0
                    )
                    one = scores[:, 128 * sub : 128 * sub + 128] + bias
                    e = jnp.exp(one - jnp.max(one, axis=0, keepdims=True))
                    p = e * (1.0 / jnp.sum(e, axis=0, keepdims=True))
                    pref[h, s, :, 128 * cb : 128 * cb + 128] = p.astype(BF)
            mixed.append(dot(v2t[HEAD * h : HEAD * h + HEAD], pref[h, s], 1, 0))
        o = jnp.concatenate(mixed, axis=0).T.astype(BF)
        attn[0, off : off + half, :] = o[:half]
        attn[1, off : off + half, :] = o[half:]


def mix_kernel(meta, attn, x, w_out, gain, hidden, normed):
    h = x[0].astype(F32) + dot(attn[0], w_out[...], 1, 0)
    r = lax.rsqrt(jnp.mean(h * h, axis=-1, keepdims=True) + EPS)
    hidden[0] = h
    normed[0] = (h * r * gain[...]).astype(BF)


def ffn_kernel(meta, normed, g, w_in, w_back, low, d_inner, *, step):
    for part in range(2):
        for lo in range(0, normed.shape[1], step):
            rows = slice(lo, lo + step)
            v = dot(normed[part, rows, :], w_in[...], 1, 0)
            gw = dot(g[part, rows, :], w_back[...], 1, 1)
            u = v * v
            t = jnp.tanh(v * (C1 + (C1 * C3) * u))
            up = 0.5 + 0.5 * t
            low[part, rows, :] = (v * up).astype(BF)
            slope = up + v * (0.5 - 0.5 * (t * t)) * (C1 + (3.0 * C1 * C3) * u)
            d_inner[part, rows, :] = (gw * slope).astype(BF)


def flat(ref):
    a = ref[...]
    return a.reshape(a.shape[0] * a.shape[1], a.shape[2])


def split_columns(meta, value, send, keep):
    half = value.shape[1] // 2
    lo, hi = value[:, :half].astype(BF), value[:, half:].astype(BF)
    first = meta[1] == 0

    @pl.when(first)
    def _():
        keep[...] = lo
        send[...] = hi

    @pl.when(jnp.logical_not(first))
    def _():
        keep[...] = hi
        send[...] = lo


def back_grad_kernel(meta, low, g, send, keep):
    split_columns(meta, dot(flat(low), flat(g), 0, 0), send, keep)


def in_grad_kernel(meta, normed, d_inner, send, keep):
    value = dot(flat(normed), flat(d_inner), 0, 0).astype(BF)
    sending = pl.program_id(0) < pl.num_programs(0) // 2

    @pl.when(sending)
    def _():
        send[...] = value

    @pl.when(jnp.logical_not(sending))
    def _():
        keep[...] = value


def rows8(value):
    return jnp.sum(value.reshape(value.shape[0] // 8, 8, value.shape[1]), axis=0)


def hidden_kernel(meta, d_inner, w_in, hidden, g, gain, w_out, attn, d_hidden, d_attn, small, send, keep, acc):
    i, last = pl.program_id(0), pl.num_programs(0) - 1
    dn = dot(d_inner[0], w_in[...], 1, 1)
    h = hidden[0]
    r = lax.rsqrt(jnp.mean(h * h, axis=-1, keepdims=True) + EPS)
    gained = dn * gain[...]
    mean = jnp.mean(gained * h, axis=-1, keepdims=True)
    dh = (g[0].astype(F32) + r * gained - h * (r * r * r * mean)).astype(BF)
    d_hidden[0] = dh
    d_attn[0] = dot(dh, w_out[...], 1, 1).astype(BF)
    part = rows8(dn * h * r)
    product = dot(attn[0], dh, 0, 0)

    @pl.when(i == 0)
    def _():
        small[...] = part
        acc[...] = product

    @pl.when(i > 0)
    def _():
        small[...] += part
        acc[...] += product

    @pl.when(i == last)
    def _():
        split_columns(meta, acc[...], send, keep)


def table_sums(acc, base, buckets):
    near0, near1 = base - 96, base + 224
    near = acc[near0:near1, :]
    rel = (near0 - base) + lax.broadcasted_iota(jnp.int32, near.shape, 0) - lax.broadcasted_iota(jnp.int32, near.shape, 1)
    far_plus = jnp.sum(acc[near1:, :], axis=0, keepdims=True) + jnp.sum(
        jnp.where(rel >= 128, near, 0.0), axis=0, keepdims=True
    )
    far_minus = jnp.sum(acc[:near0, :], axis=0, keepdims=True) + jnp.sum(
        jnp.where(rel <= -128, near, 0.0), axis=0, keepdims=True
    )
    inner = jnp.where(jnp.abs(rel) < 128, near, 0.0)
    lanes = (128, 128)
    mirror = lax.broadcasted_iota(jnp.int32, lanes, 0) + lax.broadcasted_iota(jnp.int32, lanes, 1) == 127
    inner = exact(inner, mirror.astype(F32))
    wide = jnp.concatenate([inner, jnp.zeros_like(inner)], axis=1)
    turned = pltpu.roll(wide, 0, 1, stride=1, stride_axis=0)
    line = jnp.sum(turned, axis=0, keepdims=True)
    lane = lax.broadcasted_iota(jnp.int32, (256, 128), 0)
    back = ((lane + near0 - base - 127 + 128 + 512) & 255) - 128
    hot = jnp.logical_and(
        bucket_of(back, buckets) == lax.broadcasted_iota(jnp.int32, (256, 128), 1), back > -128
    ).astype(F32)
    sums = exact(jnp.broadcast_to(line, (8, 256)), hot)[:1]
    out = lax.broadcasted_iota(jnp.int32, (1, 128), 1)
    sums = sums + jnp.where(out == buckets - 1, jnp.sum(far_plus, axis=1, keepdims=True), 0.0)
    return sums + jnp.where(out == buckets // 2 - 1, jnp.sum(far_minus, axis=1, keepdims=True), 0.0)


def attn_back_kernel(
    meta, q, k, v, do, pa, pb, normed, dq, dk, dv, table, send, keep, strip, dsa, dsb, cat, *, dims, base, buckets
):
    flip = meta[0]
    step = pl.program_id(0)
    th = normed.shape[1]
    strip[...] = jnp.zeros_like(strip)
    for kind, s, size, off in units_of(*dims):
        half = size // 2
        pref = pa if kind == 0 else pb
        ds_ref = dsa if kind == 0 else dsb
        q2, k2, v2, o2 = (joined(ref, off, half) for ref in (q, k, v, do))
        k2t = k2.T
        dvs, dks, dqs = [], [], []
        for h in range(2):
            mask = half_mask(h == 1)
            vm = v2 * mask
            for c2 in range(size // 256):
                dp = dot(vm, o2[256 * c2 : 256 * c2 + 256], 1, 1)
                for sub in range(2):
                    cb = 2 * c2 + sub
                    cols = slice(128 * cb, 128 * cb + 128)
                    p = pref[h, s, :, cols].astype(F32)
                    dpc = dp[:, 128 * sub : 128 * sub + 128]
                    delta = jnp.sum(p * dpc, axis=0, keepdims=True)
                    ds = p * (dpc - delta)
                    for kh in range(2):
                        at = pl.ds(strip_rows(flip, base, size, cb, kh), half)
                        strip[h, at, :] += ds[half * kh : half * kh + half]
                    ds_ref[:, cols] = ds.astype(BF)
            dvs.append(dot(pref[h, s], o2 * mask, 1, 0))
            dks.append(dot(ds_ref[...], q2 * mask, 1, 0))
            dqs.append(dot(k2t[HEAD * h : HEAD * h + HEAD], ds_ref[...], 1, 0))
        d_v = (dvs[0] + dvs[1]).astype(BF)
        d_k = (dks[0] + dks[1]).astype(BF)
        d_q = jnp.concatenate(dqs, axis=0).T.astype(BF)
        for part in range(2):
            rows = slice(off, off + half)
            got = slice(part * half, part * half + half)
            dq[part, rows, :] = d_q[got]
            dk[part, rows, :] = d_k[got]
            dv[part, rows, :] = d_v[got]
            at = slice(part * th + off, part * th + off + half)
            cat[step, at, 0:128] = d_q[got]
            cat[step, at, 128:256] = d_k[got]
            cat[step, at, 256:384] = d_v[got]
    rows = [table_sums(strip.at[h], base, buckets) for h in range(2)]
    table[0] = jnp.concatenate(rows + [jnp.zeros((6, 128), F32)], axis=0)

    @pl.when(step == 1)
    def _():
        both = jnp.concatenate([cat[0], cat[1]], axis=1)
        value = dot(flat(normed), both, 0, 0).astype(BF)
        send[...] = value[:, :384]
        keep[...] = value[:, 384:]


def out_kernel(meta, low, w_back, hidden, out):
    out[0] = (hidden[0] + dot(low[0], w_back[...], 1, 0)).astype(BF)


def tokens_kernel(meta, dq, dk, dv, wq, wk, wv, x_ref, d_hidden, gain, grad, small):
    i = pl.program_id(0)
    dn = dot(dq[0], wq[...], 1, 1) + dot(dk[0], wk[...], 1, 1) + dot(dv[0], wv[...], 1, 1)
    x = x_ref[0].astype(F32)
    r = lax.rsqrt(jnp.mean(x * x, axis=-1, keepdims=True) + EPS)
    gained = dn * gain[...]
    mean = jnp.mean(gained * x, axis=-1, keepdims=True)
    grad[0] = (d_hidden[0].astype(F32) + r * gained - x * (r * r * r * mean)).astype(BF)
    part = rows8(dn * x * r)

    @pl.when(i == 0)
    def _():
        small[...] = part

    @pl.when(i > 0)
    def _():
        small[...] += part


def swap(x, axis, bit):
    n = lax.axis_size(axis)
    return lax.ppermute(x, axis, [(i, i ^ bit) for i in range(n)])


def halve(x, bit_pos):
    bit = (lax.axis_index("rows") >> bit_pos) & 1
    axis = x.ndim - 3 - bit_pos
    mine = lax.dynamic_index_in_dim(x, bit, axis, keepdims=True)
    other = lax.dynamic_index_in_dim(x, 1 - bit, axis, keepdims=True)
    got = swap(other, "rows", 1 << bit_pos)
    return mine.astype(F32) + got.astype(F32)


def scatter_rows(x, order):
    n = lax.axis_size("rows")
    bits = n.bit_length() - 1
    x = x.reshape((2,) * bits + (x.shape[0] // n, x.shape[1]))
    for i, b in enumerate(order):
        x = halve(x, b)
        if i < bits - 1:
            x = x.astype(BF)
    return x.reshape(x.shape[-2:])


def body(
    tokens_a, lengths_a, cotangent_a, tokens_b, lengths_b, cotangent_b,
    gain_attn, w_query, w_key, w_value, w_out, relative_bias_table, gain_ffn, w_in, w_back,
):
    nseq, nrows = lax.axis_size("seq"), lax.axis_size("rows")
    c = lax.axis_index("seq")
    width = tokens_a.shape[2]
    ff = w_in.shape[1]
    buckets, head_count = relative_bias_table.shape
    la, lb = tokens_a.shape[1] * nseq, tokens_b.shape[1] * nseq
    na, nb = tokens_a.shape[0] // nseq, tokens_b.shape[0] // nseq
    dims = (na, la, nb, lb)
    th = (na * la + nb * lb) // 2
    tokens = 2 * th
    base = la - 128
    strip_len = 2 * la - 128
    pairs = head_count // 2
    paired = nseq == 2

    if paired:
        me = c
        flip = c

        def regroup(a, b):
            def pick(x, n, which):
                got = lax.dynamic_slice_in_dim(x, which * n, n, 0)
                return got.reshape(-1, width)

            own = jnp.concatenate([pick(a, na, c), pick(b, nb, c)], axis=0)
            give = jnp.concatenate([pick(a, na, 1 - c), pick(b, nb, 1 - c)], axis=0)
            return jnp.stack([own, swap(give, "seq", 1)])

        def ungroup(x):
            own, got = x[0], swap(x[1], "seq", 1)
            cut = na * la // 2
            first = c == 0

            def place(o, g, n, size):
                o, g = o.reshape(n, size, width), g.reshape(n, size, width)
                return jnp.concatenate([jnp.where(first, o, g), jnp.where(first, g, o)], axis=0)

            return place(own[:cut], got[:cut], na, la // 2), place(own[cut:], got[cut:], nb, lb // 2)

    else:
        me = jnp.int32(0)
        flip = jnp.int32(0)

        def regroup(a, b):
            def one(x):
                got = lax.all_to_all(x, "seq", 0, 1, tiled=True)
                n, size, _ = got.shape
                return got.reshape(n, 2, size // 2, width).transpose(1, 0, 2, 3).reshape(2, -1, width)

            return jnp.concatenate([one(a), one(b)], axis=1)

        def ungroup(x):
            cut = na * la // 2

            def one(y, n, size):
                y = y.reshape(2, n, size // 2, width).transpose(1, 0, 2, 3).reshape(n, size, width)
                return lax.all_to_all(y, "seq", 1, 0, tiled=True)

            return one(x[:, :cut], na, la), one(x[:, cut:], nb, lb)

    own_a = lax.dynamic_slice_in_dim(lengths_a, c * na, na, 0)
    own_b = lax.dynamic_slice_in_dim(lengths_b, c * nb, nb, 0)
    meta = jnp.concatenate([jnp.stack([flip, me]).astype(jnp.int32), own_a, own_b])
    x = regroup(tokens_a, tokens_b)
    g = regroup(cotangent_a, cotangent_b)
    gain1, gain2 = gain_attn[None], gain_ffn[None]

    tile = min(512, th)
    per = th // tile
    row_grid = (2 * per,)
    by_row = lambda w: pl.BlockSpec((1, tile, w), lambda i, m: (i // per, i % per, 0))
    dense = 2 * tokens * width

    strip = call(
        functools.partial(strip_kernel, base=base, buckets=buckets, head_count=head_count),
        (head_count,),
        [pl.BlockSpec(memory_space=pltpu.SMEM)],
        pl.BlockSpec((1, strip_len, 128), lambda h, m: (h, 0, 0)),
        sds((head_count, strip_len, 128), F32),
        flops=1e9,
        nbytes=4 * head_count * strip_len * 128,
    )(meta, relative_bias_table)

    tok = sds((2, th, width), BF)
    normed, q, k, v = call(
        qkv_kernel,
        row_grid,
        [by_row(width), whole((1, width))] + [whole((width, width))] * 3,
        [by_row(width)] * 4,
        [tok] * 4,
        flops=3 * dense * width,
        nbytes=10 * tokens * width,
    )(meta, x, gain1, w_query, w_key, w_value)

    by_pair = pl.BlockSpec((2, th, PAIR), lambda p, m: (0, 0, p))
    pa_shape, pb_shape = (head_count, na, la, la), (head_count, nb, lb, lb)
    score_macs = head_count * (na * la * la + nb * lb * lb)
    pa, pb, attn = call(
        functools.partial(attn_kernel, dims=dims, base=base),
        (pairs,),
        [by_pair] * 3 + [pl.BlockSpec((2, strip_len, 128), lambda p, m: (p, 0, 0))],
        [
            pl.BlockSpec((2, na, la, la), lambda p, m: (p, 0, 0, 0)),
            pl.BlockSpec((2, nb, lb, lb), lambda p, m: (p, 0, 0, 0)),
            by_pair,
        ],
        [sds(pa_shape, BF), sds(pb_shape, BF), tok],
        scratch=[pltpu.VMEM((2, th, 128), BF)],
        flops=score_macs * 256 * 4,
        nbytes=2 * score_macs,
    )(meta, q, k, v, strip)

    hidden, normed2 = call(
        mix_kernel,
        row_grid,
        [by_row(width), by_row(width), whole((width, width)), whole((1, width))],
        [by_row(width)] * 2,
        [sds((2, th, width), F32), tok],
        flops=dense * width,
        nbytes=10 * tokens * width,
    )(meta, attn, x, w_out, gain2)

    all_tok = whole((2, th, width))
    fb = 512
    by_ff = pl.BlockSpec((2, th, fb), lambda f, m: (0, 0, f))
    wide = sds((2, th, ff), BF)
    low, d_inner = call(
        functools.partial(ffn_kernel, step=min(512, th)),
        (ff // fb,),
        [
            all_tok,
            all_tok,
            pl.BlockSpec((width, fb), lambda f, m: (0, f)),
            pl.BlockSpec((fb, width), lambda f, m: (f, 0)),
        ],
        [by_ff, by_ff],
        [wide, wide],
        flops=2 * dense * ff,
        nbytes=4 * tokens * ff,
    )(meta, normed2, g, w_in, w_back)

    half_w, half_f = width // 2, ff // 2
    back_send, back_keep = call(
        back_grad_kernel,
        (ff // fb,),
        [by_ff, all_tok],
        [pl.BlockSpec((fb, half_w), lambda f, m: (f, 0))] * 2,
        [sds((ff, half_w), BF)] * 2,
        flops=dense * ff,
        nbytes=2 * tokens * ff,
    )(meta, low, g)

    nf = ff // fb
    in_send, in_keep = call(
        in_grad_kernel,
        (nf,),
        [all_tok, pl.BlockSpec((2, th, fb), lambda f, m: (0, 0, (f + (1 - m[1]) * (nf // 2)) % nf))],
        [
            pl.BlockSpec((width, fb), lambda f, m: (0, jnp.minimum(f, nf // 2 - 1))),
            pl.BlockSpec((width, fb), lambda f, m: (0, jnp.maximum(f - nf // 2, 0))),
        ],
        [sds((width, half_f), BF)] * 2,
        flops=dense * ff,
        nbytes=2 * tokens * ff,
    )(meta, normed2, d_inner)

    small = sds((8, width), F32)
    d_hidden, d_attn, small_ffn, out_send, out_keep = call(
        hidden_kernel,
        row_grid,
        [
            by_row(ff),
            whole((width, ff)),
            by_row(width),
            by_row(width),
            whole((1, width)),
            whole((width, width)),
            by_row(width),
        ],
        [by_row(width), by_row(width), whole((8, width)), whole((width, half_w)), whole((width, half_w))],
        [tok, tok, small, sds((width, half_w), BF), sds((width, half_w), BF)],
        scratch=[pltpu.VMEM((width, width), F32)],
        flops=dense * (ff + 2 * width),
        nbytes=2 * tokens * ff,
    )(meta, d_inner, w_in, hidden, g, gain2, w_out, attn)

    def seq_sum(send, keep, dim):
        if paired:
            return (keep.astype(F32) + swap(send, "seq", 1).astype(F32)).astype(BF)
        return jnp.concatenate([keep, send], axis=dim)

    back_part = seq_sum(back_send, back_keep, 1)
    in_part = seq_sum(in_send, in_keep, 1)
    out_part = seq_sum(out_send, out_keep, 1)

    group_count = pairs // 2
    groups, dqs, tables = [], [], []
    for gi in range(group_count):

        def pair_at(s, m, gi=gi):
            return jnp.where(s == 0, 1 - m[1], m[1]) * group_count + gi

        def half_at(s, m):
            return jnp.where(s == 0, 1 - m[1], m[1])

        by_cols = pl.BlockSpec((2, th, PAIR), lambda s, m, f=pair_at: (0, 0, f(s, m)))
        to_cols = pl.BlockSpec((2, th, PAIR), lambda s, m: (0, 0, half_at(s, m)))
        dq, dk, dv, table, send, keep = call(
            functools.partial(attn_back_kernel, dims=dims, base=base, buckets=buckets),
            (2,),
            [by_cols] * 4
            + [
                pl.BlockSpec((2, na, la, la), lambda s, m, f=pair_at: (f(s, m), 0, 0, 0)),
                pl.BlockSpec((2, nb, lb, lb), lambda s, m, f=pair_at: (f(s, m), 0, 0, 0)),
                all_tok,
            ],
            [to_cols] * 3
            + [
                pl.BlockSpec((1, 8, 128), lambda s, m: (half_at(s, m), 0, 0)),
                whole((width, 3 * PAIR)),
                whole((width, 3 * PAIR)),
            ],
            [sds((2, th, 2 * PAIR), BF)] * 3
            + [sds((2, 8, 128), F32), sds((width, 3 * PAIR), BF), sds((width, 3 * PAIR), BF)],
            scratch=[
                pltpu.VMEM((2, strip_len, 128), F32),
                pltpu.VMEM((la, la), BF),
                pltpu.VMEM((lb, lb), BF),
                pltpu.VMEM((2, tokens, 3 * PAIR), BF),
            ],
            flops=score_macs * 256 * 8 // 3 + dense * width,
            nbytes=2 * score_macs // 3,
        )(meta, q, k, v, d_attn, pa, pb, normed)
        dqs.append((dq, dk, dv))
        tables.append(table)
        if paired:
            groups.append(seq_sum(send, keep, 1))
        else:
            groups.append((keep, send))

    out_parts = call(
        out_kernel,
        row_grid,
        [by_row(ff), whole((ff, width)), by_row(width)],
        by_row(width),
        tok,
        flops=dense * ff,
        nbytes=2 * tokens * ff,
    )(meta, low, w_back, hidden)
    out_a, out_b = ungroup(out_parts)

    def joined_cols(which):
        pieces = [d[which] for d in dqs]
        return jnp.concatenate([p[:, :, :PAIR] for p in pieces] + [p[:, :, PAIR:] for p in pieces], axis=2)

    grads, small_attn = call(
        tokens_kernel,
        row_grid,
        [by_row(width)] * 3 + [whole((width, width))] * 3 + [by_row(width), by_row(width), whole((1, width))],
        [by_row(width), whole((8, width))],
        [tok, small],
        flops=3 * dense * width,
        nbytes=14 * tokens * width,
    )(meta, joined_cols(0), joined_cols(1), joined_cols(2), w_query, w_key, w_value, x, d_hidden, gain1)
    grad_a, grad_b = ungroup(grads)

    table_local = jnp.stack([t[:, :2, :buckets] for t in tables], axis=1).reshape(head_count, buckets).T
    gain_one, table_sum, gain_two = lax.psum(
        (jnp.sum(small_attn, axis=0), table_local, jnp.sum(small_ffn, axis=0)), ("rows", "seq")
    )

    if paired:
        bits = nrows.bit_length() - 1
        orders = [tuple(range(bits)), (1, 0) + tuple(range(2, bits))]
        g_back = jnp.concatenate(
            [scatter_rows(back_part[:, s], o) for s, o in zip((slice(0, 128), slice(128, None)), orders)], axis=1
        )
        g_in = jnp.concatenate(
            [scatter_rows(in_part[:, s], o) for s, o in zip((slice(0, 768), slice(768, None)), orders)], axis=1
        )
        g_out = scatter_rows(out_part, orders[0])
        qkv = [scatter_rows(part, orders[i % 2]) for i, part in enumerate(groups)]
        g_q, g_k, g_v = (
            jnp.concatenate([part[:, PAIR * i : PAIR * i + PAIR] for part in qkv], axis=1) for i in range(3)
        )
    else:

        def reduce(x):
            x = lax.psum_scatter(x.astype(F32), "rows", scatter_dimension=0, tiled=True)
            return lax.psum_scatter(x.astype(BF), "seq", scatter_dimension=1, tiled=True).astype(F32)

        g_back, g_in, g_out = reduce(back_part), reduce(in_part), reduce(out_part)
        g_q, g_k, g_v = (
            reduce(
                jnp.concatenate([part[s][:, PAIR * i : PAIR * i + PAIR] for s in range(2) for part in groups], axis=1)
            )
            for i in range(3)
        )
    return (
        out_a, out_b, grad_a, grad_b, gain_one, g_q, g_k, g_v, g_out, table_sum, gain_two, g_in, g_back,
    )


def solution(mesh):
    split = P("rows", "seq", None)
    placed = (split, P("rows"), split, split, P("rows"), split) + (P(),) * 9
    shard = P("rows", "seq")
    return jax.shard_map(
        body,
        mesh=mesh,
        in_specs=placed,
        out_specs=(split, split, split, split, P(), shard, shard, shard, shard, P(), P(), shard, shard),
        check_vma=False,
    )
```

```python
import functools

import jax
import jax.numpy as jnp
from jax import lax
from jax.experimental import pallas as pl
from jax.experimental.pallas import tpu as pltpu
from jax.sharding import PartitionSpec as P

EPS = 1e-06
EDGES = (12, 16, 23, 32, 46, 64, 91)
MASKED = -1e30
C1 = 0.7978845608
C3 = 0.044715
BF = jnp.bfloat16
F32 = jnp.float32
HEAD = 64
PAIR = 2 * HEAD
MIB = 1 << 20


def dot(a, b, ca, cb):
    return lax.dot_general(a, b, (((ca,), (cb,)), ((), ())), preferred_element_type=F32)


def exact(a, b):
    return lax.dot_general(
        a, b, (((1,), (0,)), ((), ())), precision=lax.Precision.HIGHEST, preferred_element_type=F32
    )


def sds(shape, dtype):
    return jax.ShapeDtypeStruct(shape, dtype)


def call(kernel, grid, in_specs, out_specs, out_shape, scratch=(), flops=0, nbytes=0, vmem=60, after=(), free=()):
    count, extra = len(in_specs), len(after)

    def run(meta, *refs):
        kernel(meta, *refs[:count], *refs[count + extra :])

    def large(x):
        return x.size * x.dtype.itemsize >= MIB

    def put(x):
        return pltpu.HBM(x.shape, x.dtype) if large(x) else x

    in_specs = list(in_specs) + [pl.BlockSpec(memory_space=pl.ANY)] * extra
    made = pl.pallas_call(
        run,
        grid_spec=pltpu.PrefetchScalarGridSpec(
            num_scalar_prefetch=1,
            grid=grid,
            in_specs=in_specs,
            out_specs=out_specs,
            scratch_shapes=list(scratch),
        ),
        out_shape=[put(x) for x in out_shape] if isinstance(out_shape, list) else put(out_shape),
        compiler_params=pltpu.CompilerParams(vmem_limit_bytes=vmem * MIB),
        cost_estimate=pl.CostEstimate(flops=int(flops), bytes_accessed=int(nbytes), transcendentals=0),
    )

    def place(i, x):
        return pltpu.with_memory_space_constraint(x, pltpu.HBM) if large(x) and i not in free else x

    return lambda *args: made(*(place(i, x) for i, x in enumerate((*args, *after))))


def whole(shape):
    return pl.BlockSpec(shape, lambda *_: (0,) * len(shape))


def bucket_of(rel, buckets):
    n = jnp.abs(rel)
    far = jnp.full(rel.shape, 8, jnp.int32)
    for edge in EDGES:
        far = far + (n >= edge).astype(jnp.int32)
    return jnp.where(n < 8, n, far) + jnp.where(rel > 0, buckets // 2, 0)


def strip_kernel(meta, table, strip, *, base, buckets):
    near0, near1 = base - 96, base + 224
    lane = lax.broadcasted_iota(jnp.int32, (256, 128), 0)
    rel = ((near0 - base - lane + 128 + 512) & 255) - 128
    hot = (bucket_of(rel, buckets) == lax.broadcasted_iota(jnp.int32, (256, 128), 1)).astype(F32)
    row = table[0]
    line = lax.dot_general(
        row, hot, (((1,), (1,)), ((), ())), precision=lax.Precision.HIGHEST, preferred_element_type=F32
    )
    wide = jnp.broadcast_to(line[:1], (near1 - near0, 256))
    near = pltpu.roll(wide, 0, 1, stride=1, stride_axis=0)[:, :128]
    rel = (
        near0 - base + lax.broadcasted_iota(jnp.int32, near.shape, 0) - lax.broadcasted_iota(jnp.int32, near.shape, 1)
    )
    minus, plus = row[:1, buckets // 2 - 1 : buckets // 2], row[:1, buckets - 1 : buckets]
    strip[0, near0:near1, :] = jnp.where(rel >= EDGES[-1], plus, jnp.where(rel <= -EDGES[-1], minus, near))
    strip[0, :near0, :] = jnp.broadcast_to(minus, (near0, 128))
    strip[0, near1:, :] = jnp.broadcast_to(plus, (strip.shape[1] - near1, 128))


def qkv_kernel(meta, x_ref, gain, wq, wk, wv, normed, q, k, v):
    x = x_ref[0].astype(F32)
    r = lax.rsqrt(jnp.mean(x * x, axis=-1, keepdims=True) + EPS)
    n = (x * r * gain[...]).astype(BF)
    normed[0] = n
    q[0] = dot(n, wq[...], 1, 0).astype(BF)
    k[0] = dot(n, wk[...], 1, 0).astype(BF)
    v[0] = dot(n, wv[...], 1, 0).astype(BF)


def units_of(na, la, nb, lb):
    out = [(0, s, la, s * la // 2) for s in range(na)]
    return out + [(1, s, lb, na * la // 2 + s * lb // 2) for s in range(nb)]


def joined(ref, off, half):
    return jnp.concatenate([ref[0, off : off + half, :], ref[1, off : off + half, :]], axis=0)


def strip_rows(flip, base, size, cb, kh):
    half = size // 2
    plain = base - 128 * cb + half * kh
    if flip is None:
        return plain
    moved = (128 * cb + half) % size
    return pl.multiple_of(jnp.where(flip == 0, plain, base - moved + half * (1 - kh)), 128)


def lanes_of(shape, high):
    lane = lax.broadcasted_iota(jnp.int32, shape, len(shape) - 1)
    return (lane >= HEAD) == high


def half_mask(high):
    return jnp.where(lanes_of((1, PAIR), high), 1.0, 0.0).astype(BF)


def attn_kernel(meta, q, k, v, strip, pa, pb, attn, linv, kaug, *, dims, base):
    na, la, nb, lb = dims
    flip = meta[0]

    @pl.when(pl.program_id(0) == 0)
    def _():
        for kind, s, size, off in units_of(*dims):
            half = size // 2
            for kh in range(2):
                row = lax.broadcasted_iota(jnp.int32, (half, 128), 0)
                start = jnp.where(flip == 0, half * kh, half * (1 - kh))
                length = meta[3 + (s if kind == 0 else na + s)]
                lane = lax.broadcasted_iota(jnp.int32, (half, 128), 1)
                gone = jnp.logical_and(row + start >= length, lane == 0)
                kaug[kh, off : off + half, :] = jnp.where(gone, MASKED, 0.0).astype(BF)

    low_lanes = lax.broadcasted_iota(jnp.int32, (1, PAIR), 1) < HEAD
    for kind, s, size, off in units_of(*dims):
        half = size // 2
        pref = pa if kind == 0 else pb
        q2, k2, v2 = joined(q, off, half), joined(k, off, half), joined(v, off, half)
        first = jnp.where(lax.broadcasted_iota(jnp.int32, (size, 128), 1) == 0, 1.0, 0.0).astype(BF)
        ones = jnp.ones((size, 128), BF)
        qa = jnp.concatenate([q2, first], axis=1)
        ka = joined(kaug, off, half)
        mixed, inverse = [], []
        for h in range(2):
            kk = jnp.concatenate([k2 * half_mask(h == 1), ka], axis=1)
            for c2 in range(size // 256):
                scores = dot(kk, qa[256 * c2 : 256 * c2 + 256], 1, 1)
                for sub in range(2):
                    cb = 2 * c2 + sub
                    bias = jnp.concatenate(
                        [strip[h, pl.ds(strip_rows(flip, base, size, cb, kh), half), :] for kh in range(2)], axis=0
                    )
                    one = scores[:, 128 * sub : 128 * sub + 128] + bias
                    e = jnp.exp(one - jnp.max(one, axis=0, keepdims=True))
                    pref[h, s, :, 128 * cb : 128 * cb + 128] = e.astype(BF)
            va = jnp.concatenate([v2 * half_mask(h == 1), ones], axis=1)
            both = dot(pref[h, s], va, 0, 0)
            inv = 1.0 / both[:, PAIR:]
            mixed.append(both[:, :PAIR] * inv)
            inverse.append(inv)
        o = (mixed[0] + mixed[1]).astype(BF)
        inv = jnp.where(low_lanes, inverse[0], inverse[1]).astype(BF)
        attn[0, off : off + half, :] = o[:half]
        attn[1, off : off + half, :] = o[half:]
        linv[0, off : off + half, :] = inv[:half]
        linv[1, off : off + half, :] = inv[half:]


def mix_kernel(meta, attn, x, w_out, gain, hidden, normed):
    h = x[0].astype(F32) + dot(attn[0], w_out[...], 1, 0)
    r = lax.rsqrt(jnp.mean(h * h, axis=-1, keepdims=True) + EPS)
    hidden[0] = h
    normed[0] = (h * r * gain[...]).astype(BF)


def ffn_kernel(meta, normed, g, w_in, w_back, low, d_inner, *, step):
    for part in range(2):
        for lo in range(0, normed.shape[1], step):
            rows = slice(lo, lo + step)
            v = dot(normed[part, rows, :], w_in[...], 1, 0)
            gw = dot(g[part, rows, :], w_back[...], 1, 1)
            u = v * v
            t = jnp.tanh(v * (C1 + (C1 * C3) * u))
            up = 0.5 + 0.5 * t
            low[part, rows, :] = (v * up).astype(BF)
            slope = up + v * (0.5 - 0.5 * (t * t)) * (C1 + (3.0 * C1 * C3) * u)
            d_inner[part, rows, :] = (gw * slope).astype(BF)


def flat(ref):
    a = ref[...]
    return a.reshape(a.shape[0] * a.shape[1], a.shape[2])


def split_columns(meta, value, send, keep):
    half = value.shape[1] // 2
    lo, hi = value[:, :half].astype(BF), value[:, half:].astype(BF)
    first = meta[1] == 0

    @pl.when(first)
    def _():
        keep[...] = lo
        send[...] = hi

    @pl.when(jnp.logical_not(first))
    def _():
        keep[...] = hi
        send[...] = lo


def back_grad_kernel(meta, low, g, send, keep):
    split_columns(meta, dot(flat(low), flat(g), 0, 0), send, keep)


def in_grad_kernel(meta, normed, d_inner, send, keep):
    value = dot(flat(normed), flat(d_inner), 0, 0).astype(BF)
    sending = pl.program_id(0) < pl.num_programs(0) // 2

    @pl.when(sending)
    def _():
        send[...] = value

    @pl.when(jnp.logical_not(sending))
    def _():
        keep[...] = value


def rows8(value):
    return jnp.sum(value.reshape(value.shape[0] // 8, 8, value.shape[1]), axis=0)


def hidden_kernel(meta, d_inner, w_in, hidden, g, gain, w_out, attn, linv, d_hidden, d_attn, small, send, keep, acc):
    i, last = pl.program_id(0), pl.num_programs(0) - 1
    dn = dot(d_inner[0], w_in[...], 1, 1)
    h = hidden[0]
    r = lax.rsqrt(jnp.mean(h * h, axis=-1, keepdims=True) + EPS)
    gained = dn * gain[...]
    mean = jnp.mean(gained * h, axis=-1, keepdims=True)
    dh = (g[0].astype(F32) + r * gained - h * (r * r * r * mean)).astype(BF)
    d_hidden[0] = dh
    d_attn[0] = (dot(dh, w_out[...], 1, 1) * linv[0].astype(F32)).astype(BF)
    part = rows8(dn * h * r)
    product = dot(attn[0], dh, 0, 0)

    @pl.when(i == 0)
    def _():
        small[...] = part
        acc[...] = product

    @pl.when(i > 0)
    def _():
        small[...] += part
        acc[...] += product

    @pl.when(i == last)
    def _():
        split_columns(meta, acc[...], send, keep)


def table_sums(strip, hot, base, buckets):
    near0, near1 = base - 96, base + 224
    lines, ends = [], []
    for h in range(strip.shape[0]):
        near = strip[h, near0:near1, :]
        rel = (
            near0 - base + lax.broadcasted_iota(jnp.int32, near.shape, 0) - lax.broadcasted_iota(jnp.int32, near.shape, 1)
        )
        plus = rows8(strip[h, near1:, :]) + rows8(jnp.where(rel >= 128, near, 0.0))
        minus = rows8(strip[h, :near0, :]) + rows8(jnp.where(rel <= -128, near, 0.0))
        wide = jnp.where(jnp.abs(rel) < 128, near, 0.0)
        wide = jnp.concatenate([wide, jnp.zeros_like(wide)], axis=1)
        line = jnp.zeros((8, 256), F32)
        for r in range(0, near1 - near0, 8):
            line = line + pltpu.roll(wide[r : r + 8], -r % 256, 1)
        one = jnp.zeros((8, 256), F32)
        row = lax.broadcasted_iota(jnp.int32, (8, 256), 0)
        for r in range(8):
            one = one + pltpu.roll(jnp.where(row == r, line, 0.0), -r % 256, 1)
        lines.append(jnp.sum(one, axis=0, keepdims=True))
        ends.append((jnp.sum(plus, keepdims=True), jnp.sum(minus, keepdims=True)))
    fill = [jnp.zeros((8 - len(lines), 256), F32)]
    sums = exact(jnp.concatenate(lines + fill, axis=0), hot[...])
    lane = lax.broadcasted_iota(jnp.int32, (8, 128), 1)
    row = lax.broadcasted_iota(jnp.int32, (8, 128), 0)
    for h, (plus, minus) in enumerate(ends):
        here = row == h
        sums = sums + jnp.where(jnp.logical_and(here, lane == buckets - 1), plus, 0.0)
        sums = sums + jnp.where(jnp.logical_and(here, lane == buckets // 2 - 1), minus, 0.0)
    return sums


def attn_back_kernel(
    meta, q, k, v, do, at_ref, pa, pb, normed, wqs, wks, wvs, wqk, wkk, wvk, hot,
    dq, dk, dv, table, send, keep, gain, strip, dsa, dsb, cat, *, dims, base, buckets
):
    flip = meta[0]
    step = pl.program_id(0)
    th = normed.shape[1]
    strip[...] = jnp.zeros_like(strip)
    lane = lax.broadcasted_iota(jnp.int32, (1, PAIR), 1)
    minus = jnp.where(lane < 2, -1.0, 0.0).astype(BF)
    for kind, s, size, off in units_of(*dims):
        half = size // 2
        pref = pa if kind == 0 else pb
        ds_ref = dsa if kind == 0 else dsb
        q2, k2, v2, o2, a2 = (joined(ref, off, half) for ref in (q, k, v, do, at_ref))
        prod = o2.astype(F32) * a2.astype(F32)
        dvs, dks, dqs = [], [], []
        for h in range(2):
            mask = half_mask(h == 1)
            delta = jnp.sum(jnp.where((lane >= HEAD) == (h == 1), prod, 0.0), axis=1, keepdims=True)
            high = delta.astype(BF).astype(F32)
            cols = jnp.where(lane == 0, high, jnp.where(lane == 1, delta - high, 0.0)).astype(BF)
            va = jnp.concatenate([v2 * mask, jnp.broadcast_to(minus, (size, PAIR))], axis=1)
            oa = jnp.concatenate([o2, cols], axis=1)
            for c2 in range(size // 256):
                dp = dot(va, oa[256 * c2 : 256 * c2 + 256], 1, 1)
                for sub in range(2):
                    cb = 2 * c2 + sub
                    cs = slice(128 * cb, 128 * cb + 128)
                    ds = pref[h, s, :, cs].astype(F32) * dp[:, 128 * sub : 128 * sub + 128]
                    for kh in range(2):
                        at = pl.ds(strip_rows(flip, base, size, cb, kh), half)
                        strip[h, at, :] += ds[half * kh : half * kh + half]
                    ds_ref[h, :, cs] = ds.astype(BF)
            dvs.append(dot(pref[h, s], o2 * mask, 1, 0))
            dks.append(dot(ds_ref[h], q2 * mask, 1, 0))
            dqs.append(dot(ds_ref[h], k2 * mask, 0, 0))
        d_v = (dvs[0] + dvs[1]).astype(BF)
        d_k = (dks[0] + dks[1]).astype(BF)
        d_q = (dqs[0] + dqs[1]).astype(BF)
        for part in range(2):
            rows = slice(off, off + half)
            got = slice(part * half, part * half + half)
            dq[part, rows, :] = d_q[got]
            dk[part, rows, :] = d_k[got]
            dv[part, rows, :] = d_v[got]
            at = slice(part * th + off, part * th + off + half)
            cat[step, at, 0:128] = d_q[got]
            cat[step, at, 128:256] = d_k[got]
            cat[step, at, 256:384] = d_v[got]
    table[0] = table_sums(strip, hot, base, buckets)

    @pl.when(step == 1)
    def _():
        both = jnp.concatenate([cat[0], cat[1]], axis=1)
        value = dot(flat(normed), both, 0, 0)
        send[...] = value[:, :384].astype(BF)
        keep[...] = value[:, 384:].astype(BF)
        gain[...] = sum(
            value[:, 128 * i : 128 * i + 128] * w[...].astype(F32) for i, w in enumerate((wqs, wks, wvs, wqk, wkk, wvk))
        )


def out_kernel(meta, low, w_back, hidden, out):
    out[0] = (hidden[0] + dot(low[0], w_back[...], 1, 0)).astype(BF)


def tokens_kernel(meta, *refs):
    (wq, wk, wv, x_ref, d_hidden, gain, grad) = refs[9:]

    def columns(of):
        return jnp.concatenate([r[0, :, :PAIR] for r in of] + [r[0, :, PAIR:] for r in of], axis=1)

    dq, dk, dv = columns(refs[0:3]), columns(refs[3:6]), columns(refs[6:9])
    dn = dot(dq, wq[...], 1, 1) + dot(dk, wk[...], 1, 1) + dot(dv, wv[...], 1, 1)
    x = x_ref[0].astype(F32)
    r = lax.rsqrt(jnp.mean(x * x, axis=-1, keepdims=True) + EPS)
    gained = dn * gain[...]
    mean = jnp.mean(gained * x, axis=-1, keepdims=True)
    grad[0] = (d_hidden[0].astype(F32) + r * gained - x * (r * r * r * mean)).astype(BF)


def swap(x, axis, bit):
    n = lax.axis_size(axis)
    return lax.ppermute(x, axis, [(i, i ^ bit) for i in range(n)])


class Piece:
    def __init__(self, parts, bits_left):
        self.parts, self.left = parts, bits_left

    @property
    def block(self):
        return sum(terms[0].shape[-2] for terms in self.parts), self.parts[0][0].shape[-1]


def blocks(x, bits):
    return x.reshape((2,) * bits + (x.shape[0] >> bits, x.shape[1]))


def masks_of(bits):
    return [tuple((m >> i) & 1 for i in range(len(bits))) for m in range(1 << len(bits))]


def shuttle(meta, work, whole_sums, finals, after):
    pieces, results = finals
    ins, outs = [], []
    for piece in [p for p, _ in work] + pieces:
        for terms in piece.parts:
            ins.extend(terms)
    for terms in whole_sums:
        ins.extend(terms)
    for piece, bits in work:
        lead = (2,) * (len(piece.left) - len(bits))
        outs.extend([sds(lead + piece.block, BF)] * (1 << len(bits)))
    for spans in results:
        outs.append(sds((spans[0][2], sum(s[4] for s in spans)), F32))
    outs.extend(sds(terms[0].shape, F32) for terms in whole_sums)

    def kernel(meta, *refs):
        got, put = list(refs[: len(ins)]), list(refs[len(ins) :])
        row = meta[2]

        def take(terms, index):
            return sum(ref[index].astype(F32) for ref in terms)

        def parts_of(piece):
            return [[got.pop(0) for _ in terms] for terms in piece.parts]

        for piece, bits in work:
            parts = parts_of(piece)
            for mask in masks_of(bits):
                out = put.pop(0)
                rest = [b for b in piece.left if b not in bits]
                for m in range(1 << len(rest)):
                    chosen = {b: (m >> i) & 1 for i, b in enumerate(rest)}
                    place = tuple(chosen[b] for b in reversed(rest))
                    for b, flip in zip(bits, mask):
                        chosen[b] = ((row >> b) & 1) ^ flip
                    index = tuple(chosen[b] for b in reversed(piece.left))
                    low = 0
                    for terms in parts:
                        value = take(terms, index).astype(BF)
                        out[place + (slice(low, low + value.shape[0]),)] = value
                        low += value.shape[0]
        sums = [[take(terms, ...) for terms in parts_of(piece)] for piece in pieces]
        sums = [jnp.concatenate(v, axis=0) if len(v) > 1 else v[0] for v in sums]
        for spans in results:
            out, low = put.pop(0), 0
            for piece, r0, r, c0, c in spans:
                out[:, low : low + c] = sums[piece][r0 : r0 + r, c0 : c0 + c]
                low += c
        for terms in whole_sums:
            put.pop(0)[...] = take([got.pop(0) for _ in terms], ...)

    made = call(
        kernel,
        (1,),
        [whole(x.shape) for x in ins],
        [whole(x.shape) for x in outs],
        outs,
        nbytes=sum(x.size * 2 for x in ins),
        vmem=30,
        after=after,
    )(meta, *ins)
    made = list(made)
    waits = list(made)
    for piece, bits in work:
        terms = []
        for mask in masks_of(bits):
            part = made.pop(0)
            wide = sum(flip << b for flip, b in zip(mask, bits))
            terms.append(swap(part, "rows", wide) if wide else part)
        piece.parts = [terms]
        piece.left = tuple(b for b in piece.left if b not in bits)
    return made[: len(results)], made[len(results) :], waits


def body(
    tokens_a, lengths_a, cotangent_a, tokens_b, lengths_b, cotangent_b,
    gain_attn, w_query, w_key, w_value, w_out, relative_bias_table, gain_ffn, w_in, w_back,
):
    nseq, nrows = lax.axis_size("seq"), lax.axis_size("rows")
    c = lax.axis_index("seq")
    width = tokens_a.shape[2]
    ff = w_in.shape[1]
    buckets, head_count = relative_bias_table.shape
    la, lb = tokens_a.shape[1] * nseq, tokens_b.shape[1] * nseq
    na, nb = tokens_a.shape[0] // nseq, tokens_b.shape[0] // nseq
    dims = (na, la, nb, lb)
    th = (na * la + nb * lb) // 2
    tokens = 2 * th
    base = la - 128
    strip_len = 2 * la - 128
    pairs = head_count // 2
    paired = nseq == 2 and nrows == 16

    if paired:
        me = c
        flip = c

        def regroup(a, b):
            def pick(x, n, which):
                got = lax.dynamic_slice_in_dim(x, which * n, n, 0)
                return got.reshape(-1, width)

            own = jnp.concatenate([pick(a, na, c), pick(b, nb, c)], axis=0)
            give = jnp.concatenate([pick(a, na, 1 - c), pick(b, nb, 1 - c)], axis=0)
            return jnp.stack([own, swap(give, "seq", 1)])

        def ungroup(own, give):
            got = swap(give, "seq", 1)
            cut = na * la // 2
            first = c == 0

            def place(o, g, n, size):
                o, g = o.reshape(n, size, width), g.reshape(n, size, width)
                return jnp.concatenate([jnp.where(first, o, g), jnp.where(first, g, o)], axis=0)

            return place(own[:cut], got[:cut], na, la // 2), place(own[cut:], got[cut:], nb, lb // 2)

    else:
        me = jnp.int32(0)
        flip = jnp.int32(0)

        def regroup(a, b):
            def one(x):
                got = lax.all_to_all(x, "seq", 0, 1, tiled=True)
                n, size, _ = got.shape
                return got.reshape(n, 2, size // 2, width).transpose(1, 0, 2, 3).reshape(2, -1, width)

            return jnp.concatenate([one(a), one(b)], axis=1)

        def ungroup(own, give):
            x = jnp.stack([own, give])
            cut = na * la // 2

            def one(y, n, size):
                y = y.reshape(2, n, size // 2, width).transpose(1, 0, 2, 3).reshape(n, size, width)
                return lax.all_to_all(y, "seq", 1, 0, tiled=True)

            return one(x[:, :cut], na, la), one(x[:, cut:], nb, lb)

    own_a = lax.dynamic_slice_in_dim(lengths_a, c * na, na, 0)
    own_b = lax.dynamic_slice_in_dim(lengths_b, c * nb, nb, 0)
    meta = jnp.concatenate([jnp.stack([flip, me, lax.axis_index("rows")]).astype(jnp.int32), own_a, own_b])
    x = regroup(tokens_a, tokens_b)
    g = regroup(cotangent_a, cotangent_b)
    gain1, gain2 = gain_attn[None], gain_ffn[None]

    tile = min(512, th)
    per = th // tile
    row_grid = (2 * per,)
    by_row = lambda w: pl.BlockSpec((1, tile, w), lambda i, m: (i // per, i % per, 0))
    dense = 2 * tokens * width

    rows_of_table = jnp.broadcast_to(
        jnp.pad(relative_bias_table.T, ((0, 0), (0, 128 - buckets)))[:, None], (head_count, 8, 128)
    )
    strip = call(
        functools.partial(strip_kernel, base=base, buckets=buckets),
        (head_count,),
        [pl.BlockSpec((1, 8, 128), lambda h, m: (h, 0, 0))],
        pl.BlockSpec((1, strip_len, 128), lambda h, m: (h, 0, 0)),
        sds((head_count, strip_len, 128), F32),
        vmem=8,
        flops=1e9,
        nbytes=4 * head_count * strip_len * 128,
    )(meta, rows_of_table)

    tok = sds((2, th, width), BF)
    normed, q, k, v = call(
        qkv_kernel,
        row_grid,
        [by_row(width), whole((1, width))] + [whole((width, width))] * 3,
        [by_row(width)] * 4,
        [tok] * 4,
        free=(3, 4, 5),
        vmem=24,
        flops=3 * dense * width,
        nbytes=10 * tokens * width,
    )(meta, x, gain1, w_query, w_key, w_value)

    by_pair = pl.BlockSpec((2, th, PAIR), lambda p, m: (0, 0, p))
    pa_shape, pb_shape = (head_count, na, la, la), (head_count, nb, lb, lb)
    score_macs = head_count * (na * la * la + nb * lb * lb)
    pa, pb, attn, linv = call(
        functools.partial(attn_kernel, dims=dims, base=base),
        (pairs,),
        [by_pair] * 3 + [pl.BlockSpec((2, strip_len, 128), lambda p, m: (p, 0, 0))],
        [
            pl.BlockSpec((2, na, la, la), lambda p, m: (p, 0, 0, 0)),
            pl.BlockSpec((2, nb, lb, lb), lambda p, m: (p, 0, 0, 0)),
            by_pair,
            by_pair,
        ],
        [sds(pa_shape, BF), sds(pb_shape, BF), tok, tok],
        scratch=[pltpu.VMEM((2, th, 128), BF)],
        vmem=34,
        flops=score_macs * 256 * 4,
        nbytes=2 * score_macs,
    )(meta, q, k, v, strip)

    hidden, normed2 = call(
        mix_kernel,
        row_grid,
        [by_row(width), by_row(width), whole((width, width)), whole((1, width))],
        [by_row(width)] * 2,
        [sds((2, th, width), F32), tok],
        free=(3,),
        vmem=24,
        flops=dense * width,
        nbytes=10 * tokens * width,
    )(meta, attn, x, w_out, gain2)

    all_tok = whole((2, th, width))
    fb = 512
    by_ff = pl.BlockSpec((2, th, fb), lambda f, m: (0, 0, f))
    wide = sds((2, th, ff), BF)
    low, d_inner = call(
        functools.partial(ffn_kernel, step=min(512, th)),
        (ff // fb,),
        [
            all_tok,
            all_tok,
            pl.BlockSpec((width, fb), lambda f, m: (0, f)),
            pl.BlockSpec((fb, width), lambda f, m: (f, 0)),
        ],
        [by_ff, by_ff],
        [wide, wide],
        free=(3, 4),
        vmem=44,
        flops=2 * dense * ff,
        nbytes=4 * tokens * ff,
    )(meta, normed2, g, w_in, w_back)

    half_w, half_f = width // 2, ff // 2
    back_send, back_keep = call(
        back_grad_kernel,
        (ff // fb,),
        [by_ff, all_tok],
        [pl.BlockSpec((fb, half_w), lambda f, m: (f, 0))] * 2,
        [sds((ff, half_w), BF)] * 2,
        vmem=30,
        flops=dense * ff,
        nbytes=2 * tokens * ff,
    )(meta, low, g)

    bit_count = nrows.bit_length() - 1
    low_bits, high_bits = (0, 1), tuple(range(2, bit_count))
    every_bit = tuple(range(bit_count))

    def pair_sum(keep, send):
        return [blocks(keep, bit_count), blocks(swap(send, "seq", 1), bit_count)]

    hold = []
    if paired:
        back = Piece([pair_sum(back_keep, back_send)], every_bit)
        hold = [back_send]
    nf = ff // fb
    in_send, in_keep = call(
        in_grad_kernel,
        (nf,),
        [all_tok, pl.BlockSpec((2, th, fb), lambda f, m: (0, 0, (f + (1 - m[1]) * (nf // 2)) % nf))],
        [
            pl.BlockSpec((width, fb), lambda f, m: (0, jnp.minimum(f, nf // 2 - 1))),
            pl.BlockSpec((width, fb), lambda f, m: (0, jnp.maximum(f - nf // 2, 0))),
        ],
        [sds((width, half_f), BF)] * 2,
        vmem=30,
        flops=dense * ff,
        nbytes=2 * tokens * ff,
        after=hold,
    )(meta, normed2, d_inner)

    small = sds((8, width), F32)
    none = ([], [])
    if paired:
        inner = Piece([pair_sum(in_keep, in_send)], every_bit)
        _, _, hold = shuttle(meta, [(back, (0,))], [], none, [in_send])
        hold.append(in_send)
    d_hidden, d_attn, small_ffn, out_send, out_keep = call(
        hidden_kernel,
        row_grid,
        [
            by_row(ff),
            whole((width, ff)),
            by_row(width),
            by_row(width),
            whole((1, width)),
            whole((width, width)),
            by_row(width),
            by_row(width),
        ],
        [by_row(width), by_row(width), whole((8, width)), whole((width, half_w)), whole((width, half_w))],
        [tok, tok, small, sds((width, half_w), BF), sds((width, half_w), BF)],
        scratch=[pltpu.VMEM((width, width), F32)],
        free=(2, 6),
        vmem=44,
        flops=dense * (ff + 2 * width),
        nbytes=2 * tokens * ff,
        after=hold,
    )(meta, d_inner, w_in, hidden, g, gain2, w_out, attn, linv)

    group_count = pairs // 2
    lane = jnp.arange(256, dtype=jnp.int32)
    back_rel = ((-96 - lane + 128 + 512) & 255) - 128
    hot = jnp.logical_and(
        bucket_of(back_rel, buckets)[:, None] == jnp.arange(128, dtype=jnp.int32)[None], back_rel[:, None] > -128
    ).astype(F32)
    groups, dqs, tables, gains = [], [], [], []
    for gi in range(group_count):
        if paired:
            if gi == 0:
                out_sum = pair_sum(out_keep, out_send)
                _, _, hold = shuttle(meta, [(inner, (0,)), (back, (1,))], [], none, [d_attn])
                hold.append(out_send)
            elif gi == 1:
                first = Piece([out_sum, pair_sum(*groups[0])], every_bit)
                _, _, hold = shuttle(meta, [(back, (2,))], [], none, [dqs[0][0]])
                hold.append(groups[0][1])
            else:
                _, _, hold = shuttle(meta, [(inner, (1,)), (first, (0,)), (back, (3,))], [], none, [dqs[1][0]])
                second = pair_sum(*groups[1])
                hold.append(groups[1][1])

        def pair_at(s, m, gi=gi):
            return jnp.where(s == 0, 1 - m[1], m[1]) * group_count + gi

        def half_at(s, m):
            return jnp.where(s == 0, 1 - m[1], m[1])

        by_cols = pl.BlockSpec((2, th, PAIR), lambda s, m, f=pair_at: (0, 0, f(s, m)))
        to_cols = pl.BlockSpec((2, th, PAIR), lambda s, m: (0, 0, half_at(s, m)))
        weight_cols = [
            pl.BlockSpec((width, PAIR), lambda s, m, f=pair_at, at=at: (0, f(at, m))) for at in (0, 0, 0, 1, 1, 1)
        ]
        dq, dk, dv, table, send, keep, gain = call(
            functools.partial(attn_back_kernel, dims=dims, base=base, buckets=buckets),
            (2,),
            [by_cols] * 5
            + [
                pl.BlockSpec((2, na, la, la), lambda s, m, f=pair_at: (f(s, m), 0, 0, 0)),
                pl.BlockSpec((2, nb, lb, lb), lambda s, m, f=pair_at: (f(s, m), 0, 0, 0)),
                all_tok,
            ]
            + weight_cols
            + [whole((256, 128))],
            [to_cols] * 3
            + [
                pl.BlockSpec((1, 8, 128), lambda s, m: (half_at(s, m), 0, 0)),
                whole((width, 3 * PAIR)),
                whole((width, 3 * PAIR)),
                whole((width, 128)),
            ],
            [sds((2, th, 2 * PAIR), BF)] * 3
            + [
                sds((2, 8, 128), F32),
                sds((width, 3 * PAIR), BF),
                sds((width, 3 * PAIR), BF),
                sds((width, 128), F32),
            ],
            scratch=[
                pltpu.VMEM((2, strip_len, 128), F32),
                pltpu.VMEM((2, la, la), BF),
                pltpu.VMEM((2, lb, lb), BF),
                pltpu.VMEM((2, tokens, 3 * PAIR), BF),
            ],
            vmem=44,
        flops=score_macs * 256 * 8 // 3 + dense * width,
            nbytes=2 * score_macs // 3,
            after=hold,
        )(meta, q, k, v, d_attn, attn, pa, pb, normed, *([w_query, w_key, w_value] * 2), hot)
        dqs.append((dq, dk, dv))
        tables.append(table)
        gains.append(gain)
        groups.append((keep, send))

    table_local = jnp.stack([t[:, :2, :buckets] for t in tables], axis=1).reshape(head_count, buckets).T
    gain_local = jnp.sum(sum(gains), axis=1) / gain_attn
    small_sum = jnp.concatenate([gain_local, jnp.sum(small_ffn, axis=0), table_local.reshape(-1)]).reshape(-1, 128)
    if paired:
        last = Piece([second, pair_sum(*groups[2])], every_bit)
        smalls = [small_sum, swap(small_sum, "seq", 1)]
        back_rows = back.block
        (g_back,), _, hold = shuttle(
            meta,
            [(inner, (2,)), (first, (1,))],
            [],
            ([back], [[(0, 0, back_rows[0], 0, back_rows[1])]]),
            [dqs[2][0]],
        )
        hold += [groups[2][1], small_sum]

    out_parts = call(
        out_kernel,
        row_grid,
        [by_row(ff), whole((ff, width)), by_row(width)],
        by_row(width),
        tok,
        free=(2,),
        vmem=34,
        flops=dense * ff,
        nbytes=2 * tokens * ff,
        after=hold,
    )(meta, low, w_back, hidden)

    if paired:
        _, (small_part,), hold = shuttle(
            meta, [(inner, (3,)), (first, (2,)), (last, low_bits)], [smalls], none, [out_parts]
        )
        smalls = [small_part] + [swap(small_part, "rows", m) for m in (1, 2, 3)]

    def token_grads(part):
        of_part = lambda w: pl.BlockSpec((1, tile, w), lambda i, m: (part, i, 0))
        return call(
            tokens_kernel,
            (per,),
            [of_part(2 * PAIR)] * 9
            + [whole((width, width))] * 3
            + [of_part(width), of_part(width), whole((1, width))],
            pl.BlockSpec((1, tile, width), lambda i, m: (0, i, 0)),
            sds((1, th, width), BF),
            free=(10, 11, 12),
        vmem=28,
        flops=3 * dense * width // 2,
            nbytes=7 * tokens * width,
            after=hold,
        )(meta, *(d[i] for i in range(3) for d in dqs), w_query, w_key, w_value, x, d_hidden, gain1)

    grads1 = token_grads(1)
    if paired:
        in_rows = inner.block
        (g_in,), (small_part,), hold = shuttle(
            meta,
            [(first, (3,)), (last, high_bits)],
            [smalls],
            ([inner], [[(0, 0, in_rows[0], 0, in_rows[1])]]),
            [grads1],
        )
        smalls = [small_part] + [swap(small_part, "rows", m << 2) for m in range(1, nrows >> 2)]
    grads0 = token_grads(0)
    out_a, out_b = ungroup(out_parts[0], out_parts[1])
    grad_a, grad_b = ungroup(grads0[0], grads1[0])

    if paired:
        r = width // nrows

        def of(col):
            at = [(0, r), (1, 0), (1, r)]
            return [(piece, row, r, PAIR * col, PAIR) for piece, row in at]

        (g_out, g_q, g_k, g_v), (small_all,), _ = shuttle(
            meta, [], [smalls], ([first, last], [[(0, 0, r, 0, half_w)], of(0), of(1), of(2)]), [grads0]
        )
    else:
        small_all = lax.psum(small_sum, ("rows", "seq"))

        def reduce(x):
            x = lax.psum_scatter(x.astype(F32), "rows", scatter_dimension=0, tiled=True)
            return lax.psum_scatter(x.astype(BF), "seq", scatter_dimension=1, tiled=True).astype(F32)

        def both(keep, send):
            return reduce(jnp.concatenate([keep, send], axis=1))

        g_back, g_in, g_out = both(back_keep, back_send), both(in_keep, in_send), both(out_keep, out_send)
        g_q, g_k, g_v = (
            reduce(
                jnp.concatenate([part[s][:, PAIR * i : PAIR * i + PAIR] for s in range(2) for part in groups], axis=1)
            )
            for i in range(3)
        )
    small_all = small_all.reshape(-1)
    gain_one, gain_two = small_all[:width], small_all[width : 2 * width]
    table_sum = small_all[2 * width :].reshape(buckets, head_count)
    return (
        out_a, out_b, grad_a, grad_b, gain_one, g_q, g_k, g_v, g_out, table_sum, gain_two, g_in, g_back,
    )


def solution(mesh):
    split = P("rows", "seq", None)
    placed = (split, P("rows"), split, split, P("rows"), split) + (P(),) * 9
    shard = P("rows", "seq")
    return jax.shard_map(
        body,
        mesh=mesh,
        in_specs=placed,
        out_specs=(split, split, split, split, P(), shard, shard, shard, shard, P(), P(), shard, shard),
        check_vma=False,
    )
```

```python
import functools

import jax
import jax.numpy as jnp
from jax import lax
from jax.experimental import pallas as pl
from jax.experimental.pallas import tpu as pltpu
from jax.sharding import PartitionSpec as P

EPS = 1e-06
EDGES = (12, 16, 23, 32, 46, 64, 91)
MASKED = -1e30
C1 = 0.7978845608
C3 = 0.044715
BF = jnp.bfloat16
F32 = jnp.float32
HEAD = 64
PAIR = 2 * HEAD
MIB = 1 << 20


def dot(a, b, ca, cb):
    return lax.dot_general(a, b, (((ca,), (cb,)), ((), ())), preferred_element_type=F32)


def exact(a, b):
    return lax.dot_general(
        a, b, (((1,), (0,)), ((), ())), precision=lax.Precision.HIGHEST, preferred_element_type=F32
    )


def sds(shape, dtype):
    return jax.ShapeDtypeStruct(shape, dtype)


def call(kernel, grid, in_specs, out_specs, out_shape, scratch=(), flops=0, nbytes=0, vmem=60, after=(), free=(), aliases=None):
    count, extra = len(in_specs), len(after)

    def run(meta, *refs):
        kernel(meta, *refs[:count], *refs[count + extra :])

    def large(x):
        return x.size * x.dtype.itemsize >= MIB

    def put(x):
        return pltpu.HBM(x.shape, x.dtype) if large(x) else x

    in_specs = list(in_specs) + [pl.BlockSpec(memory_space=pl.ANY)] * extra
    made = pl.pallas_call(
        run,
        grid_spec=pltpu.PrefetchScalarGridSpec(
            num_scalar_prefetch=1,
            grid=grid,
            in_specs=in_specs,
            out_specs=out_specs,
            scratch_shapes=list(scratch),
        ),
        out_shape=[put(x) for x in out_shape] if isinstance(out_shape, list) else put(out_shape),
        input_output_aliases=aliases or {},
        compiler_params=pltpu.CompilerParams(vmem_limit_bytes=vmem * MIB),
        cost_estimate=pl.CostEstimate(flops=int(flops), bytes_accessed=int(nbytes), transcendentals=0),
    )

    def place(i, x):
        return pltpu.with_memory_space_constraint(x, pltpu.HBM) if large(x) and i not in free else x

    return lambda *args: made(*(place(i, x) for i, x in enumerate((*args, *after))))


def whole(shape):
    return pl.BlockSpec(shape, lambda *_: (0,) * len(shape))


def bucket_of(rel, buckets):
    n = jnp.abs(rel)
    far = jnp.full(rel.shape, 8, jnp.int32)
    for edge in EDGES:
        far = far + (n >= edge).astype(jnp.int32)
    return jnp.where(n < 8, n, far) + jnp.where(rel > 0, buckets // 2, 0)


def strip_kernel(meta, table, hot, strip, *, base, buckets):
    near0, near1 = base - 96, base + 224
    heads = strip.shape[0]
    lines = lax.dot_general(
        table[0], hot[...], (((1,), (1,)), ((), ())), precision=lax.Precision.HIGHEST, preferred_element_type=F32
    )
    shape = (near1 - near0, 128)
    rel = near0 - base + lax.broadcasted_iota(jnp.int32, shape, 0) - lax.broadcasted_iota(jnp.int32, shape, 1)
    for h in range(heads):
        wide = jnp.broadcast_to(lines[h : h + 1], (near1 - near0, 256))
        near = pltpu.roll(wide, 0, 1, stride=1, stride_axis=0)[:, :128]
        minus = table[0, h : h + 1, buckets // 2 - 1 : buckets // 2]
        plus = table[0, h : h + 1, buckets - 1 : buckets]
        strip[h, near0:near1, :] = jnp.where(rel >= EDGES[-1], plus, jnp.where(rel <= -EDGES[-1], minus, near))
        strip[h, :near0, :] = jnp.broadcast_to(minus, (near0, 128))
        strip[h, near1:, :] = jnp.broadcast_to(plus, (strip.shape[1] - near1, 128))


def pick_kernel(meta, a, b, out):
    @pl.when(pl.program_id(0) == 0)
    def _():
        out[...] = flat(a)

    @pl.when(pl.program_id(0) == 1)
    def _():
        out[...] = flat(b)


def place_kernel(meta, out_got, grad_got, a0, b0, a1, b1, out_a, out_b, grad_a, grad_b):
    @pl.when(pl.program_id(0) == 0)
    def _():
        out_a[...] = out_got[...].reshape(out_a.shape)
        grad_a[...] = grad_got[...].reshape(grad_a.shape)

    @pl.when(pl.program_id(0) == 1)
    def _():
        out_b[...] = out_got[...].reshape(out_b.shape)
        grad_b[...] = grad_got[...].reshape(grad_b.shape)


def gathered(i, a, b, rest, out):
    @pl.when(i == 0)
    def _():
        out[...] = flat(a)

    @pl.when(i == 1)
    def _():
        out[...] = flat(b)

    @pl.when(i > 1)
    def _():
        out[...] = rest[...]


def qkv_kernel(meta, xa, xb, xr, gain, wq, wk, wv, x_ref, normed, q, k, v):
    gathered(pl.program_id(0), xa, xb, xr, x_ref.at[0])
    x = x_ref[0].astype(F32)
    r = lax.rsqrt(jnp.mean(x * x, axis=-1, keepdims=True) + EPS)
    n = (x * r * gain[...]).astype(BF)
    normed[0] = n
    q[0] = dot(n, wq[...], 1, 0).astype(BF)
    k[0] = dot(n, wk[...], 1, 0).astype(BF)
    v[0] = dot(n, wv[...], 1, 0).astype(BF)


def units_of(na, la, nb, lb):
    out = [(0, s, la, s * la // 2) for s in range(na)]
    return out + [(1, s, lb, na * la // 2 + s * lb // 2) for s in range(nb)]


def joined(ref, off, half):
    return jnp.concatenate([ref[0, off : off + half, :], ref[1, off : off + half, :]], axis=0)


def strip_rows(flip, base, size, cb, kh):
    half = size // 2
    plain = base - 128 * cb + half * kh
    if flip is None:
        return plain
    moved = (128 * cb + half) % size
    return pl.multiple_of(jnp.where(flip == 0, plain, base - moved + half * (1 - kh)), 128)


def lanes_of(shape, high):
    lane = lax.broadcasted_iota(jnp.int32, shape, len(shape) - 1)
    return (lane >= HEAD) == high


def half_mask(high):
    return jnp.where(lanes_of((1, PAIR), high), 1.0, 0.0).astype(BF)


def attn_kernel(meta, q, k, v, strip, pa, pb, attn, linv, kaug, *, dims, base):
    na, la, nb, lb = dims
    flip = meta[0]

    @pl.when(pl.program_id(0) == 0)
    def _():
        for kind, s, size, off in units_of(*dims):
            half = size // 2
            for kh in range(2):
                row = lax.broadcasted_iota(jnp.int32, (half, 128), 0)
                start = jnp.where(flip == 0, half * kh, half * (1 - kh))
                length = meta[3 + (s if kind == 0 else na + s)]
                lane = lax.broadcasted_iota(jnp.int32, (half, 128), 1)
                gone = jnp.logical_and(row + start >= length, lane == 0)
                kaug[kh, off : off + half, :] = jnp.where(gone, MASKED, 0.0).astype(BF)

    low_lanes = lax.broadcasted_iota(jnp.int32, (1, PAIR), 1) < HEAD
    for kind, s, size, off in units_of(*dims):
        half = size // 2
        pref = pa if kind == 0 else pb
        q2, k2, v2 = joined(q, off, half), joined(k, off, half), joined(v, off, half)
        first = jnp.where(lax.broadcasted_iota(jnp.int32, (size, 128), 1) == 0, 1.0, 0.0).astype(BF)
        ones = jnp.ones((size, 128), BF)
        qa = jnp.concatenate([q2, first], axis=1)
        ka = joined(kaug, off, half)
        mixed, inverse = [], []
        for h in range(2):
            kk = jnp.concatenate([k2 * half_mask(h == 1), ka], axis=1)
            for c2 in range(size // 256):
                scores = dot(kk, qa[256 * c2 : 256 * c2 + 256], 1, 1)
                for sub in range(2):
                    cb = 2 * c2 + sub
                    bias = jnp.concatenate(
                        [strip[h, pl.ds(strip_rows(flip, base, size, cb, kh), half), :] for kh in range(2)], axis=0
                    )
                    one = scores[:, 128 * sub : 128 * sub + 128] + bias
                    e = jnp.exp(one - jnp.max(one, axis=0, keepdims=True))
                    pref[h, s, :, 128 * cb : 128 * cb + 128] = e.astype(BF)
            va = jnp.concatenate([v2 * half_mask(h == 1), ones], axis=1)
            both = dot(pref[h, s], va, 0, 0)
            inv = 1.0 / both[:, PAIR:]
            mixed.append(both[:, :PAIR] * inv)
            inverse.append(inv)
        o = (mixed[0] + mixed[1]).astype(BF)
        inv = jnp.where(low_lanes, inverse[0], inverse[1]).astype(BF)
        attn[0, off : off + half, :] = o[:half]
        attn[1, off : off + half, :] = o[half:]
        linv[0, off : off + half, :] = inv[:half]
        linv[1, off : off + half, :] = inv[half:]


def ffn_kernel(
    meta, attn, x, w_out, gain, ga, gb, gr, w_in, w_back,
    hidden, g_out, low, back_send, back_keep, in_send, in_keep, d_normed, normed, d_inner, acc, g, *, mixes, chunk,
):
    i = pl.program_id(0)
    th, tile = g.shape[1], x.shape[1]
    per = th // tile

    @pl.when(i < mixes)
    def _():
        h = x[0].astype(F32) + dot(attn[0], w_out[...], 1, 0)
        r = lax.rsqrt(jnp.mean(h * h, axis=-1, keepdims=True) + EPS)
        hidden[0] = h.astype(BF)
        at = pl.ds(pl.multiple_of((i % per) * tile, tile), tile)
        normed[i // per, at, :] = (h * r * gain[...]).astype(BF)
        gathered(i, ga, gb, gr, g_out.at[0])
        g[i // per, at, :] = g_out[0]

    @pl.when(i == mixes)
    def _():
        acc[...] = jnp.zeros_like(acc)

    @pl.when(i >= mixes)
    def _():
        for part in range(2):
            for lo in range(0, th, chunk):
                rows = slice(lo, lo + chunk)
                v = dot(normed[part, rows, :], w_in[...], 1, 0)
                gw = dot(g[part, rows, :], w_back[...], 1, 1)
                u = v * v
                up = 0.5 + 0.5 * jnp.tanh(v * (C1 + (C1 * C3) * u))
                low[part, rows, :] = (v * up).astype(BF)
                slope = up + up * ((1.0 - up) * (v * (2.0 * C1 + (6.0 * C1 * C3) * u)))
                inner = (gw * slope).astype(BF)
                d_inner[part, rows, :] = inner
                acc[part, rows, :] += dot(inner, w_in[...], 1, 1)
        split_columns(meta, dot(flat(low), flat(g), 0, 0), back_send, back_keep)
        value = dot(flat(normed), flat(d_inner), 0, 0).astype(BF)
        sending = i < mixes + (pl.num_programs(0) - mixes) // 2

        @pl.when(sending)
        def _():
            in_send[...] = value

        @pl.when(jnp.logical_not(sending))
        def _():
            in_keep[...] = value

    @pl.when(i == pl.num_programs(0) - 1)
    def _():
        d_normed[...] = acc[...].astype(BF)


def flat(ref):
    a = ref[...]
    return a.reshape(a.shape[0] * a.shape[1], a.shape[2])


def split_columns(meta, value, send, keep):
    half = value.shape[1] // 2
    lo, hi = value[:, :half].astype(BF), value[:, half:].astype(BF)
    first = meta[1] == 0

    @pl.when(first)
    def _():
        keep[...] = lo
        send[...] = hi

    @pl.when(jnp.logical_not(first))
    def _():
        keep[...] = hi
        send[...] = lo


def rows8(value):
    return jnp.sum(value.reshape(value.shape[0] // 8, 8, value.shape[1]), axis=0)


def hidden_kernel(meta, d_normed, hidden, g, gain, w_out, attn, linv, d_hidden, d_attn, small, send, keep, acc):
    i, last = pl.program_id(0), pl.num_programs(0) - 1
    dn = d_normed[0].astype(F32)
    h = hidden[0].astype(F32)
    r = lax.rsqrt(jnp.mean(h * h, axis=-1, keepdims=True) + EPS)
    gained = dn * gain[...]
    mean = jnp.mean(gained * h, axis=-1, keepdims=True)
    dh = (g[0].astype(F32) + r * gained - h * (r * r * r * mean)).astype(BF)
    d_hidden[0] = dh
    d_attn[0] = (dot(dh, w_out[...], 1, 1) * linv[0].astype(F32)).astype(BF)
    part = rows8(dn * h * r)
    product = dot(attn[0], dh, 0, 0)

    @pl.when(i == 0)
    def _():
        small[...] = part
        acc[...] = product

    @pl.when(i > 0)
    def _():
        small[...] += part
        acc[...] += product

    @pl.when(i == last)
    def _():
        split_columns(meta, acc[...], send, keep)


def table_sums(strip, hot, base, buckets):
    near0, near1 = base - 96, base + 224
    lines, ends = [], []
    for h in range(strip.shape[0]):
        near = strip[h, near0:near1, :]
        rel = (
            near0 - base + lax.broadcasted_iota(jnp.int32, near.shape, 0) - lax.broadcasted_iota(jnp.int32, near.shape, 1)
        )
        plus = rows8(strip[h, near1:, :]) + rows8(jnp.where(rel >= 128, near, 0.0))
        minus = rows8(strip[h, :near0, :]) + rows8(jnp.where(rel <= -128, near, 0.0))
        wide = jnp.where(jnp.abs(rel) < 128, near, 0.0)
        wide = jnp.concatenate([wide, jnp.zeros_like(wide)], axis=1)
        line = jnp.zeros((8, 256), F32)
        for r in range(0, near1 - near0, 8):
            line = line + pltpu.roll(wide[r : r + 8], -r % 256, 1)
        one = jnp.zeros((8, 256), F32)
        row = lax.broadcasted_iota(jnp.int32, (8, 256), 0)
        for r in range(8):
            one = one + pltpu.roll(jnp.where(row == r, line, 0.0), -r % 256, 1)
        lines.append(jnp.sum(one, axis=0, keepdims=True))
        ends.append((jnp.sum(plus, keepdims=True), jnp.sum(minus, keepdims=True)))
    fill = [jnp.zeros((8 - len(lines), 256), F32)]
    sums = exact(jnp.concatenate(lines + fill, axis=0), hot[...])
    lane = lax.broadcasted_iota(jnp.int32, (8, 128), 1)
    row = lax.broadcasted_iota(jnp.int32, (8, 128), 0)
    for h, (plus, minus) in enumerate(ends):
        here = row == h
        sums = sums + jnp.where(jnp.logical_and(here, lane == buckets - 1), plus, 0.0)
        sums = sums + jnp.where(jnp.logical_and(here, lane == buckets // 2 - 1), minus, 0.0)
    return sums


def attn_back_kernel(
    meta, q, k, v, do, at_ref, pa, pb, normed, wqs, wks, wvs, wqk, wkk, wvk, hot,
    dq, dk, dv, table, send, keep, gain, strip, dsa, dsb, cat, *, dims, base, buckets
):
    flip = meta[0]
    step = pl.program_id(0)
    th = normed.shape[1]
    strip[...] = jnp.zeros_like(strip)
    lane = lax.broadcasted_iota(jnp.int32, (1, PAIR), 1)
    minus = jnp.where(lane < 2, -1.0, 0.0).astype(BF)
    for kind, s, size, off in units_of(*dims):
        half = size // 2
        pref = pa if kind == 0 else pb
        ds_ref = dsa if kind == 0 else dsb
        q2, k2, v2, o2, a2 = (joined(ref, off, half) for ref in (q, k, v, do, at_ref))
        prod = o2.astype(F32) * a2.astype(F32)
        dvs, dks, dqs = [], [], []
        for h in range(2):
            mask = half_mask(h == 1)
            delta = jnp.sum(jnp.where((lane >= HEAD) == (h == 1), prod, 0.0), axis=1, keepdims=True)
            high = delta.astype(BF).astype(F32)
            cols = jnp.where(lane == 0, high, jnp.where(lane == 1, delta - high, 0.0)).astype(BF)
            va = jnp.concatenate([v2 * mask, jnp.broadcast_to(minus, (size, PAIR))], axis=1)
            oa = jnp.concatenate([o2, cols], axis=1)
            for c2 in range(size // 256):
                dp = dot(va, oa[256 * c2 : 256 * c2 + 256], 1, 1)
                for sub in range(2):
                    cb = 2 * c2 + sub
                    cs = slice(128 * cb, 128 * cb + 128)
                    ds = pref[h, s, :, cs].astype(F32) * dp[:, 128 * sub : 128 * sub + 128]
                    for kh in range(2):
                        at = pl.ds(strip_rows(flip, base, size, cb, kh), half)
                        strip[h, at, :] += ds[half * kh : half * kh + half]
                    ds_ref[h, :, cs] = ds.astype(BF)
            dvs.append(dot(pref[h, s], o2 * mask, 1, 0))
            dks.append(dot(ds_ref[h], q2 * mask, 1, 0))
            dqs.append(dot(ds_ref[h], k2 * mask, 0, 0))
        d_v = (dvs[0] + dvs[1]).astype(BF)
        d_k = (dks[0] + dks[1]).astype(BF)
        d_q = (dqs[0] + dqs[1]).astype(BF)
        for part in range(2):
            rows = slice(off, off + half)
            got = slice(part * half, part * half + half)
            dq[part, rows, :] = d_q[got]
            dk[part, rows, :] = d_k[got]
            dv[part, rows, :] = d_v[got]
            at = slice(part * th + off, part * th + off + half)
            cat[step, at, 0:128] = d_q[got]
            cat[step, at, 128:256] = d_k[got]
            cat[step, at, 256:384] = d_v[got]
    table[0] = table_sums(strip, hot, base, buckets)

    @pl.when(step == 1)
    def _():
        both = jnp.concatenate([cat[0], cat[1]], axis=1)
        value = dot(flat(normed), both, 0, 0)
        send[...] = value[:, :384].astype(BF)
        keep[...] = value[:, 384:].astype(BF)
        gain[...] = sum(
            value[:, 128 * i : 128 * i + 128] * w[...].astype(F32) for i, w in enumerate((wqs, wks, wvs, wqk, wkk, wvk))
        )


def spread(i, value, first, second):
    @pl.when(i == 0)
    def _():
        first[...] = value.reshape(first.shape)

    @pl.when(i == 1)
    def _():
        second[...] = value.reshape(second.shape)


def out_kernel(meta, low, w_back, hidden, give, out_a, out_b):
    i = pl.program_id(0)
    value = (hidden[0].astype(F32) + dot(low[0], w_back[...], 1, 0)).astype(BF)

    @pl.when(i < 2)
    def _():
        give[...] = value

    spread(i - 2, value, out_a, out_b)


def tokens_kernel(meta, *refs):
    wq, wk, wv, x_ref, d_hidden, gain = refs[9:15]
    outs = refs[15:]

    def columns(of):
        return jnp.concatenate([r[0, :, :PAIR] for r in of] + [r[0, :, PAIR:] for r in of], axis=1)

    dq, dk, dv = columns(refs[0:3]), columns(refs[3:6]), columns(refs[6:9])
    dn = dot(dq, wq[...], 1, 1) + dot(dk, wk[...], 1, 1) + dot(dv, wv[...], 1, 1)
    x = x_ref[0].astype(F32)
    r = lax.rsqrt(jnp.mean(x * x, axis=-1, keepdims=True) + EPS)
    gained = dn * gain[...]
    mean = jnp.mean(gained * x, axis=-1, keepdims=True)
    value = (d_hidden[0].astype(F32) + r * gained - x * (r * r * r * mean)).astype(BF)
    if len(outs) == 1:
        outs[0][...] = value
    else:
        spread(pl.program_id(0), value, *outs)


def swap(x, axis, bit):
    n = lax.axis_size(axis)
    return lax.ppermute(x, axis, [(i, i ^ bit) for i in range(n)])


TAIL = 16


class Piece:
    def __init__(self, parts, bits_left, carrier=False):
        self.parts, self.left, self.carrier, self.flat = parts, bits_left, carrier, 0

    def rows(self, cols):
        return self.flat or sum(t[0].shape[-2] * t[0].shape[-1] // cols for t in self.parts)

    def count(self, bits):
        return 1 << (len(self.left) - len(bits))


def blocks(x, bits):
    return x.reshape((2,) * bits + (x.shape[0] >> bits, x.shape[1]))


def masks_of(bits):
    return [tuple((m >> i) & 1 for i in range(len(bits))) for m in range(1 << len(bits))]


def shuttle(meta, cols, work, finals, after, small=((), ()), through=()):
    pieces, results = finals
    ins = []

    def slot(x):
        for i, y in enumerate(ins):
            if y is x:
                return i
        ins.append(x)
        return len(ins) - 1

    every = [piece for piece, _ in work] + pieces
    slots = []
    for piece in every:
        slots.append([[(slot(t[0]), t[1]) if piece.flat else (slot(t), 0) for t in terms] for terms in piece.parts])
    small_at, tail_at = [slot(x) for x in small[0]], [slot(x) for x in small[1]]
    messages = {}
    for number, (piece, bits) in enumerate(work):
        for mask in masks_of(bits):
            wide = sum(flip << b for flip, b in zip(mask, bits))
            entry = messages.setdefault(wide, [0, False, []])
            entry[2].append((number, mask, entry[0]))
            entry[0] += piece.count(bits) * piece.rows(cols)
            entry[1] |= piece.carrier and wide > 0
    outs = [sds((rows + (TAIL if tail else 0), cols), BF) for rows, tail, _ in messages.values()]
    outs += [sds((spans[0][2], sum(s[4] for s in spans)), F32) for spans in results]
    if small_at:
        outs.append(sds(small[0][0].shape, F32))

    def kernel(meta, *refs):
        got, put = refs[: len(ins)], list(refs[len(ins) + len(through) : len(ins) + len(through) + len(outs)])
        row = meta[2]
        if small_at:
            total = sum(got[i][...] for i in small_at)
            for i in tail_at:
                end = got[i].shape[0]
                tail = got[i][end - TAIL : end, :].astype(F32)
                total = total + tail[: TAIL // 2] + tail[TAIL // 2 :]
            put[-1][...] = total
            high = total.astype(BF).astype(F32)
            tail = jnp.concatenate([high, total - high], axis=0).astype(BF)

        def take(piece, terms, index):
            if not piece.flat:
                return sum(got[i][index].astype(F32) for i, _ in terms)
            at = 0
            for bit in index:
                at = 2 * at + bit
            value = 0.0
            for i, low in terms:
                start = low + at * piece.flat
                value = value + got[i][pl.ds(pl.multiple_of(start, 16) if index else start, piece.flat), :].astype(F32)
            return value

        for (rows, tailed, entries), out in zip(messages.values(), put):
            for number, mask, low in entries:
                piece, bits = work[number]
                rest = [b for b in piece.left if b not in bits]
                for m in range(1 << len(rest)):
                    chosen = {b: (m >> i) & 1 for i, b in enumerate(rest)}
                    for b, flip in zip(bits, mask):
                        chosen[b] = ((row >> b) & 1) ^ flip
                    index = tuple(chosen[b] for b in reversed(piece.left))
                    for terms in slots[number]:
                        value = take(piece, terms, index).astype(BF)
                        high = value.shape[0]
                        for c in range(0, value.shape[1], cols):
                            out[low : low + high, :] = value[:, c : c + cols]
                            low += high
            if tailed:
                out[rows : rows + TAIL, :] = tail
        sums = [take(piece, slots[len(work) + i][0], ()) for i, piece in enumerate(pieces)]
        for spans, out in zip(results, put[len(messages) :]):
            low = 0
            for piece, r0, r, c0, c in spans:
                out[:, low : low + c] = sums[piece][r0 : r0 + r, c0 : c0 + c]
                low += c

    made = call(
        kernel,
        (1,),
        [whole(x.shape) for x in ins] + [pl.BlockSpec(memory_space=pl.ANY)] * len(through),
        [whole(x.shape) for x in outs] + [pl.BlockSpec(memory_space=pl.ANY)] * len(through),
        outs + [sds(x.shape, x.dtype) for x in through],
        nbytes=sum(x.size * 2 for x in ins),
        vmem=30,
        after=after,
        aliases={1 + len(ins) + i: len(outs) + i for i in range(len(through))},
    )(meta, *ins, *through)
    made, passed = list(made[: len(outs)]), made[len(outs) :]
    got = {wide: swap(x, "rows", wide) if wide else x for wide, x in zip(messages, made)}
    tails = []
    for number, (piece, bits) in enumerate(work):
        rows = piece.rows(cols)
        terms = []
        for wide, (_, tailed, entries) in messages.items():
            for other, _, low in entries:
                if other == number:
                    terms.append((got[wide], low))
                    if piece.carrier and tailed:
                        tails.append(got[wide])
        piece.parts, piece.flat = [terms], rows
        piece.left = tuple(b for b in piece.left if b not in bits)
    ends = len(messages) + len(results)
    return made[len(messages) : ends], (made[ends:], tails), [*made, *passed]


def body(
    tokens_a, lengths_a, cotangent_a, tokens_b, lengths_b, cotangent_b,
    gain_attn, w_query, w_key, w_value, w_out, relative_bias_table, gain_ffn, w_in, w_back,
):
    nseq, nrows = lax.axis_size("seq"), lax.axis_size("rows")
    c = lax.axis_index("seq")
    width = tokens_a.shape[2]
    ff = w_in.shape[1]
    buckets, head_count = relative_bias_table.shape
    la, lb = tokens_a.shape[1] * nseq, tokens_b.shape[1] * nseq
    na, nb = tokens_a.shape[0] // nseq, tokens_b.shape[0] // nseq
    dims = (na, la, nb, lb)
    th = (na * la + nb * lb) // 2
    tokens = 2 * th
    base = la - 128
    strip_len = 2 * la - 128
    pairs = head_count // 2
    paired = nseq == 2 and nrows == 16

    me = c if paired else jnp.int32(0)
    flip = me
    own_a = lax.dynamic_slice_in_dim(lengths_a, c * na, na, 0)
    own_b = lax.dynamic_slice_in_dim(lengths_b, c * nb, nb, 0)
    meta = jnp.concatenate([jnp.stack([flip, me, lax.axis_index("rows")]).astype(jnp.int32), own_a, own_b])
    gain1, gain2 = gain_attn[None], gain_ffn[None]

    tile = th // 2
    per = 2
    row_grid = (2 * per,)
    by_row = lambda w: pl.BlockSpec((1, tile, w), lambda i, m: (i // per, i % per, 0))
    dense = 2 * tokens * width
    shape_a, shape_b = (na, la // 2, width), (nb, lb // 2, width)
    of_core = lambda shape: pl.BlockSpec(shape, lambda i, m: (m[1], 0, 0))
    of_other = lambda shape: pl.BlockSpec(shape, lambda i, m: (1 - m[1], 0, 0))
    cores = 2 if paired else 1
    all_a, all_b = (cores * na,) + shape_a[1:], (cores * nb,) + shape_b[1:]
    cut = na * la // 2

    def regroup(a, b):
        if paired:
            give = call(
                pick_kernel,
                (2,),
                [of_other(shape_a), of_other(shape_b)],
                pl.BlockSpec((tile, width), lambda i, m: (i, 0)),
                sds((th, width), BF),
                nbytes=4 * th * width,
                vmem=16,
            )(meta, a, b)
            return a, b, swap(give, "seq", 1)

        def one(x):
            got = lax.all_to_all(x, "seq", 0, 1, tiled=True)
            n, size, _ = got.shape
            return got.reshape(n, 2, size // 2, width).transpose(1, 0, 2, 3)

        whole_a, whole_b = one(a), one(b)
        rest = jnp.concatenate([whole_a[1].reshape(-1, width), whole_b[1].reshape(-1, width)], axis=0)
        return whole_a[0], whole_b[0], rest

    def ungroup(own_a, own_b, rest):
        def one(own, other, n, size):
            y = jnp.stack([own, other.reshape(own.shape)], axis=1).reshape(n, size, width)
            return lax.all_to_all(y, "seq", 1, 0, tiled=True)

        return one(own_a, rest[:cut], na, la), one(own_b, rest[cut:], nb, lb)

    received = pl.BlockSpec((tile, width), lambda i, m: (jnp.clip(i - per, 0, per - 1), 0))
    x_in = regroup(tokens_a, tokens_b)
    g_in3 = regroup(cotangent_a, cotangent_b)
    lane = jnp.arange(256, dtype=jnp.int32)
    back_rel = ((-96 - lane + 128 + 512) & 255) - 128
    hot = jnp.logical_and(
        bucket_of(back_rel, buckets)[:, None] == jnp.arange(128, dtype=jnp.int32)[None], back_rel[:, None] > -128
    ).astype(F32)

    at_once = 4
    rows_of_table = jnp.pad(
        relative_bias_table.T.reshape(head_count // at_once, at_once, buckets), ((0, 0), (0, 4), (0, 128 - buckets))
    )
    strip = call(
        functools.partial(strip_kernel, base=base, buckets=buckets),
        (head_count // at_once,),
        [pl.BlockSpec((1, 8, 128), lambda h, m: (h, 0, 0)), whole((256, 128))],
        pl.BlockSpec((at_once, strip_len, 128), lambda h, m: (h, 0, 0)),
        sds((head_count, strip_len, 128), F32),
        vmem=16,
        nbytes=4 * head_count * strip_len * 128,
    )(meta, rows_of_table, hot)

    tok = sds((2, th, width), BF)
    x, normed, q, k, v = call(
        qkv_kernel,
        row_grid,
        [of_core(shape_a), of_core(shape_b), received, whole((1, width))] + [whole((width, width))] * 3,
        [by_row(width)] * 5,
        [tok] * 5,
        vmem=30,
        free=(5, 6, 7),
        flops=3 * dense * width,
        nbytes=10 * tokens * width,
        after=[strip],
    )(meta, *x_in, gain1, w_query, w_key, w_value)

    by_pair = pl.BlockSpec((2, th, PAIR), lambda p, m: (0, 0, p))
    pa_shape, pb_shape = (head_count, na, la, la), (head_count, nb, lb, lb)
    score_macs = head_count * (na * la * la + nb * lb * lb)
    pa, pb, attn, linv = call(
        functools.partial(attn_kernel, dims=dims, base=base),
        (pairs,),
        [by_pair] * 3 + [pl.BlockSpec((2, strip_len, 128), lambda p, m: (p, 0, 0))],
        [
            pl.BlockSpec((2, na, la, la), lambda p, m: (p, 0, 0, 0)),
            pl.BlockSpec((2, nb, lb, lb), lambda p, m: (p, 0, 0, 0)),
            by_pair,
            by_pair,
        ],
        [sds(pa_shape, BF), sds(pb_shape, BF), tok, tok],
        scratch=[pltpu.VMEM((2, th, 128), BF)],
        vmem=34,
        flops=score_macs * 256 * 4,
        nbytes=2 * score_macs,
    )(meta, q, k, v, strip)

    all_tok = whole((2, th, width))
    fb = 512
    half_w, half_f, nf, mixes = width // 2, ff // 2, ff // fb, 2 * per

    def unit_at(i, m):
        return (jnp.maximum(i - mixes, 0) + (1 - m[1]) * (nf // 2)) % nf

    def mix_at(i):
        return jnp.minimum(i, mixes - 1)

    mix_rows = pl.BlockSpec((1, tile, width), lambda i, m: (mix_at(i) // per, mix_at(i) % per, 0))
    unit_rows = pl.BlockSpec((fb, half_w), lambda i, m: (unit_at(i, m), 0))
    hidden, g, low, back_send, back_keep, in_send, in_keep, d_normed2 = call(
        functools.partial(ffn_kernel, mixes=mixes, chunk=min(512, th)),
        (mixes + nf,),
        [
            mix_rows,
            mix_rows,
            whole((width, width)),
            whole((1, width)),
            of_core(shape_a),
            of_core(shape_b),
            received,
            pl.BlockSpec((width, fb), lambda i, m: (0, unit_at(i, m))),
            pl.BlockSpec((fb, width), lambda i, m: (unit_at(i, m), 0)),
        ],
        [
            mix_rows,
            mix_rows,
            pl.BlockSpec((2, th, fb), lambda i, m: (0, 0, unit_at(i, m))),
            unit_rows,
            unit_rows,
            pl.BlockSpec((width, fb), lambda i, m: (0, jnp.clip(i - mixes, 0, nf // 2 - 1))),
            pl.BlockSpec((width, fb), lambda i, m: (0, jnp.maximum(i - mixes - nf // 2, 0))),
            all_tok,
        ],
        [tok, tok, sds((2, th, ff), BF)]
        + [sds((ff, half_w), BF)] * 2
        + [sds((width, half_f), BF)] * 2
        + [tok],
        scratch=[
            pltpu.VMEM((2, th, width), BF),
            pltpu.VMEM((2, th, fb), BF),
            pltpu.VMEM((2, th, width), F32),
            pltpu.VMEM((2, th, width), BF),
        ],
        flops=dense * (5 * ff + width),
        nbytes=2 * tokens * ff,
        vmem=60,
        free=(3, 8, 9),
    )(meta, attn, x, w_out, gain2, *g_in3, w_in, w_back)

    bit_count = nrows.bit_length() - 1
    low_bits, high_bits = (0, 1), tuple(range(2, bit_count))
    every_bit = tuple(range(bit_count))

    def pair_sum(keep, send):
        return [blocks(keep, bit_count), blocks(swap(send, "seq", 1), bit_count)]

    hold = []
    if paired:
        back = Piece([pair_sum(back_keep, back_send)], every_bit)
        inner = Piece([pair_sum(in_keep, in_send)], every_bit)
        hold = [back_send, in_send]

    small = sds((8, width), F32)
    none = ([], [])
    d_hidden, d_attn, small_ffn, out_send, out_keep = call(
        hidden_kernel,
        row_grid,
        [
            by_row(width),
            by_row(width),
            by_row(width),
            whole((1, width)),
            whole((width, width)),
            by_row(width),
            by_row(width),
        ],
        [by_row(width), by_row(width), whole((8, width)), whole((width, half_w)), whole((width, half_w))],
        [tok, tok, small, sds((width, half_w), BF), sds((width, half_w), BF)],
        scratch=[pltpu.VMEM((width, width), F32)],
        free=(2, 6),
        vmem=44,
        flops=dense * (ff + 2 * width),
        nbytes=2 * tokens * ff,
        after=hold,
    )(meta, d_normed2, hidden, g, gain2, w_out, attn, linv)

    group_count = pairs // 2
    groups, dqs, tables, gains = [], [], [], []
    for gi in range(group_count):
        if paired:
            if gi == 0:
                out_sum = pair_sum(out_keep, out_send)
                _, _, hold = shuttle(meta, half_w, [(back, (0,)), (inner, (1,))], none, [d_attn])
                hold.append(out_send)
            elif gi == 1:
                first = [out_sum, pair_sum(*groups[0])]
                hold = [groups[0][1]]
            else:
                first = Piece(first, every_bit)
                _, _, hold = shuttle(
                    meta, half_w, [(back, (1,)), (inner, (0,)), (first, (2,))], none, [dqs[1][0]]
                )
                second = pair_sum(*groups[1])
                hold.append(groups[1][1])

        def pair_at(s, m, gi=gi):
            return jnp.where(s == 0, 1 - m[1], m[1]) * group_count + gi

        def half_at(s, m):
            return jnp.where(s == 0, 1 - m[1], m[1])

        by_cols = pl.BlockSpec((2, th, PAIR), lambda s, m, f=pair_at: (0, 0, f(s, m)))
        to_cols = pl.BlockSpec((2, th, PAIR), lambda s, m: (0, 0, half_at(s, m)))
        weight_cols = [
            pl.BlockSpec((width, PAIR), lambda s, m, f=pair_at, at=at: (0, f(at, m))) for at in (0, 0, 0, 1, 1, 1)
        ]
        dq, dk, dv, table, send, keep, gain = call(
            functools.partial(attn_back_kernel, dims=dims, base=base, buckets=buckets),
            (2,),
            [by_cols] * 5
            + [
                pl.BlockSpec((2, na, la, la), lambda s, m, f=pair_at: (f(s, m), 0, 0, 0)),
                pl.BlockSpec((2, nb, lb, lb), lambda s, m, f=pair_at: (f(s, m), 0, 0, 0)),
                all_tok,
            ]
            + weight_cols
            + [whole((256, 128))],
            [to_cols] * 3
            + [
                pl.BlockSpec((1, 8, 128), lambda s, m: (half_at(s, m), 0, 0)),
                whole((width, 3 * PAIR)),
                whole((width, 3 * PAIR)),
                whole((width, 128)),
            ],
            [sds((2, th, 2 * PAIR), BF)] * 3
            + [
                sds((2, 8, 128), F32),
                sds((width, 3 * PAIR), BF),
                sds((width, 3 * PAIR), BF),
                sds((width, 128), F32),
            ],
            scratch=[
                pltpu.VMEM((2, strip_len, 128), F32),
                pltpu.VMEM((2, la, la), BF),
                pltpu.VMEM((2, lb, lb), BF),
                pltpu.VMEM((2, tokens, 3 * PAIR), BF),
            ],
            vmem=44,
        flops=score_macs * 256 * 8 // 3 + dense * width,
            nbytes=2 * score_macs // 3,
            after=hold,
        )(meta, q, k, v, d_attn, attn, pa, pb, normed, *([w_query, w_key, w_value] * 2), hot)
        dqs.append((dq, dk, dv))
        tables.append(table)
        gains.append(gain)
        groups.append((keep, send))

    table_local = jnp.stack([t[:, :2, :buckets] for t in tables], axis=1).reshape(head_count, buckets).T
    gain_local = jnp.sum(sum(gains), axis=1) / gain_attn
    small_sum = jnp.concatenate([gain_local, jnp.sum(small_ffn, axis=0), table_local.reshape(-1)])
    small_sum = jnp.pad(small_sum, (0, 8 * half_w - small_sum.size)).reshape(8, half_w)
    if paired:
        last = Piece([second, pair_sum(*groups[2])], every_bit, carrier=True)
        smalls = [small_sum, swap(small_sum, "seq", 1)]
        _, _, hold = shuttle(meta, half_w, [(back, (2,)), (inner, (2,)), (first, (0,))], none, [dqs[2][0]])
        hold += [groups[2][1], small_sum]

    def token_grads(part):
        of_part = lambda w: pl.BlockSpec((1, tile, w), lambda i, m: (part, i, 0))
        own = [of_core(shape_a), of_core(shape_b)]
        return call(
            tokens_kernel,
            (per,),
            [of_part(2 * PAIR)] * 9
            + [whole((width, width))] * 3
            + [of_part(width), of_part(width), whole((1, width))],
            [pl.BlockSpec((tile, width), lambda i, m: (i, 0))] if part else own,
            [sds((th, width), BF)] if part else [sds(all_a, BF), sds(all_b, BF)],
            vmem=28,
            free=(10, 11, 12),
            flops=3 * dense * width // 2,
            nbytes=7 * tokens * width,
            after=hold,
        )(meta, *(d[i] for i in range(3) for d in dqs), w_query, w_key, w_value, x, d_hidden, gain1)

    (grads1,) = token_grads(1)
    if paired:
        _, small_state, hold = shuttle(
            meta,
            half_w,
            [(back, (3,)), (inner, (3,)), (first, (1,)), (last, low_bits)],
            none,
            [grads1],
            (smalls, ()),
        )
        hold.append(grads1)
    out_rows = lambda w: pl.BlockSpec((1, tile, w), lambda i, m: (1 - i // per, i % per, 0))
    outs1, out_a, out_b = call(
        out_kernel,
        row_grid,
        [out_rows(ff), whole((ff, width)), out_rows(width)],
        [pl.BlockSpec((tile, width), lambda i, m: (jnp.minimum(i, per - 1), 0)), of_core(shape_a), of_core(shape_b)],
        [sds((th, width), BF), sds(all_a, BF), sds(all_b, BF)],
        vmem=34,
        free=(2,),
        flops=dense * ff,
        nbytes=2 * tokens * ff,
        after=hold,
    )(meta, low, w_back, hidden)
    if paired:
        r = width // nrows
        in_back = [(0, 0, ff // nrows, 0, half_w)]
        in_in = [(1, r * j, r, 0, half_w) for j in range(half_f // half_w)]
        (g_back, g_in), small_state, hold = shuttle(
            meta,
            half_w,
            [(first, (3,)), (last, high_bits)],
            ([back, inner], [in_back, in_in]),
            [],
            small_state,
            [grads1, outs1],
        )
        grads1_got, outs1_got = (swap(y, "seq", 1) for y in hold[-2:])
    grad_a, grad_b = token_grads(0)

    if paired:
        def of(col):
            at = [(0, r), (1, 0), (1, r)]
            return [(piece, row, r, PAIR * col, PAIR) for piece, row in at]

        (g_out, g_q, g_k, g_v), ((small_all,), _), _ = shuttle(
            meta,
            half_w,
            [],
            ([first, last], [[(0, 0, r, 0, half_w)], of(0), of(1), of(2)]),
            [grad_a],
            small_state,
        )
        anywhere = pl.BlockSpec(memory_space=pl.ANY)
        out_a, out_b, grad_a, grad_b = call(
            place_kernel,
            (2,),
            [pl.BlockSpec((tile, width), lambda i, m: (i, 0))] * 2 + [anywhere] * 4,
            [of_other(shape_a), of_other(shape_b)] * 2,
            [sds(all_a, BF), sds(all_b, BF)] * 2,
            vmem=24,
            aliases={3: 0, 4: 1, 5: 2, 6: 3},
        )(meta, outs1_got, grads1_got, out_a, out_b, grad_a, grad_b)
    else:
        out_a, out_b = ungroup(out_a, out_b, outs1)
        grad_a, grad_b = ungroup(grad_a, grad_b, grads1)
        small_all = lax.psum(small_sum, ("rows", "seq"))

        def reduce(x):
            x = lax.psum_scatter(x.astype(F32), "rows", scatter_dimension=0, tiled=True)
            return lax.psum_scatter(x.astype(BF), "seq", scatter_dimension=1, tiled=True).astype(F32)

        def both(keep, send):
            return reduce(jnp.concatenate([keep, send], axis=1))

        g_back, g_in, g_out = both(back_keep, back_send), both(in_keep, in_send), both(out_keep, out_send)
        g_q, g_k, g_v = (
            reduce(
                jnp.concatenate([part[s][:, PAIR * i : PAIR * i + PAIR] for s in range(2) for part in groups], axis=1)
            )
            for i in range(3)
        )
    small_all = small_all.reshape(-1)
    gain_one, gain_two = small_all[:width], small_all[width : 2 * width]
    table_sum = small_all[2 * width : 2 * width + buckets * head_count].reshape(buckets, head_count)
    return (
        out_a, out_b, grad_a, grad_b, gain_one, g_q, g_k, g_v, g_out, table_sum, gain_two, g_in, g_back,
    )


def solution(mesh):
    split = P("rows", "seq", None)
    placed = (split, P("rows"), split, split, P("rows"), split) + (P(),) * 9
    shard = P("rows", "seq")
    return jax.shard_map(
        body,
        mesh=mesh,
        in_specs=placed,
        out_specs=(split, split, split, split, P(), shard, shard, shard, shard, P(), P(), shard, shard),
        check_vma=False,
    )
```

```python
import functools

import jax
import jax.numpy as jnp
from jax import lax
from jax.experimental import pallas as pl
from jax.experimental.pallas import tpu as pltpu
from jax.sharding import PartitionSpec as P

EPS = 1e-06
EDGES = (12, 16, 23, 32, 46, 64, 91)
MASKED = -1e30
C1 = 0.7978845608
C3 = 0.044715
BF = jnp.bfloat16
F32 = jnp.float32
HEAD = 64
PAIR = 2 * HEAD
MIB = 1 << 20


def dot(a, b, ca, cb):
    return lax.dot_general(a, b, (((ca,), (cb,)), ((), ())), preferred_element_type=F32)


def exact(a, b):
    return lax.dot_general(
        a, b, (((1,), (0,)), ((), ())), precision=lax.Precision.HIGHEST, preferred_element_type=F32
    )


def sds(shape, dtype):
    return jax.ShapeDtypeStruct(shape, dtype)


def call(kernel, grid, in_specs, out_specs, out_shape, scratch=(), flops=0, nbytes=0, vmem=60, after=(), free=(), aliases=None):
    count, extra = len(in_specs), len(after)

    def run(meta, *refs):
        kernel(meta, *refs[:count], *refs[count + extra :])

    def large(x):
        return x.size * x.dtype.itemsize >= MIB

    def put(x):
        return pltpu.HBM(x.shape, x.dtype) if large(x) else x

    in_specs = list(in_specs) + [pl.BlockSpec(memory_space=pl.ANY)] * extra
    made = pl.pallas_call(
        run,
        grid_spec=pltpu.PrefetchScalarGridSpec(
            num_scalar_prefetch=1,
            grid=grid,
            in_specs=in_specs,
            out_specs=out_specs,
            scratch_shapes=list(scratch),
        ),
        out_shape=[put(x) for x in out_shape] if isinstance(out_shape, list) else put(out_shape),
        input_output_aliases=aliases or {},
        compiler_params=pltpu.CompilerParams(vmem_limit_bytes=vmem * MIB),
        cost_estimate=pl.CostEstimate(flops=int(flops), bytes_accessed=int(nbytes), transcendentals=0),
    )

    def place(i, x):
        return pltpu.with_memory_space_constraint(x, pltpu.HBM) if large(x) and i not in free else x

    return lambda *args: made(*(place(i, x) for i, x in enumerate((*args, *after))))


def whole(shape):
    return pl.BlockSpec(shape, lambda *_: (0,) * len(shape))


def bucket_of(rel, buckets):
    n = jnp.abs(rel)
    far = jnp.full(rel.shape, 8, jnp.int32)
    for edge in EDGES:
        far = far + (n >= edge).astype(jnp.int32)
    return jnp.where(n < 8, n, far) + jnp.where(rel > 0, buckets // 2, 0)


def strip_kernel(meta, table, hot, strip, *, base, buckets):
    near0, near1 = base - 96, base + 224
    heads = strip.shape[0]
    lines = lax.dot_general(
        table[0], hot[...], (((1,), (1,)), ((), ())), precision=lax.Precision.HIGHEST, preferred_element_type=F32
    )
    shape = (near1 - near0, 128)
    rel = near0 - base + lax.broadcasted_iota(jnp.int32, shape, 0) - lax.broadcasted_iota(jnp.int32, shape, 1)
    for h in range(heads):
        wide = jnp.broadcast_to(lines[h : h + 1], (near1 - near0, 256))
        near = pltpu.roll(wide, 0, 1, stride=1, stride_axis=0)[:, :128]
        minus = table[0, h : h + 1, buckets // 2 - 1 : buckets // 2]
        plus = table[0, h : h + 1, buckets - 1 : buckets]
        strip[h, near0:near1, :] = jnp.where(rel >= EDGES[-1], plus, jnp.where(rel <= -EDGES[-1], minus, near))
        strip[h, :near0, :] = jnp.broadcast_to(minus, (near0, 128))
        strip[h, near1:, :] = jnp.broadcast_to(plus, (strip.shape[1] - near1, 128))


def moved(copies, held, arrive, leave):
    first = [pltpu.make_async_copy(src, held.at[at], arrive.at[i]) for i, (src, at, _) in enumerate(copies)]
    then = [pltpu.make_async_copy(held.at[at], dst, leave.at[i]) for i, (_, at, dst) in enumerate(copies)]
    for one in first:
        one.start()
    for one, two in zip(first, then):
        one.wait()
        two.start()
    for two in then:
        two.wait()


def flat_rows(dims):
    na, la, nb, lb = dims
    first = [(0, s, pl.ds(s * la // 2, la // 2)) for s in range(na)]
    return first + [(1, s, pl.ds(na * la // 2 + s * lb // 2, lb // 2)) for s in range(nb)]


def pick_kernel(meta, ta, tb, ca, cb, out_x, out_g, held, arrive, leave, *, dims):
    first = [(1 - meta[1]) * n for n in (dims[0], dims[2])]
    moved(
        [
            (pair[kind].at[first[kind] + s], (i, rows), out.at[rows])
            for i, (pair, out) in enumerate((((ta, tb), out_x), ((ca, cb), out_g)))
            for kind, s, rows in flat_rows(dims)
        ],
        held,
        arrive,
        leave,
    )


def place_kernel(
    meta, out_got, grad_got, a0, b0, a1, b1, out_a, out_b, grad_a, grad_b, held, arrive, leave, *, dims
):
    first = [(1 - meta[1]) * n for n in (dims[0], dims[2])]
    moved(
        [
            (got.at[rows], (i, rows), pair[kind].at[first[kind] + s])
            for i, (got, pair) in enumerate(((out_got, (out_a, out_b)), (grad_got, (grad_a, grad_b))))
            for kind, s, rows in flat_rows(dims)
        ],
        held,
        arrive,
        leave,
    )


def gathered(i, a, b, rest, out):
    @pl.when(i == 0)
    def _():
        out[...] = flat(a)

    @pl.when(i == 1)
    def _():
        out[...] = flat(b)

    @pl.when(i > 1)
    def _():
        out[...] = rest[...]


def qkv_kernel(meta, xa, xb, xr, gain, wq, wk, wv, x_ref, normed, q, k, v):
    gathered(pl.program_id(0), xa, xb, xr, x_ref.at[0])
    x = x_ref[0].astype(F32)
    r = lax.rsqrt(jnp.mean(x * x, axis=-1, keepdims=True) + EPS)
    n = (x * r * gain[...]).astype(BF)
    normed[0] = n
    q[0] = dot(n, wq[...], 1, 0).astype(BF)
    k[0] = dot(n, wk[...], 1, 0).astype(BF)
    v[0] = dot(n, wv[...], 1, 0).astype(BF)


def units_of(na, la, nb, lb):
    out = [(0, s, la, s * la // 2) for s in range(na)]
    return out + [(1, s, lb, na * la // 2 + s * lb // 2) for s in range(nb)]


def joined(ref, off, half):
    return jnp.concatenate([ref[0, off : off + half, :], ref[1, off : off + half, :]], axis=0)


def strip_rows(flip, base, size, cb, kh):
    half = size // 2
    plain = base - 128 * cb + half * kh
    if flip is None:
        return plain
    moved = (128 * cb + half) % size
    return pl.multiple_of(jnp.where(flip == 0, plain, base - moved + half * (1 - kh)), 128)


def lanes_of(shape, high):
    lane = lax.broadcasted_iota(jnp.int32, shape, len(shape) - 1)
    return (lane >= HEAD) == high


def half_mask(high):
    return jnp.where(lanes_of((1, PAIR), high), 1.0, 0.0).astype(BF)


def attn_kernel(meta, q, k, v, strip, pa, pb, attn, linv, kaug, *, dims, base, seqs_a):
    na, la, nb, lb = dims
    flip = meta[0]

    @pl.when(pl.program_id(0) == 0)
    def _():
        for kind, s, size, off in units_of(*dims):
            half = size // 2
            for kh in range(2):
                row = lax.broadcasted_iota(jnp.int32, (half, 128), 0)
                start = jnp.where(flip == 0, half * kh, half * (1 - kh))
                length = meta[4 + (meta[3] * na if kind == 0 else seqs_a + meta[3] * nb) + s]
                lane = lax.broadcasted_iota(jnp.int32, (half, 128), 1)
                gone = jnp.logical_and(row + start >= length, lane == 0)
                kaug[kh, off : off + half, :] = jnp.where(gone, MASKED, 0.0).astype(BF)

    low_lanes = lax.broadcasted_iota(jnp.int32, (1, PAIR), 1) < HEAD
    for kind, s, size, off in units_of(*dims):
        half = size // 2
        pref = pa if kind == 0 else pb
        q2, k2, v2 = joined(q, off, half), joined(k, off, half), joined(v, off, half)
        first = jnp.where(lax.broadcasted_iota(jnp.int32, (size, 128), 1) == 0, 1.0, 0.0).astype(BF)
        ones = jnp.ones((size, 128), BF)
        qa = jnp.concatenate([q2, first], axis=1)
        ka = joined(kaug, off, half)
        mixed, inverse = [], []
        for h in range(2):
            kk = jnp.concatenate([k2 * half_mask(h == 1), ka], axis=1)
            for c2 in range(size // 256):
                scores = dot(kk, qa[256 * c2 : 256 * c2 + 256], 1, 1)
                for sub in range(2):
                    cb = 2 * c2 + sub
                    bias = jnp.concatenate(
                        [strip[h, pl.ds(strip_rows(flip, base, size, cb, kh), half), :] for kh in range(2)], axis=0
                    )
                    one = scores[:, 128 * sub : 128 * sub + 128] + bias
                    e = jnp.exp(one - jnp.max(one, axis=0, keepdims=True))
                    pref[h, s, :, 128 * cb : 128 * cb + 128] = e.astype(BF)
            va = jnp.concatenate([v2 * half_mask(h == 1), ones], axis=1)
            both = dot(pref[h, s], va, 0, 0)
            inv = 1.0 / both[:, PAIR:]
            mixed.append(both[:, :PAIR] * inv)
            inverse.append(inv)
        o = (mixed[0] + mixed[1]).astype(BF)
        inv = jnp.where(low_lanes, inverse[0], inverse[1]).astype(BF)
        attn[0, off : off + half, :] = o[:half]
        attn[1, off : off + half, :] = o[half:]
        linv[0, off : off + half, :] = inv[:half]
        linv[1, off : off + half, :] = inv[half:]


def ffn_kernel(
    meta, attn, x, w_out, gain, ga, gb, gr, w_in, w_back,
    hidden, g_out, low, back_send, back_keep, in_send, in_keep, d_normed, normed, d_inner, acc, g, *, mixes, chunk,
):
    i = pl.program_id(0)
    th, tile = g.shape[1], x.shape[1]
    per = th // tile

    @pl.when(i < mixes)
    def _():
        h = x[0].astype(F32) + dot(attn[0], w_out[...], 1, 0)
        r = lax.rsqrt(jnp.mean(h * h, axis=-1, keepdims=True) + EPS)
        hidden[0] = h.astype(BF)
        at = pl.ds(pl.multiple_of((i % per) * tile, tile), tile)
        normed[i // per, at, :] = (h * r * gain[...]).astype(BF)
        gathered(i, ga, gb, gr, g_out.at[0])
        g[i // per, at, :] = g_out[0]

    @pl.when(i == mixes)
    def _():
        acc[...] = jnp.zeros_like(acc)

    @pl.when(i >= mixes)
    def _():
        for part in range(2):
            for lo in range(0, th, chunk):
                rows = slice(lo, lo + chunk)
                v = dot(normed[part, rows, :], w_in[...], 1, 0)
                gw = dot(g[part, rows, :], w_back[...], 1, 1)
                u = v * v
                up = 0.5 + 0.5 * jnp.tanh(v * (C1 + (C1 * C3) * u))
                low[part, rows, :] = (v * up).astype(BF)
                slope = up + up * ((1.0 - up) * (v * (2.0 * C1 + (6.0 * C1 * C3) * u)))
                inner = (gw * slope).astype(BF)
                d_inner[part, rows, :] = inner
                acc[part, rows, :] += dot(inner, w_in[...], 1, 1)
        split_columns(meta, dot(flat(low), flat(g), 0, 0), back_send, back_keep)
        value = dot(flat(normed), flat(d_inner), 0, 0).astype(BF)
        sending = i < mixes + (pl.num_programs(0) - mixes) // 2

        @pl.when(sending)
        def _():
            in_send[...] = value

        @pl.when(jnp.logical_not(sending))
        def _():
            in_keep[...] = value

    @pl.when(i == pl.num_programs(0) - 1)
    def _():
        d_normed[...] = acc[...].astype(BF)


def flat(ref):
    a = ref[...]
    return a.reshape(a.shape[0] * a.shape[1], a.shape[2])


def split_columns(meta, value, send, keep):
    half = value.shape[1] // 2
    lo, hi = value[:, :half].astype(BF), value[:, half:].astype(BF)
    first = meta[1] == 0

    @pl.when(first)
    def _():
        keep[...] = lo
        send[...] = hi

    @pl.when(jnp.logical_not(first))
    def _():
        keep[...] = hi
        send[...] = lo


def rows8(value):
    return jnp.sum(value.reshape(value.shape[0] // 8, 8, value.shape[1]), axis=0)


def hidden_kernel(meta, d_normed, hidden, g, gain, w_out, attn, linv, d_hidden, d_attn, small, send, keep, acc, gains):
    i, last = pl.program_id(0), pl.num_programs(0) - 1
    dn = d_normed[0].astype(F32)
    h = hidden[0].astype(F32)
    r = lax.rsqrt(jnp.mean(h * h, axis=-1, keepdims=True) + EPS)
    gained = dn * gain[...]
    mean = jnp.mean(gained * h, axis=-1, keepdims=True)
    dh = (g[0].astype(F32) + r * gained - h * (r * r * r * mean)).astype(BF)
    d_hidden[0] = dh
    d_attn[0] = (dot(dh, w_out[...], 1, 1) * linv[0].astype(F32)).astype(BF)
    part = rows8(dn * h * r)
    product = dot(attn[0], dh, 0, 0)

    @pl.when(i == 0)
    def _():
        gains[...] = part
        acc[...] = product

    @pl.when(i > 0)
    def _():
        gains[...] += part
        acc[...] += product

    @pl.when(i == last)
    def _():
        split_columns(meta, acc[...], send, keep)
        line = jnp.sum(gains[...], axis=0, keepdims=True)
        half = small.shape[1]
        small[...] = jnp.zeros_like(small)
        small[2:3, :] = line[:, :half]
        small[3:4, :] = line[:, half:]


def table_sums(strip, hot, base, buckets):
    near0, near1 = base - 96, base + 224
    lines, ends = [], []
    for h in range(strip.shape[0]):
        near = strip[h, near0:near1, :]
        rel = (
            near0 - base + lax.broadcasted_iota(jnp.int32, near.shape, 0) - lax.broadcasted_iota(jnp.int32, near.shape, 1)
        )
        plus = rows8(strip[h, near1:, :]) + rows8(jnp.where(rel >= 128, near, 0.0))
        minus = rows8(strip[h, :near0, :]) + rows8(jnp.where(rel <= -128, near, 0.0))
        wide = jnp.where(jnp.abs(rel) < 128, near, 0.0)
        wide = jnp.concatenate([wide, jnp.zeros_like(wide)], axis=1)
        line = jnp.zeros((8, 256), F32)
        for r in range(0, near1 - near0, 8):
            line = line + pltpu.roll(wide[r : r + 8], -r % 256, 1)
        one = jnp.zeros((8, 256), F32)
        row = lax.broadcasted_iota(jnp.int32, (8, 256), 0)
        for r in range(8):
            one = one + pltpu.roll(jnp.where(row == r, line, 0.0), -r % 256, 1)
        lines.append(jnp.sum(one, axis=0, keepdims=True))
        ends.append((jnp.sum(plus, keepdims=True), jnp.sum(minus, keepdims=True)))
    fill = [jnp.zeros((8 - len(lines), 256), F32)]
    sums = exact(jnp.concatenate(lines + fill, axis=0), hot[...])
    lane = lax.broadcasted_iota(jnp.int32, (8, 128), 1)
    row = lax.broadcasted_iota(jnp.int32, (8, 128), 0)
    for h, (plus, minus) in enumerate(ends):
        here = row == h
        sums = sums + jnp.where(jnp.logical_and(here, lane == buckets - 1), plus, 0.0)
        sums = sums + jnp.where(jnp.logical_and(here, lane == buckets // 2 - 1), minus, 0.0)
    return sums


def attn_back_kernel(
    meta, q, k, v, do, at_ref, pa, pb, normed, wqs, wks, wvs, wqk, wkk, wvk, hot, gain_attn, small_in, *rest, dims, base, buckets, pair_at, place
):
    before = [] if place[0] else [rest[0]]
    dq, dk, dv, send, keep, small, gain, strip, dsa, dsb, cat = rest[len(before) :]
    flip = meta[0]
    step = pl.program_id(0)
    th = normed.shape[1]
    strip[...] = jnp.zeros_like(strip)
    lane = lax.broadcasted_iota(jnp.int32, (1, PAIR), 1)
    minus = jnp.where(lane < 2, -1.0, 0.0).astype(BF)
    for kind, s, size, off in units_of(*dims):
        half = size // 2
        pref = pa if kind == 0 else pb
        ds_ref = dsa if kind == 0 else dsb
        q2, k2, v2, o2, a2 = (joined(ref, off, half) for ref in (q, k, v, do, at_ref))
        prod = o2.astype(F32) * a2.astype(F32)
        dvs, dks, dqs = [], [], []
        for h in range(2):
            mask = half_mask(h == 1)
            delta = jnp.sum(jnp.where((lane >= HEAD) == (h == 1), prod, 0.0), axis=1, keepdims=True)
            high = delta.astype(BF).astype(F32)
            cols = jnp.where(lane == 0, high, jnp.where(lane == 1, delta - high, 0.0)).astype(BF)
            va = jnp.concatenate([v2 * mask, jnp.broadcast_to(minus, (size, PAIR))], axis=1)
            oa = jnp.concatenate([o2, cols], axis=1)
            for c2 in range(size // 256):
                dp = dot(va, oa[256 * c2 : 256 * c2 + 256], 1, 1)
                for sub in range(2):
                    cb = 2 * c2 + sub
                    cs = slice(128 * cb, 128 * cb + 128)
                    ds = pref[h, s, :, cs].astype(F32) * dp[:, 128 * sub : 128 * sub + 128]
                    for kh in range(2):
                        at = pl.ds(strip_rows(flip, base, size, cb, kh), half)
                        strip[h, at, :] += ds[half * kh : half * kh + half]
                    ds_ref[h, :, cs] = ds.astype(BF)
            dvs.append(dot(pref[h, s], o2 * mask, 1, 0))
            dks.append(dot(ds_ref[h], q2 * mask, 1, 0))
            dqs.append(dot(ds_ref[h], k2 * mask, 0, 0))
        d_v = (dvs[0] + dvs[1]).astype(BF)
        d_k = (dks[0] + dks[1]).astype(BF)
        d_q = (dqs[0] + dqs[1]).astype(BF)
        for part in range(2):
            rows = slice(off, off + half)
            got = slice(part * half, part * half + half)
            dq[part, rows, :] = d_q[got]
            dk[part, rows, :] = d_k[got]
            dv[part, rows, :] = d_v[got]
            at = slice(part * th + off, part * th + off + half)
            cat[step, at, 0:128] = d_q[got]
            cat[step, at, 128:256] = d_k[got]
            cat[step, at, 256:384] = d_v[got]
    @pl.when(step == 0)
    def _():
        small[...] = small_in[...]

    sums = table_sums(strip, hot, base, buckets)
    row = lax.broadcasted_iota(jnp.int32, (small.shape[0], 128), 0) - (4 + 2 * pair_at(step, meta))
    small[:, 0:128] += jnp.where(row == 0, sums[0:1], jnp.where(row == 1, sums[1:2], 0.0))

    @pl.when(step == 1)
    def _():
        both = jnp.concatenate([cat[0], cat[1]], axis=1)
        value = dot(flat(normed), both, 0, 0)
        send[...] = value[:, :384].astype(BF)
        keep[...] = value[:, 384:].astype(BF)
        part = sum(
            value[:, 128 * i : 128 * i + 128] * w[...].astype(F32) for i, w in enumerate((wqs, wks, wvs, wqk, wkk, wvk))
        )
        for ref in before:
            part = part + ref[...]
        gain[...] = part
        if place[1]:
            line = lax.dot_general(
                jnp.ones((8, 128), F32), part, (((1,), (1,)), ((), ())), precision=lax.Precision.HIGHEST,
                preferred_element_type=F32,
            )[:1] / gain_attn[...]
            half = small.shape[1]
            small[0:1, :] += line[:, :half]
            small[1:2, :] += line[:, half:]


def spread(i, value, first, second):
    @pl.when(i == 0)
    def _():
        first[...] = value.reshape(first.shape)

    @pl.when(i == 1)
    def _():
        second[...] = value.reshape(second.shape)


def out_kernel(meta, low, w_back, hidden, give, out_a, out_b):
    i = pl.program_id(0)
    value = (hidden[0].astype(F32) + dot(low[0], w_back[...], 1, 0)).astype(BF)

    @pl.when(i < 2)
    def _():
        give[...] = value

    spread(i - 2, value, out_a, out_b)


def tokens_kernel(meta, *refs):
    wq, wk, wv, x_ref, d_hidden, gain = refs[9:15]
    outs = refs[15:]

    def columns(of):
        return jnp.concatenate([r[0, :, :PAIR] for r in of] + [r[0, :, PAIR:] for r in of], axis=1)

    dq, dk, dv = columns(refs[0:3]), columns(refs[3:6]), columns(refs[6:9])
    dn = dot(dq, wq[...], 1, 1) + dot(dk, wk[...], 1, 1) + dot(dv, wv[...], 1, 1)
    x = x_ref[0].astype(F32)
    r = lax.rsqrt(jnp.mean(x * x, axis=-1, keepdims=True) + EPS)
    gained = dn * gain[...]
    mean = jnp.mean(gained * x, axis=-1, keepdims=True)
    value = (d_hidden[0].astype(F32) + r * gained - x * (r * r * r * mean)).astype(BF)
    if len(outs) == 1:
        outs[0][...] = value
    else:
        spread(pl.program_id(0), value, *outs)


def swap(x, axis, bit):
    n = lax.axis_size(axis)
    return lax.ppermute(x, axis, [(i, i ^ bit) for i in range(n)])


TAIL = 32


class Piece:
    def __init__(self, parts, bits_left, carrier=False):
        self.parts, self.left, self.carrier, self.flat = parts, bits_left, carrier, 0

    def rows(self, cols):
        return self.flat or sum(t[0].shape[-2] * t[0].shape[-1] // cols for t in self.parts)

    def count(self, bits):
        return 1 << (len(self.left) - len(bits))


def blocks(x, bits):
    return x.reshape((2,) * bits + (x.shape[0] >> bits, x.shape[1]))


def masks_of(bits):
    return [tuple((m >> i) & 1 for i in range(len(bits))) for m in range(1 << len(bits))]


def shuttle(meta, cols, work, finals, after, small=((), ()), through=()):
    pieces, results = finals
    ins = []

    def slot(x):
        for i, y in enumerate(ins):
            if y is x:
                return i
        ins.append(x)
        return len(ins) - 1

    every = [piece for piece, _ in work] + pieces
    slots = []
    received = set()
    for piece in every:
        for terms in piece.parts:
            received |= {1 + slot(t[0] if piece.flat else t) for t in terms[1:]}
        slots.append([[(slot(t[0]), t[1]) if piece.flat else (slot(t), 0) for t in terms] for terms in piece.parts])
    small_at, tail_at = [slot(x) for x in small[0]], [slot(x) for x in small[1]]
    messages = {}
    for number, (piece, bits) in enumerate(work):
        for mask in masks_of(bits):
            wide = sum(flip << b for flip, b in zip(mask, bits))
            entry = messages.setdefault(wide, [0, False, []])
            entry[2].append((number, mask, entry[0]))
            entry[0] += piece.count(bits) * piece.rows(cols)
            entry[1] |= piece.carrier and wide > 0
    outs = [sds((rows + (TAIL if tail else 0), cols), BF) for rows, tail, _ in messages.values()]
    outs += [sds((spans[0][2], sum(s[4] for s in spans)), F32) for spans in results]
    if small_at:
        outs.append(sds(small[0][0].shape, F32))

    def kernel(meta, *refs):
        got, put = refs[: len(ins)], list(refs[len(ins) + len(through) : len(ins) + len(through) + len(outs)])
        row = meta[2]
        if small_at:
            total = sum(got[i][...] for i in small_at)
            for i in tail_at:
                end = got[i].shape[0]
                tail = got[i][end - TAIL : end, :].astype(F32)
                total = total + tail[: TAIL // 2] + tail[TAIL // 2 :]
            put[-1][...] = total
            high = total.astype(BF).astype(F32)
            tail = jnp.concatenate([high, total - high], axis=0).astype(BF)

        def take(piece, terms, index):
            if not piece.flat:
                return sum(got[i][index].astype(F32) for i, _ in terms)
            at = 0
            for bit in index:
                at = 2 * at + bit
            value = 0.0
            for i, low in terms:
                start = low + at * piece.flat
                value = value + got[i][pl.ds(pl.multiple_of(start, 16) if index else start, piece.flat), :].astype(F32)
            return value

        for (rows, tailed, entries), out in zip(messages.values(), put):
            for number, mask, low in entries:
                piece, bits = work[number]
                rest = [b for b in piece.left if b not in bits]
                for m in range(1 << len(rest)):
                    chosen = {b: (m >> i) & 1 for i, b in enumerate(rest)}
                    for b, flip in zip(bits, mask):
                        chosen[b] = ((row >> b) & 1) ^ flip
                    index = tuple(chosen[b] for b in reversed(piece.left))
                    for terms in slots[number]:
                        value = take(piece, terms, index).astype(BF)
                        high = value.shape[0]
                        for c in range(0, value.shape[1], cols):
                            out[low : low + high, :] = value[:, c : c + cols]
                            low += high
            if tailed:
                out[rows : rows + TAIL, :] = tail
        sums = [take(piece, slots[len(work) + i][0], ()) for i, piece in enumerate(pieces)]
        for spans, out in zip(results, put[len(messages) :]):
            low = 0
            for piece, r0, r, c0, c in spans:
                out[:, low : low + c] = sums[piece][r0 : r0 + r, c0 : c0 + c]
                low += c

    made = call(
        kernel,
        (1,),
        [whole(x.shape) for x in ins] + [pl.BlockSpec(memory_space=pl.ANY)] * len(through),
        [whole(x.shape) for x in outs] + [pl.BlockSpec(memory_space=pl.ANY)] * len(through),
        outs + [sds(x.shape, x.dtype) for x in through],
        nbytes=sum(x.size * 2 for x in ins),
        vmem=30,
        free=tuple(received),
        after=after,
        aliases={1 + len(ins) + i: len(outs) + i for i in range(len(through))},
    )(meta, *ins, *through)
    made, passed = list(made[: len(outs)]), made[len(outs) :]
    got = {wide: swap(x, "rows", wide) if wide else x for wide, x in zip(messages, made)}
    tails = []
    for number, (piece, bits) in enumerate(work):
        rows = piece.rows(cols)
        terms = []
        for wide, (_, tailed, entries) in messages.items():
            for other, _, low in entries:
                if other == number:
                    terms.append((got[wide], low))
                    if piece.carrier and tailed:
                        tails.append(got[wide])
        piece.parts, piece.flat = [terms], rows
        piece.left = tuple(b for b in piece.left if b not in bits)
    ends = len(messages) + len(results)
    return made[len(messages) : ends], (made[ends:], tails), [*made[: len(messages)], *passed]


def body(
    tokens_a, lengths_a, cotangent_a, tokens_b, lengths_b, cotangent_b,
    gain_attn, w_query, w_key, w_value, w_out, relative_bias_table, gain_ffn, w_in, w_back,
):
    nseq, nrows = lax.axis_size("seq"), lax.axis_size("rows")
    c = lax.axis_index("seq")
    width = tokens_a.shape[2]
    ff = w_in.shape[1]
    buckets, head_count = relative_bias_table.shape
    la, lb = tokens_a.shape[1] * nseq, tokens_b.shape[1] * nseq
    na, nb = tokens_a.shape[0] // nseq, tokens_b.shape[0] // nseq
    dims = (na, la, nb, lb)
    th = (na * la + nb * lb) // 2
    tokens = 2 * th
    base = la - 128
    strip_len = 2 * la - 128
    pairs = head_count // 2
    paired = nseq == 2 and nrows == 16

    me = c if paired else jnp.int32(0)
    flip = me
    meta = jnp.concatenate(
        [jnp.stack([flip, me, lax.axis_index("rows"), c]).astype(jnp.int32), lengths_a, lengths_b]
    )
    gain1, gain2 = gain_attn[None], gain_ffn[None]

    tile = th // 2
    per = 2
    row_grid = (2 * per,)
    by_row = lambda w: pl.BlockSpec((1, tile, w), lambda i, m: (i // per, i % per, 0))
    dense = 2 * tokens * width
    shape_a, shape_b = (na, la // 2, width), (nb, lb // 2, width)
    of_core = lambda shape: pl.BlockSpec(shape, lambda i, m: (m[1], 0, 0))
    of_other = lambda shape: pl.BlockSpec(shape, lambda i, m: (1 - m[1], 0, 0))
    cores = 2 if paired else 1
    all_a, all_b = (cores * na,) + shape_a[1:], (cores * nb,) + shape_b[1:]
    cut = na * la // 2

    def regroup(a, b):
        def one(x):
            got = lax.all_to_all(x, "seq", 0, 1, tiled=True)
            n, size, _ = got.shape
            return got.reshape(n, 2, size // 2, width).transpose(1, 0, 2, 3)

        whole_a, whole_b = one(a), one(b)
        rest = jnp.concatenate([whole_a[1].reshape(-1, width), whole_b[1].reshape(-1, width)], axis=0)
        return whole_a[0], whole_b[0], rest

    def ungroup(own_a, own_b, rest):
        def one(own, other, n, size):
            y = jnp.stack([own, other.reshape(own.shape)], axis=1).reshape(n, size, width)
            return lax.all_to_all(y, "seq", 1, 0, tiled=True)

        return one(own_a, rest[:cut], na, la), one(own_b, rest[cut:], nb, lb)

    received = pl.BlockSpec((tile, width), lambda i, m: (jnp.clip(i - per, 0, per - 1), 0))
    anywhere = pl.BlockSpec(memory_space=pl.ANY)
    copies = [pltpu.VMEM((2, th, width), BF)] + [pltpu.SemaphoreType.DMA((2 * (na + nb),))] * 2
    if paired:
        give = call(
            functools.partial(pick_kernel, dims=dims),
            (1,),
            [anywhere] * 4,
            [anywhere] * 2,
            [sds((th, width), BF)] * 2,
            scratch=copies,
            nbytes=8 * th * width,
            vmem=8,
        )(meta, tokens_a, tokens_b, cotangent_a, cotangent_b)
        x_in = (tokens_a, tokens_b, swap(give[0], "seq", 1))
        g_in3 = (cotangent_a, cotangent_b, swap(give[1], "seq", 1))
    else:
        x_in = regroup(tokens_a, tokens_b)
        g_in3 = regroup(cotangent_a, cotangent_b)
    lane = jnp.arange(256, dtype=jnp.int32)
    back_rel = ((-96 - lane + 128 + 512) & 255) - 128
    hot = jnp.logical_and(
        bucket_of(back_rel, buckets)[:, None] == jnp.arange(128, dtype=jnp.int32)[None], back_rel[:, None] > -128
    ).astype(F32)

    at_once = 4
    rows_of_table = jnp.pad(
        relative_bias_table.T.reshape(head_count // at_once, at_once, buckets), ((0, 0), (0, 4), (0, 128 - buckets))
    )
    strip = call(
        functools.partial(strip_kernel, base=base, buckets=buckets),
        (head_count // at_once,),
        [pl.BlockSpec((1, 8, 128), lambda h, m: (h, 0, 0)), whole((256, 128))],
        pl.BlockSpec((at_once, strip_len, 128), lambda h, m: (h, 0, 0)),
        sds((head_count, strip_len, 128), F32),
        vmem=16,
        nbytes=4 * head_count * strip_len * 128,
    )(meta, rows_of_table, hot)

    tok = sds((2, th, width), BF)
    x, normed, q, k, v = call(
        qkv_kernel,
        row_grid,
        [of_core(shape_a), of_core(shape_b), received, whole((1, width))] + [whole((width, width))] * 3,
        [by_row(width)] * 5,
        [tok] * 5,
        vmem=30,
        free=(5, 6, 7),
        flops=3 * dense * width,
        nbytes=10 * tokens * width,
        after=[strip],
    )(meta, *x_in, gain1, w_query, w_key, w_value)

    by_pair = pl.BlockSpec((2, th, PAIR), lambda p, m: (0, 0, p))
    pa_shape, pb_shape = (head_count, na, la, la), (head_count, nb, lb, lb)
    score_macs = head_count * (na * la * la + nb * lb * lb)
    pa, pb, attn, linv = call(
        functools.partial(attn_kernel, dims=dims, base=base, seqs_a=tokens_a.shape[0]),
        (pairs,),
        [by_pair] * 3 + [pl.BlockSpec((2, strip_len, 128), lambda p, m: (p, 0, 0))],
        [
            pl.BlockSpec((2, na, la, la), lambda p, m: (p, 0, 0, 0)),
            pl.BlockSpec((2, nb, lb, lb), lambda p, m: (p, 0, 0, 0)),
            by_pair,
            by_pair,
        ],
        [sds(pa_shape, BF), sds(pb_shape, BF), tok, tok],
        scratch=[pltpu.VMEM((2, th, 128), BF)],
        vmem=34,
        flops=score_macs * 256 * 4,
        nbytes=2 * score_macs,
    )(meta, q, k, v, strip)

    all_tok = whole((2, th, width))
    fb = 512
    half_w, half_f, nf, mixes = width // 2, ff // 2, ff // fb, 2 * per

    def unit_at(i, m):
        return (jnp.maximum(i - mixes, 0) + (1 - m[1]) * (nf // 2)) % nf

    def mix_at(i):
        return jnp.minimum(i, mixes - 1)

    mix_rows = pl.BlockSpec((1, tile, width), lambda i, m: (mix_at(i) // per, mix_at(i) % per, 0))
    unit_rows = pl.BlockSpec((fb, half_w), lambda i, m: (unit_at(i, m), 0))
    hidden, g, low, back_send, back_keep, in_send, in_keep, d_normed2 = call(
        functools.partial(ffn_kernel, mixes=mixes, chunk=min(512, th)),
        (mixes + nf,),
        [
            mix_rows,
            mix_rows,
            whole((width, width)),
            whole((1, width)),
            of_core(shape_a),
            of_core(shape_b),
            received,
            pl.BlockSpec((width, fb), lambda i, m: (0, unit_at(i, m))),
            pl.BlockSpec((fb, width), lambda i, m: (unit_at(i, m), 0)),
        ],
        [
            mix_rows,
            mix_rows,
            pl.BlockSpec((2, th, fb), lambda i, m: (0, 0, unit_at(i, m))),
            unit_rows,
            unit_rows,
            pl.BlockSpec((width, fb), lambda i, m: (0, jnp.clip(i - mixes, 0, nf // 2 - 1))),
            pl.BlockSpec((width, fb), lambda i, m: (0, jnp.maximum(i - mixes - nf // 2, 0))),
            all_tok,
        ],
        [tok, tok, sds((2, th, ff), BF)]
        + [sds((ff, half_w), BF)] * 2
        + [sds((width, half_f), BF)] * 2
        + [tok],
        scratch=[
            pltpu.VMEM((2, th, width), BF),
            pltpu.VMEM((2, th, fb), BF),
            pltpu.VMEM((2, th, width), F32),
            pltpu.VMEM((2, th, width), BF),
        ],
        flops=dense * (5 * ff + width),
        nbytes=2 * tokens * ff,
        vmem=60,
        free=(3, 8, 9),
    )(meta, attn, x, w_out, gain2, *g_in3, w_in, w_back)

    bit_count = nrows.bit_length() - 1
    low_bits, high_bits = (0, 1), tuple(range(2, bit_count))
    every_bit = tuple(range(bit_count))

    def pair_sum(keep, send):
        return [blocks(keep, bit_count), blocks(swap(send, "seq", 1), bit_count)]

    hold = []
    if paired:
        back = Piece([pair_sum(back_keep, back_send)], every_bit)
        inner = Piece([pair_sum(in_keep, in_send)], every_bit)
        hold = [back_send, in_send]

    small = sds((16, half_w), F32)
    none = ([], [])
    d_hidden, d_attn, small_sum, out_send, out_keep = call(
        hidden_kernel,
        row_grid,
        [
            by_row(width),
            by_row(width),
            by_row(width),
            whole((1, width)),
            whole((width, width)),
            by_row(width),
            by_row(width),
        ],
        [by_row(width), by_row(width), whole((16, half_w)), whole((width, half_w)), whole((width, half_w))],
        [tok, tok, small, sds((width, half_w), BF), sds((width, half_w), BF)],
        scratch=[pltpu.VMEM((width, width), F32), pltpu.VMEM((8, width), F32)],
        free=(5,),
        vmem=44,
        flops=dense * (ff + 2 * width),
        nbytes=2 * tokens * ff,
        after=hold,
    )(meta, d_normed2, hidden, g, gain2, w_out, attn, linv)

    group_count = pairs // 2
    groups, dqs, gains = [], [], []
    for gi in range(group_count):
        if paired:
            if gi == 0:
                out_sum = pair_sum(out_keep, out_send)
                _, _, hold = shuttle(meta, half_w, [(back, (0,)), (inner, (1,))], none, [d_attn])
                hold.append(out_send)
            elif gi == 1:
                first = [out_sum, pair_sum(*groups[0])]
                hold = [groups[0][1]]
            else:
                first = Piece(first, every_bit)
                _, _, hold = shuttle(
                    meta, half_w, [(back, (1,)), (inner, (0,)), (first, (2,))], none, [dqs[1][0]]
                )
                second = pair_sum(*groups[1])
                hold.append(groups[1][1])

        def pair_at(s, m, gi=gi):
            return jnp.where(s == 0, 1 - m[1], m[1]) * group_count + gi

        def half_at(s, m):
            return jnp.where(s == 0, 1 - m[1], m[1])

        by_cols = pl.BlockSpec((2, th, PAIR), lambda s, m, f=pair_at: (0, 0, f(s, m)))
        to_cols = pl.BlockSpec((2, th, PAIR), lambda s, m: (0, 0, half_at(s, m)))
        weight_cols = [
            pl.BlockSpec((width, PAIR), lambda s, m, f=pair_at, at=at: (0, f(at, m))) for at in (0, 0, 0, 1, 1, 1)
        ]
        dq, dk, dv, send, keep, small_sum, gain = call(
            functools.partial(
                attn_back_kernel, dims=dims, base=base, buckets=buckets, pair_at=pair_at,
                place=(gi == 0, gi == group_count - 1),
            ),
            (2,),
            [by_cols] * 5
            + [
                pl.BlockSpec((2, na, la, la), lambda s, m, f=pair_at: (f(s, m), 0, 0, 0)),
                pl.BlockSpec((2, nb, lb, lb), lambda s, m, f=pair_at: (f(s, m), 0, 0, 0)),
                all_tok,
            ]
            + weight_cols
            + [whole((256, 128)), whole((1, width)), whole((16, half_w))]
            + [whole((width, 128))] * len(gains),
            [to_cols] * 3
            + [
                whole((width, 3 * PAIR)),
                whole((width, 3 * PAIR)),
                whole((16, half_w)),
                whole((width, 128)),
            ],
            [sds((2, th, 2 * PAIR), BF)] * 3
            + [
                sds((width, 3 * PAIR), BF),
                sds((width, 3 * PAIR), BF),
                small,
                sds((width, 128), F32),
            ],
            scratch=[
                pltpu.VMEM((2, strip_len, 128), F32),
                pltpu.VMEM((2, la, la), BF),
                pltpu.VMEM((2, lb, lb), BF),
                pltpu.VMEM((2, tokens, 3 * PAIR), BF),
            ],
            vmem=44,
        flops=score_macs * 256 * 8 // 3 + dense * width,
            nbytes=2 * score_macs // 3,
            after=hold,
        )(meta, q, k, v, d_attn, attn, pa, pb, normed, *([w_query, w_key, w_value] * 2), hot, gain1, small_sum, *gains)
        dqs.append((dq, dk, dv))
        gains = [gain]
        groups.append((keep, send))

    if paired:
        last = Piece([second, pair_sum(*groups[2])], every_bit, carrier=True)
        smalls = [small_sum, swap(small_sum, "seq", 1)]
        _, _, hold = shuttle(meta, half_w, [(back, (2,)), (inner, (2,)), (first, (0,))], none, [dqs[2][0]])
        hold += [groups[2][1], small_sum]

    def token_grads(part):
        of_part = lambda w: pl.BlockSpec((1, tile, w), lambda i, m: (part, i, 0))
        own = [of_core(shape_a), of_core(shape_b)]
        return call(
            tokens_kernel,
            (per,),
            [of_part(2 * PAIR)] * 9
            + [whole((width, width))] * 3
            + [of_part(width), of_part(width), whole((1, width))],
            [pl.BlockSpec((tile, width), lambda i, m: (i, 0))] if part else own,
            [sds((th, width), BF)] if part else [sds(all_a, BF), sds(all_b, BF)],
            vmem=28,
            free=(10, 11, 12),
            flops=3 * dense * width // 2,
            nbytes=7 * tokens * width,
            after=hold,
        )(meta, *(d[i] for i in range(3) for d in dqs), w_query, w_key, w_value, x, d_hidden, gain1)

    (grads1,) = token_grads(1)
    if paired:
        _, small_state, hold = shuttle(
            meta,
            half_w,
            [(back, (3,)), (inner, (3,)), (first, (1,)), (last, low_bits)],
            none,
            [grads1],
            (smalls, ()),
        )
        hold.append(grads1)
    out_rows = lambda w: pl.BlockSpec((1, tile, w), lambda i, m: (1 - i // per, i % per, 0))
    outs1, out_a, out_b = call(
        out_kernel,
        row_grid,
        [out_rows(ff), whole((ff, width)), out_rows(width)],
        [pl.BlockSpec((tile, width), lambda i, m: (jnp.minimum(i, per - 1), 0)), of_core(shape_a), of_core(shape_b)],
        [sds((th, width), BF), sds(all_a, BF), sds(all_b, BF)],
        vmem=34,
        free=(2,),
        flops=dense * ff,
        nbytes=2 * tokens * ff,
        after=hold,
    )(meta, low, w_back, hidden)
    if paired:
        r = width // nrows
        in_back = [(0, 0, ff // nrows, 0, half_w)]
        in_in = [(1, r * j, r, 0, half_w) for j in range(half_f // half_w)]
        (g_back, g_in), small_state, hold = shuttle(
            meta,
            half_w,
            [(first, (3,)), (last, high_bits)],
            ([back, inner], [in_back, in_in]),
            [],
            small_state,
            [grads1, outs1],
        )
        grads1_got, outs1_got = (swap(y, "seq", 1) for y in hold[-2:])
    grad_a, grad_b = token_grads(0)

    if paired:
        def of(col):
            at = [(0, r), (1, 0), (1, r)]
            return [(piece, row, r, PAIR * col, PAIR) for piece, row in at]

        (g_out, g_q, g_k, g_v), ((small_all,), _), _ = shuttle(
            meta,
            half_w,
            [],
            ([first, last], [[(0, 0, r, 0, half_w)], of(0), of(1), of(2)]),
            [grad_a],
            small_state,
        )
        out_a, out_b, grad_a, grad_b = call(
            functools.partial(place_kernel, dims=dims),
            (1,),
            [anywhere] * 6,
            [anywhere] * 4,
            [sds(all_a, BF), sds(all_b, BF)] * 2,
            scratch=copies,
            vmem=8,
            free=(1, 2),
            aliases={3: 0, 4: 1, 5: 2, 6: 3},
        )(meta, outs1_got, grads1_got, out_a, out_b, grad_a, grad_b)
    else:
        out_a, out_b = ungroup(out_a, out_b, outs1)
        grad_a, grad_b = ungroup(grad_a, grad_b, grads1)
        small_all = lax.psum(small_sum, ("rows", "seq"))

        def reduce(x):
            x = lax.psum_scatter(x.astype(F32), "rows", scatter_dimension=0, tiled=True)
            return lax.psum_scatter(x.astype(BF), "seq", scatter_dimension=1, tiled=True).astype(F32)

        def both(keep, send):
            return reduce(jnp.concatenate([keep, send], axis=1))

        g_back, g_in, g_out = both(back_keep, back_send), both(in_keep, in_send), both(out_keep, out_send)
        g_q, g_k, g_v = (
            reduce(
                jnp.concatenate([part[s][:, PAIR * i : PAIR * i + PAIR] for s in range(2) for part in groups], axis=1)
            )
            for i in range(3)
        )
    gain_one, gain_two = small_all[0:2].reshape(width), small_all[2:4].reshape(width)
    table_sum = small_all[4 : 4 + head_count, :buckets].T
    return (
        out_a, out_b, grad_a, grad_b, gain_one, g_q, g_k, g_v, g_out, table_sum, gain_two, g_in, g_back,
    )


def solution(mesh):
    split = P("rows", "seq", None)
    placed = (split, P("rows"), split, split, P("rows"), split) + (P(),) * 9
    shard = P("rows", "seq")
    return jax.shard_map(
        body,
        mesh=mesh,
        in_specs=placed,
        out_specs=(split, split, split, split, P(), shard, shard, shard, shard, P(), P(), shard, shard),
        check_vma=False,
    )
```

```python
import functools

import jax
import jax.numpy as jnp
from jax import lax
from jax.experimental import pallas as pl
from jax.experimental.pallas import tpu as pltpu
from jax.sharding import PartitionSpec as P

EPS = 1e-06
EDGES = (12, 16, 23, 32, 46, 64, 91)
MASKED = -1e30
C1 = 0.7978845608
C3 = 0.044715
BF = jnp.bfloat16
F32 = jnp.float32
HEAD = 64
PAIR = 2 * HEAD
MIB = 1 << 20


def dot(a, b, ca, cb):
    return lax.dot_general(a, b, (((ca,), (cb,)), ((), ())), preferred_element_type=F32)


def exact(a, b):
    return lax.dot_general(
        a, b, (((1,), (0,)), ((), ())), precision=lax.Precision.HIGHEST, preferred_element_type=F32
    )


def sds(shape, dtype):
    return jax.ShapeDtypeStruct(shape, dtype)


def call(kernel, grid, in_specs, out_specs, out_shape, scratch=(), flops=0, nbytes=0, vmem=60, after=(), free=(), aliases=None):
    count, extra = len(in_specs), len(after)

    def run(meta, *refs):
        kernel(meta, *refs[:count], *refs[count + extra :])

    def large(x):
        return x.size * x.dtype.itemsize >= MIB

    def put(x):
        return pltpu.HBM(x.shape, x.dtype) if large(x) else x

    in_specs = list(in_specs) + [pl.BlockSpec(memory_space=pl.ANY)] * extra
    made = pl.pallas_call(
        run,
        grid_spec=pltpu.PrefetchScalarGridSpec(
            num_scalar_prefetch=1,
            grid=grid,
            in_specs=in_specs,
            out_specs=out_specs,
            scratch_shapes=list(scratch),
        ),
        out_shape=[put(x) for x in out_shape] if isinstance(out_shape, list) else put(out_shape),
        input_output_aliases=aliases or {},
        compiler_params=pltpu.CompilerParams(vmem_limit_bytes=vmem * MIB),
        cost_estimate=pl.CostEstimate(flops=int(flops), bytes_accessed=int(nbytes), transcendentals=0),
    )

    def place(i, x):
        return pltpu.with_memory_space_constraint(x, pltpu.HBM) if large(x) and i not in free else x

    return lambda *args: made(*(place(i, x) for i, x in enumerate((*args, *after))))


def whole(shape):
    return pl.BlockSpec(shape, lambda *_: (0,) * len(shape))


def bucket_of(rel, buckets):
    n = jnp.abs(rel)
    far = jnp.full(rel.shape, 8, jnp.int32)
    for edge in EDGES:
        far = far + (n >= edge).astype(jnp.int32)
    return jnp.where(n < 8, n, far) + jnp.where(rel > 0, buckets // 2, 0)


def strip_kernel(meta, table, hot, strip, *, base, buckets):
    near0, near1 = base - 96, base + 224
    heads = strip.shape[0]
    lines = lax.dot_general(
        table[0], hot[...], (((1,), (1,)), ((), ())), precision=lax.Precision.HIGHEST, preferred_element_type=F32
    )
    shape = (near1 - near0, 128)
    rel = near0 - base + lax.broadcasted_iota(jnp.int32, shape, 0) - lax.broadcasted_iota(jnp.int32, shape, 1)
    for h in range(heads):
        wide = jnp.broadcast_to(lines[h : h + 1], (near1 - near0, 256))
        near = pltpu.roll(wide, 0, 1, stride=1, stride_axis=0)[:, :128]
        minus = table[0, h : h + 1, buckets // 2 - 1 : buckets // 2]
        plus = table[0, h : h + 1, buckets - 1 : buckets]
        strip[h, near0:near1, :] = jnp.where(rel >= EDGES[-1], plus, jnp.where(rel <= -EDGES[-1], minus, near))
        strip[h, :near0, :] = jnp.broadcast_to(minus, (near0, 128))
        strip[h, near1:, :] = jnp.broadcast_to(plus, (strip.shape[1] - near1, 128))


def moved(copies, sems):
    started = [pltpu.make_async_copy(src, dst, sems.at[i]) for i, (src, dst) in enumerate(copies)]
    for one in started:
        one.start()
    for one in started:
        one.wait()


def moved_on(copies, held, arrive, leave):
    first = [pltpu.make_async_copy(src, held.at[at], arrive.at[i]) for i, (src, at, _) in enumerate(copies)]
    then = [pltpu.make_async_copy(held.at[at], dst, leave.at[i]) for i, (_, at, dst) in enumerate(copies)]
    for one in first:
        one.start()
    for one, two in zip(first, then):
        one.wait()
        two.start()
    for two in then:
        two.wait()


def flat_rows(dims):
    na, la, nb, lb = dims
    first = [(0, s, pl.ds(s * la // 2, la // 2)) for s in range(na)]
    return first + [(1, s, pl.ds(na * la // 2 + s * lb // 2, lb // 2)) for s in range(nb)]


def pick_kernel(meta, ta, tb, ca, cb, out_x, out_g, held, arrive, leave, *, dims):
    first = [(1 - meta[1]) * n for n in (dims[0], dims[2])]
    moved_on(
        [
            (pair[kind].at[first[kind] + s], (i, rows), out.at[rows])
            for i, (pair, out) in enumerate((((ta, tb), out_x), ((ca, cb), out_g)))
            for kind, s, rows in flat_rows(dims)
        ],
        held,
        arrive,
        leave,
    )


def place_kernel(meta, out_got, grad_got, a0, b0, a1, b1, out_a, out_b, grad_a, grad_b, sems, *, dims):
    first = [(1 - meta[1]) * n for n in (dims[0], dims[2])]
    moved(
        [
            (got.at[rows], pair[kind].at[first[kind] + s])
            for got, pair in ((out_got, (out_a, out_b)), (grad_got, (grad_a, grad_b)))
            for kind, s, rows in flat_rows(dims)
        ],
        sems,
    )


def gathered(i, a, b, rest, out):
    @pl.when(i == 0)
    def _():
        out[...] = flat(a)

    @pl.when(i == 1)
    def _():
        out[...] = flat(b)

    @pl.when(i > 1)
    def _():
        out[...] = rest[...]


def qkv_kernel(meta, xa, xb, xr, gain, wq, wk, wv, x_ref, normed, q, k, v):
    gathered(pl.program_id(0), xa, xb, xr, x_ref.at[0])
    x = x_ref[0].astype(F32)
    r = lax.rsqrt(jnp.mean(x * x, axis=-1, keepdims=True) + EPS)
    n = (x * r * gain[...]).astype(BF)
    normed[0] = n
    q[0] = dot(n, wq[...], 1, 0).astype(BF)
    k[0] = dot(n, wk[...], 1, 0).astype(BF)
    v[0] = dot(n, wv[...], 1, 0).astype(BF)


def units_of(na, la, nb, lb):
    out = [(0, s, la, s * la // 2) for s in range(na)]
    return out + [(1, s, lb, na * la // 2 + s * lb // 2) for s in range(nb)]


def joined(ref, off, half):
    return jnp.concatenate([ref[0, off : off + half, :], ref[1, off : off + half, :]], axis=0)


def strip_rows(flip, base, size, cb, kh):
    half = size // 2
    plain = base - 128 * cb + half * kh
    if flip is None:
        return plain
    moved = (128 * cb + half) % size
    return pl.multiple_of(jnp.where(flip == 0, plain, base - moved + half * (1 - kh)), 128)


def lanes_of(shape, high):
    lane = lax.broadcasted_iota(jnp.int32, shape, len(shape) - 1)
    return (lane >= HEAD) == high


def half_mask(high):
    return jnp.where(lanes_of((1, PAIR), high), 1.0, 0.0).astype(BF)


def attn_kernel(meta, q, k, v, strip, pa, pb, attn, linv, kaug, *, dims, base, seqs_a):
    na, la, nb, lb = dims
    flip = meta[0]

    @pl.when(pl.program_id(0) == 0)
    def _():
        for kind, s, size, off in units_of(*dims):
            half = size // 2
            for kh in range(2):
                row = lax.broadcasted_iota(jnp.int32, (half, 128), 0)
                start = jnp.where(flip == 0, half * kh, half * (1 - kh))
                length = meta[4 + (meta[3] * na if kind == 0 else seqs_a + meta[3] * nb) + s]
                lane = lax.broadcasted_iota(jnp.int32, (half, 128), 1)
                gone = jnp.logical_and(row + start >= length, lane == 0)
                kaug[kh, off : off + half, :] = jnp.where(gone, MASKED, 0.0).astype(BF)

    low_lanes = lax.broadcasted_iota(jnp.int32, (1, PAIR), 1) < HEAD
    for kind, s, size, off in units_of(*dims):
        half = size // 2
        pref = pa if kind == 0 else pb
        q2, k2, v2 = joined(q, off, half), joined(k, off, half), joined(v, off, half)
        first = jnp.where(lax.broadcasted_iota(jnp.int32, (size, 128), 1) == 0, 1.0, 0.0).astype(BF)
        ones = jnp.ones((size, 128), BF)
        qa = jnp.concatenate([q2, first], axis=1)
        ka = joined(kaug, off, half)
        mixed, inverse = [], []
        for h in range(2):
            kk = jnp.concatenate([k2 * half_mask(h == 1), ka], axis=1)
            for c2 in range(size // 256):
                scores = dot(kk, qa[256 * c2 : 256 * c2 + 256], 1, 1)
                for sub in range(2):
                    cb = 2 * c2 + sub
                    bias = jnp.concatenate(
                        [strip[h, pl.ds(strip_rows(flip, base, size, cb, kh), half), :] for kh in range(2)], axis=0
                    )
                    one = scores[:, 128 * sub : 128 * sub + 128] + bias
                    e = jnp.exp(one - jnp.max(one, axis=0, keepdims=True))
                    pref[h, s, :, 128 * cb : 128 * cb + 128] = e.astype(BF)
            va = jnp.concatenate([v2 * half_mask(h == 1), ones], axis=1)
            both = dot(pref[h, s], va, 0, 0)
            inv = 1.0 / both[:, PAIR:]
            mixed.append(both[:, :PAIR] * inv)
            inverse.append(inv)
        o = (mixed[0] + mixed[1]).astype(BF)
        inv = jnp.where(low_lanes, inverse[0], inverse[1]).astype(BF)
        attn[0, off : off + half, :] = o[:half]
        attn[1, off : off + half, :] = o[half:]
        linv[0, off : off + half, :] = inv[:half]
        linv[1, off : off + half, :] = inv[half:]


def ffn_kernel(
    meta, attn, x, w_out, gain, ga, gb, gr, w_in, w_back,
    hidden, g_out, low, back_send, back_keep, in_send, in_keep, d_normed, normed, d_inner, acc, g, *, mixes, chunk,
):
    i = pl.program_id(0)
    th, tile = g.shape[1], x.shape[1]
    per = th // tile

    @pl.when(i < mixes)
    def _():
        h = x[0].astype(F32) + dot(attn[0], w_out[...], 1, 0)
        r = lax.rsqrt(jnp.mean(h * h, axis=-1, keepdims=True) + EPS)
        hidden[0] = h.astype(BF)
        at = pl.ds(pl.multiple_of((i % per) * tile, tile), tile)
        normed[i // per, at, :] = (h * r * gain[...]).astype(BF)
        gathered(i, ga, gb, gr, g_out.at[0])
        g[i // per, at, :] = g_out[0]

    @pl.when(i == mixes)
    def _():
        acc[...] = jnp.zeros_like(acc)

    @pl.when(i >= mixes)
    def _():
        for part in range(2):
            for lo in range(0, th, chunk):
                rows = slice(lo, lo + chunk)
                v = dot(normed[part, rows, :], w_in[...], 1, 0)
                gw = dot(g[part, rows, :], w_back[...], 1, 1)
                u = v * v
                up = 0.5 + 0.5 * jnp.tanh(v * (C1 + (C1 * C3) * u))
                low[part, rows, :] = (v * up).astype(BF)
                slope = up + up * ((1.0 - up) * (v * (2.0 * C1 + (6.0 * C1 * C3) * u)))
                inner = (gw * slope).astype(BF)
                d_inner[part, rows, :] = inner
                acc[part, rows, :] += dot(inner, w_in[...], 1, 1)
        split_columns(meta, dot(flat(low), flat(g), 0, 0), back_send, back_keep)
        value = dot(flat(normed), flat(d_inner), 0, 0).astype(BF)
        sending = i < mixes + (pl.num_programs(0) - mixes) // 2

        @pl.when(sending)
        def _():
            in_send[...] = value

        @pl.when(jnp.logical_not(sending))
        def _():
            in_keep[...] = value

    @pl.when(i == pl.num_programs(0) - 1)
    def _():
        d_normed[...] = acc[...].astype(BF)


def flat(ref):
    a = ref[...]
    return a.reshape(a.shape[0] * a.shape[1], a.shape[2])


def split_columns(meta, value, send, keep):
    half = value.shape[1] // 2
    lo, hi = value[:, :half].astype(BF), value[:, half:].astype(BF)
    first = meta[1] == 0

    @pl.when(first)
    def _():
        keep[...] = lo
        send[...] = hi

    @pl.when(jnp.logical_not(first))
    def _():
        keep[...] = hi
        send[...] = lo


def rows8(value):
    return jnp.sum(value.reshape(value.shape[0] // 8, 8, value.shape[1]), axis=0)


def hidden_kernel(meta, d_normed, hidden, g, gain, w_out, attn, linv, d_hidden, d_attn, small, send, keep, acc, gains):
    i, last = pl.program_id(0), pl.num_programs(0) - 1
    dn = d_normed[0].astype(F32)
    h = hidden[0].astype(F32)
    r = lax.rsqrt(jnp.mean(h * h, axis=-1, keepdims=True) + EPS)
    gained = dn * gain[...]
    mean = jnp.mean(gained * h, axis=-1, keepdims=True)
    dh = (g[0].astype(F32) + r * gained - h * (r * r * r * mean)).astype(BF)
    d_hidden[0] = dh
    d_attn[0] = (dot(dh, w_out[...], 1, 1) * linv[0].astype(F32)).astype(BF)
    part = rows8(dn * h * r)
    product = dot(attn[0], dh, 0, 0)

    @pl.when(i == 0)
    def _():
        gains[...] = part
        acc[...] = product

    @pl.when(i > 0)
    def _():
        gains[...] += part
        acc[...] += product

    @pl.when(i == last)
    def _():
        split_columns(meta, acc[...], send, keep)
        line = jnp.sum(gains[...], axis=0, keepdims=True)
        half = small.shape[1]
        small[...] = jnp.zeros_like(small)
        small[2:3, :] = line[:, :half]
        small[3:4, :] = line[:, half:]


def table_sums(strip, hot, base, buckets):
    near0, near1 = base - 96, base + 224
    lines, ends = [], []
    for h in range(strip.shape[0]):
        near = strip[h, near0:near1, :]
        rel = (
            near0 - base + lax.broadcasted_iota(jnp.int32, near.shape, 0) - lax.broadcasted_iota(jnp.int32, near.shape, 1)
        )
        plus = rows8(strip[h, near1:, :]) + rows8(jnp.where(rel >= 128, near, 0.0))
        minus = rows8(strip[h, :near0, :]) + rows8(jnp.where(rel <= -128, near, 0.0))
        wide = jnp.where(jnp.abs(rel) < 128, near, 0.0)
        wide = jnp.concatenate([wide, jnp.zeros_like(wide)], axis=1)
        line = jnp.zeros((8, 256), F32)
        for r in range(0, near1 - near0, 8):
            line = line + pltpu.roll(wide[r : r + 8], -r % 256, 1)
        one = jnp.zeros((8, 256), F32)
        row = lax.broadcasted_iota(jnp.int32, (8, 256), 0)
        for r in range(8):
            one = one + pltpu.roll(jnp.where(row == r, line, 0.0), -r % 256, 1)
        lines.append(jnp.sum(one, axis=0, keepdims=True))
        ends.append((jnp.sum(plus, keepdims=True), jnp.sum(minus, keepdims=True)))
    fill = [jnp.zeros((8 - len(lines), 256), F32)]
    sums = exact(jnp.concatenate(lines + fill, axis=0), hot[...])
    lane = lax.broadcasted_iota(jnp.int32, (8, 128), 1)
    row = lax.broadcasted_iota(jnp.int32, (8, 128), 0)
    for h, (plus, minus) in enumerate(ends):
        here = row == h
        sums = sums + jnp.where(jnp.logical_and(here, lane == buckets - 1), plus, 0.0)
        sums = sums + jnp.where(jnp.logical_and(here, lane == buckets // 2 - 1), minus, 0.0)
    return sums


def attn_back_kernel(
    meta, q, k, v, do, at_ref, pa, pb, normed, wqs, wks, wvs, wqk, wkk, wvk, hot, gain_attn, small_in, *rest, dims, base, buckets, pair_at, place
):
    before = [] if place[0] else [rest[0]]
    dq, dk, dv, send, keep, small, gain, strip, dsa, dsb, cat = rest[len(before) :]
    flip = meta[0]
    step = pl.program_id(0)
    th = normed.shape[1]
    strip[...] = jnp.zeros_like(strip)
    lane = lax.broadcasted_iota(jnp.int32, (1, PAIR), 1)
    minus = jnp.where(lane < 2, -1.0, 0.0).astype(BF)
    for kind, s, size, off in units_of(*dims):
        half = size // 2
        pref = pa if kind == 0 else pb
        ds_ref = dsa if kind == 0 else dsb
        q2, k2, v2, o2, a2 = (joined(ref, off, half) for ref in (q, k, v, do, at_ref))
        prod = o2.astype(F32) * a2.astype(F32)
        dvs, dks, dqs = [], [], []
        for h in range(2):
            mask = half_mask(h == 1)
            delta = jnp.sum(jnp.where((lane >= HEAD) == (h == 1), prod, 0.0), axis=1, keepdims=True)
            high = delta.astype(BF).astype(F32)
            cols = jnp.where(lane == 0, high, jnp.where(lane == 1, delta - high, 0.0)).astype(BF)
            va = jnp.concatenate([v2 * mask, jnp.broadcast_to(minus, (size, PAIR))], axis=1)
            oa = jnp.concatenate([o2, cols], axis=1)
            for c2 in range(size // 256):
                dp = dot(va, oa[256 * c2 : 256 * c2 + 256], 1, 1)
                for sub in range(2):
                    cb = 2 * c2 + sub
                    cs = slice(128 * cb, 128 * cb + 128)
                    ds = pref[h, s, :, cs].astype(F32) * dp[:, 128 * sub : 128 * sub + 128]
                    for kh in range(2):
                        at = pl.ds(strip_rows(flip, base, size, cb, kh), half)
                        strip[h, at, :] += ds[half * kh : half * kh + half]
                    ds_ref[h, :, cs] = ds.astype(BF)
            dvs.append(dot(pref[h, s], o2 * mask, 1, 0))
            dks.append(dot(ds_ref[h], q2 * mask, 1, 0))
            dqs.append(dot(ds_ref[h], k2 * mask, 0, 0))
        d_v = (dvs[0] + dvs[1]).astype(BF)
        d_k = (dks[0] + dks[1]).astype(BF)
        d_q = (dqs[0] + dqs[1]).astype(BF)
        for part in range(2):
            rows = slice(off, off + half)
            got = slice(part * half, part * half + half)
            dq[part, rows, :] = d_q[got]
            dk[part, rows, :] = d_k[got]
            dv[part, rows, :] = d_v[got]
            at = slice(part * th + off, part * th + off + half)
            cat[step, at, 0:128] = d_q[got]
            cat[step, at, 128:256] = d_k[got]
            cat[step, at, 256:384] = d_v[got]
    @pl.when(step == 0)
    def _():
        small[...] = small_in[...]

    sums = table_sums(strip, hot, base, buckets)
    row = lax.broadcasted_iota(jnp.int32, (small.shape[0], 128), 0) - (4 + 2 * pair_at(step, meta))
    small[:, 0:128] += jnp.where(row == 0, sums[0:1], jnp.where(row == 1, sums[1:2], 0.0))

    @pl.when(step == 1)
    def _():
        both = jnp.concatenate([cat[0], cat[1]], axis=1)
        value = dot(flat(normed), both, 0, 0)
        send[...] = value[:, :384].astype(BF)
        keep[...] = value[:, 384:].astype(BF)
        part = sum(
            value[:, 128 * i : 128 * i + 128] * w[...].astype(F32) for i, w in enumerate((wqs, wks, wvs, wqk, wkk, wvk))
        )
        for ref in before:
            part = part + ref[...]
        gain[...] = part
        if place[1]:
            high = part.astype(BF)
            low = (part - high.astype(F32)).astype(BF)
            ones = jnp.ones((16, 128), BF)
            line = (dot(ones, high, 1, 1) + dot(ones, low, 1, 1))[:1] / gain_attn[...]
            half = small.shape[1]
            small[0:1, :] += line[:, :half]
            small[1:2, :] += line[:, half:]


def spread(i, value, first, second):
    @pl.when(i == 0)
    def _():
        first[...] = value.reshape(first.shape)

    @pl.when(i == 1)
    def _():
        second[...] = value.reshape(second.shape)


def out_kernel(meta, low, w_back, hidden, give, out_a, out_b):
    i = pl.program_id(0)
    value = (hidden[0].astype(F32) + dot(low[0], w_back[...], 1, 0)).astype(BF)

    @pl.when(i < 2)
    def _():
        give[...] = value

    spread(i - 2, value, out_a, out_b)


def tokens_kernel(meta, *refs):
    wq, wk, wv, x_ref, d_hidden, gain = refs[9:15]
    outs = refs[15:]

    def columns(of):
        return jnp.concatenate([r[0, :, :PAIR] for r in of] + [r[0, :, PAIR:] for r in of], axis=1)

    dq, dk, dv = columns(refs[0:3]), columns(refs[3:6]), columns(refs[6:9])
    dn = dot(dq, wq[...], 1, 1) + dot(dk, wk[...], 1, 1) + dot(dv, wv[...], 1, 1)
    x = x_ref[0].astype(F32)
    r = lax.rsqrt(jnp.mean(x * x, axis=-1, keepdims=True) + EPS)
    gained = dn * gain[...]
    mean = jnp.mean(gained * x, axis=-1, keepdims=True)
    value = (d_hidden[0].astype(F32) + r * gained - x * (r * r * r * mean)).astype(BF)
    if len(outs) == 1:
        outs[0][...] = value
    else:
        spread(pl.program_id(0), value, *outs)


def swap(x, axis, bit):
    n = lax.axis_size(axis)
    return lax.ppermute(x, axis, [(i, i ^ bit) for i in range(n)])


TAIL = 32


class Piece:
    def __init__(self, parts, bits_left, carrier=False):
        self.parts, self.left, self.carrier, self.flat = parts, bits_left, carrier, 0

    def rows(self, cols):
        return self.flat or sum(t[0].shape[-2] * t[0].shape[-1] // cols for t in self.parts)

    def count(self, bits):
        return 1 << (len(self.left) - len(bits))


def blocks(x, bits):
    return x.reshape((2,) * bits + (x.shape[0] >> bits, x.shape[1]))


def masks_of(bits):
    return [tuple((m >> i) & 1 for i in range(len(bits))) for m in range(1 << len(bits))]


def shuttle(meta, cols, work, finals, after, small=((), ()), through=()):
    pieces, results = finals
    ins = []

    def slot(x):
        for i, y in enumerate(ins):
            if y is x:
                return i
        ins.append(x)
        return len(ins) - 1

    every = [piece for piece, _ in work] + pieces
    slots = []
    received = set()
    for piece in every:
        for terms in piece.parts:
            received |= {1 + slot(t[0] if piece.flat else t) for t in terms[1:]}
        slots.append([[(slot(t[0]), t[1]) if piece.flat else (slot(t), 0) for t in terms] for terms in piece.parts])
    small_at, tail_at = [slot(x) for x in small[0]], [slot(x) for x in small[1]]
    messages = {}
    for number, (piece, bits) in enumerate(work):
        for mask in masks_of(bits):
            wide = sum(flip << b for flip, b in zip(mask, bits))
            entry = messages.setdefault(wide, [0, False, []])
            entry[2].append((number, mask, entry[0]))
            entry[0] += piece.count(bits) * piece.rows(cols)
            entry[1] |= piece.carrier and wide > 0
    outs = [sds((rows + (TAIL if tail else 0), cols), BF) for rows, tail, _ in messages.values()]
    outs += [sds((spans[0][2], sum(s[4] for s in spans)), F32) for spans in results]
    if small_at:
        outs.append(sds(small[0][0].shape, F32))

    def kernel(meta, *refs):
        got, put = refs[: len(ins)], list(refs[len(ins) + len(through) : len(ins) + len(through) + len(outs)])
        row = meta[2]
        if small_at:
            total = sum(got[i][...] for i in small_at)
            for i in tail_at:
                end = got[i].shape[0]
                tail = got[i][end - TAIL : end, :].astype(F32)
                total = total + tail[: TAIL // 2] + tail[TAIL // 2 :]
            put[-1][...] = total
            high = total.astype(BF).astype(F32)
            tail = jnp.concatenate([high, total - high], axis=0).astype(BF)

        def take(piece, terms, index):
            if not piece.flat:
                return sum(got[i][index].astype(F32) for i, _ in terms)
            at = 0
            for bit in index:
                at = 2 * at + bit
            value = 0.0
            for i, low in terms:
                start = low + at * piece.flat
                value = value + got[i][pl.ds(pl.multiple_of(start, 16) if index else start, piece.flat), :].astype(F32)
            return value

        for (rows, tailed, entries), out in zip(messages.values(), put):
            for number, mask, low in entries:
                piece, bits = work[number]
                rest = [b for b in piece.left if b not in bits]
                for m in range(1 << len(rest)):
                    chosen = {b: (m >> i) & 1 for i, b in enumerate(rest)}
                    for b, flip in zip(bits, mask):
                        chosen[b] = ((row >> b) & 1) ^ flip
                    index = tuple(chosen[b] for b in reversed(piece.left))
                    for terms in slots[number]:
                        value = take(piece, terms, index).astype(BF)
                        high = value.shape[0]
                        for c in range(0, value.shape[1], cols):
                            out[low : low + high, :] = value[:, c : c + cols]
                            low += high
            if tailed:
                out[rows : rows + TAIL, :] = tail
        sums = [take(piece, slots[len(work) + i][0], ()) for i, piece in enumerate(pieces)]
        for spans, out in zip(results, put[len(messages) :]):
            low = 0
            for piece, r0, r, c0, c in spans:
                out[:, low : low + c] = sums[piece][r0 : r0 + r, c0 : c0 + c]
                low += c

    made = call(
        kernel,
        (1,),
        [whole(x.shape) for x in ins] + [pl.BlockSpec(memory_space=pl.ANY)] * len(through),
        [whole(x.shape) for x in outs] + [pl.BlockSpec(memory_space=pl.ANY)] * len(through),
        outs + [sds(x.shape, x.dtype) for x in through],
        nbytes=sum(x.size * 2 for x in ins),
        vmem=30,
        free=tuple(received),
        after=after,
        aliases={1 + len(ins) + i: len(outs) + i for i in range(len(through))},
    )(meta, *ins, *through)
    made, passed = list(made[: len(outs)]), made[len(outs) :]
    got = {wide: swap(x, "rows", wide) if wide else x for wide, x in zip(messages, made)}
    tails = []
    for number, (piece, bits) in enumerate(work):
        rows = piece.rows(cols)
        terms = []
        for wide, (_, tailed, entries) in messages.items():
            for other, _, low in entries:
                if other == number:
                    terms.append((got[wide], low))
                    if piece.carrier and tailed:
                        tails.append(got[wide])
        piece.parts, piece.flat = [terms], rows
        piece.left = tuple(b for b in piece.left if b not in bits)
    ends = len(messages) + len(results)
    return made[len(messages) : ends], (made[ends:], tails), [*made[: len(messages)], *passed]


def body(
    tokens_a, lengths_a, cotangent_a, tokens_b, lengths_b, cotangent_b,
    gain_attn, w_query, w_key, w_value, w_out, relative_bias_table, gain_ffn, w_in, w_back,
):
    nseq, nrows = lax.axis_size("seq"), lax.axis_size("rows")
    c = lax.axis_index("seq")
    width = tokens_a.shape[2]
    ff = w_in.shape[1]
    buckets, head_count = relative_bias_table.shape
    la, lb = tokens_a.shape[1] * nseq, tokens_b.shape[1] * nseq
    na, nb = tokens_a.shape[0] // nseq, tokens_b.shape[0] // nseq
    dims = (na, la, nb, lb)
    th = (na * la + nb * lb) // 2
    tokens = 2 * th
    base = la - 128
    strip_len = 2 * la - 128
    pairs = head_count // 2
    paired = nseq == 2 and nrows == 16

    me = c if paired else jnp.int32(0)
    flip = me
    meta = jnp.concatenate(
        [jnp.stack([flip, me, lax.axis_index("rows"), c]).astype(jnp.int32), lengths_a, lengths_b]
    )
    gain1, gain2 = gain_attn[None], gain_ffn[None]

    tile = th // 2
    per = 2
    row_grid = (2 * per,)
    by_row = lambda w: pl.BlockSpec((1, tile, w), lambda i, m: (i // per, i % per, 0))
    dense = 2 * tokens * width
    shape_a, shape_b = (na, la // 2, width), (nb, lb // 2, width)
    of_core = lambda shape: pl.BlockSpec(shape, lambda i, m: (m[1], 0, 0))
    of_other = lambda shape: pl.BlockSpec(shape, lambda i, m: (1 - m[1], 0, 0))
    cores = 2 if paired else 1
    all_a, all_b = (cores * na,) + shape_a[1:], (cores * nb,) + shape_b[1:]
    cut = na * la // 2

    def regroup(a, b):
        def one(x):
            got = lax.all_to_all(x, "seq", 0, 1, tiled=True)
            n, size, _ = got.shape
            return got.reshape(n, 2, size // 2, width).transpose(1, 0, 2, 3)

        whole_a, whole_b = one(a), one(b)
        rest = jnp.concatenate([whole_a[1].reshape(-1, width), whole_b[1].reshape(-1, width)], axis=0)
        return whole_a[0], whole_b[0], rest

    def ungroup(own_a, own_b, rest):
        def one(own, other, n, size):
            y = jnp.stack([own, other.reshape(own.shape)], axis=1).reshape(n, size, width)
            return lax.all_to_all(y, "seq", 1, 0, tiled=True)

        return one(own_a, rest[:cut], na, la), one(own_b, rest[cut:], nb, lb)

    received = pl.BlockSpec((tile, width), lambda i, m: (jnp.clip(i - per, 0, per - 1), 0))
    anywhere = pl.BlockSpec(memory_space=pl.ANY)
    copies = [pltpu.SemaphoreType.DMA((2 * (na + nb),))]
    in_vmem = pl.BlockSpec(memory_space=pltpu.VMEM)
    if paired:
        give = call(
            functools.partial(pick_kernel, dims=dims),
            (1,),
            [anywhere] * 4,
            [anywhere] * 2,
            [sds((th, width), BF)] * 2,
            scratch=[pltpu.VMEM((2, th, width), BF)] + copies * 2,
            nbytes=8 * th * width,
            vmem=8,
        )(meta, tokens_a, tokens_b, cotangent_a, cotangent_b)
        x_in = (tokens_a, tokens_b, swap(give[0], "seq", 1))
        g_in3 = (cotangent_a, cotangent_b, swap(give[1], "seq", 1))
    else:
        x_in = regroup(tokens_a, tokens_b)
        g_in3 = regroup(cotangent_a, cotangent_b)
    lane = jnp.arange(256, dtype=jnp.int32)
    back_rel = ((-96 - lane + 128 + 512) & 255) - 128
    hot = jnp.logical_and(
        bucket_of(back_rel, buckets)[:, None] == jnp.arange(128, dtype=jnp.int32)[None], back_rel[:, None] > -128
    ).astype(F32)

    at_once = 4
    rows_of_table = jnp.pad(
        relative_bias_table.T.reshape(head_count // at_once, at_once, buckets), ((0, 0), (0, 4), (0, 128 - buckets))
    )
    strip = call(
        functools.partial(strip_kernel, base=base, buckets=buckets),
        (head_count // at_once,),
        [pl.BlockSpec((1, 8, 128), lambda h, m: (h, 0, 0)), whole((256, 128))],
        pl.BlockSpec((at_once, strip_len, 128), lambda h, m: (h, 0, 0)),
        sds((head_count, strip_len, 128), F32),
        vmem=16,
        nbytes=4 * head_count * strip_len * 128,
    )(meta, rows_of_table, hot)

    tok = sds((2, th, width), BF)
    x, normed, q, k, v = call(
        qkv_kernel,
        row_grid,
        [of_core(shape_a), of_core(shape_b), received, whole((1, width))] + [whole((width, width))] * 3,
        [by_row(width)] * 5,
        [tok] * 5,
        vmem=30,
        free=(3, 5, 6, 7),
        flops=3 * dense * width,
        nbytes=10 * tokens * width,
        after=[strip],
    )(meta, *x_in, gain1, w_query, w_key, w_value)

    by_pair = pl.BlockSpec((2, th, PAIR), lambda p, m: (0, 0, p))
    pa_shape, pb_shape = (head_count, na, la, la), (head_count, nb, lb, lb)
    score_macs = head_count * (na * la * la + nb * lb * lb)
    pa, pb, attn, linv = call(
        functools.partial(attn_kernel, dims=dims, base=base, seqs_a=tokens_a.shape[0]),
        (pairs,),
        [by_pair] * 3 + [pl.BlockSpec((2, strip_len, 128), lambda p, m: (p, 0, 0))],
        [
            pl.BlockSpec((2, na, la, la), lambda p, m: (p, 0, 0, 0)),
            pl.BlockSpec((2, nb, lb, lb), lambda p, m: (p, 0, 0, 0)),
            by_pair,
            by_pair,
        ],
        [sds(pa_shape, BF), sds(pb_shape, BF), tok, tok],
        scratch=[pltpu.VMEM((2, th, 128), BF)],
        vmem=34,
        flops=score_macs * 256 * 4,
        nbytes=2 * score_macs,
    )(meta, q, k, v, strip)

    all_tok = whole((2, th, width))
    fb = 512
    half_w, half_f, nf, mixes = width // 2, ff // 2, ff // fb, 2 * per

    def unit_at(i, m):
        return (jnp.maximum(i - mixes, 0) + (1 - m[1]) * (nf // 2)) % nf

    def mix_at(i):
        return jnp.minimum(i, mixes - 1)

    mix_rows = pl.BlockSpec((1, tile, width), lambda i, m: (mix_at(i) // per, mix_at(i) % per, 0))
    unit_rows = pl.BlockSpec((fb, half_w), lambda i, m: (unit_at(i, m), 0))
    hidden, g, low, back_send, back_keep, in_send, in_keep, d_normed2 = call(
        functools.partial(ffn_kernel, mixes=mixes, chunk=min(512, th)),
        (mixes + nf,),
        [
            mix_rows,
            mix_rows,
            whole((width, width)),
            whole((1, width)),
            of_core(shape_a),
            of_core(shape_b),
            received,
            pl.BlockSpec((width, fb), lambda i, m: (0, unit_at(i, m))),
            pl.BlockSpec((fb, width), lambda i, m: (unit_at(i, m), 0)),
        ],
        [
            mix_rows,
            mix_rows,
            pl.BlockSpec((2, th, fb), lambda i, m: (0, 0, unit_at(i, m))),
            unit_rows,
            unit_rows,
            pl.BlockSpec((width, fb), lambda i, m: (0, jnp.clip(i - mixes, 0, nf // 2 - 1))),
            pl.BlockSpec((width, fb), lambda i, m: (0, jnp.maximum(i - mixes - nf // 2, 0))),
            all_tok,
        ],
        [tok, tok, sds((2, th, ff), BF)]
        + [sds((ff, half_w), BF)] * 2
        + [sds((width, half_f), BF)] * 2
        + [tok],
        scratch=[
            pltpu.VMEM((2, th, width), BF),
            pltpu.VMEM((2, th, fb), BF),
            pltpu.VMEM((2, th, width), F32),
            pltpu.VMEM((2, th, width), BF),
        ],
        flops=dense * (5 * ff + width),
        nbytes=2 * tokens * ff,
        vmem=52,
        free=(3, 7, 8, 9),
    )(meta, attn, x, w_out, gain2, *g_in3, w_in, w_back)

    bit_count = nrows.bit_length() - 1
    low_bits, high_bits = (0, 1), tuple(range(2, bit_count))
    every_bit = tuple(range(bit_count))

    def pair_sum(keep, send):
        return [blocks(keep, bit_count), blocks(swap(send, "seq", 1), bit_count)]

    hold = []
    if paired:
        back = Piece([pair_sum(back_keep, back_send)], every_bit)
        inner = Piece([pair_sum(in_keep, in_send)], every_bit)
        hold = [back_send, in_send]

    small = sds((16, half_w), F32)
    none = ([], [])
    d_hidden, d_attn, small_sum, out_send, out_keep = call(
        hidden_kernel,
        row_grid,
        [
            by_row(width),
            by_row(width),
            by_row(width),
            whole((1, width)),
            whole((width, width)),
            by_row(width),
            by_row(width),
        ],
        [by_row(width), by_row(width), whole((16, half_w)), whole((width, half_w)), whole((width, half_w))],
        [tok, tok, small, sds((width, half_w), BF), sds((width, half_w), BF)],
        scratch=[pltpu.VMEM((width, width), F32), pltpu.VMEM((8, width), F32)],
        free=(5,),
        vmem=44,
        flops=dense * (ff + 2 * width),
        nbytes=2 * tokens * ff,
        after=hold,
    )(meta, d_normed2, hidden, g, gain2, w_out, attn, linv)

    group_count = pairs // 2
    groups, dqs, gains = [], [], []
    for gi in range(group_count):
        if paired:
            if gi == 0:
                out_sum = pair_sum(out_keep, out_send)
                _, _, hold = shuttle(meta, half_w, [(back, (0,)), (inner, (1,))], none, [d_attn])
                hold.append(out_send)
            elif gi == 1:
                first = [out_sum, pair_sum(*groups[0])]
                hold = [groups[0][1]]
            else:
                first = Piece(first, every_bit)
                _, _, hold = shuttle(
                    meta, half_w, [(back, (1,)), (inner, (2,)), (first, (0,))], none, [dqs[1][0]]
                )
                second = pair_sum(*groups[1])
                hold.append(groups[1][1])

        def pair_at(s, m, gi=gi):
            return jnp.where(s == 0, 1 - m[1], m[1]) * group_count + gi

        def half_at(s, m):
            return jnp.where(s == 0, 1 - m[1], m[1])

        by_cols = pl.BlockSpec((2, th, PAIR), lambda s, m, f=pair_at: (0, 0, f(s, m)))
        to_cols = pl.BlockSpec((2, th, PAIR), lambda s, m: (0, 0, half_at(s, m)))
        weight_cols = [
            pl.BlockSpec((width, PAIR), lambda s, m, f=pair_at, at=at: (0, f(at, m))) for at in (0, 0, 0, 1, 1, 1)
        ]
        dq, dk, dv, send, keep, small_sum, gain = call(
            functools.partial(
                attn_back_kernel, dims=dims, base=base, buckets=buckets, pair_at=pair_at,
                place=(gi == 0, gi == group_count - 1),
            ),
            (2,),
            [by_cols] * 5
            + [
                pl.BlockSpec((2, na, la, la), lambda s, m, f=pair_at: (f(s, m), 0, 0, 0)),
                pl.BlockSpec((2, nb, lb, lb), lambda s, m, f=pair_at: (f(s, m), 0, 0, 0)),
                all_tok,
            ]
            + weight_cols
            + [whole((256, 128)), whole((1, width)), whole((16, half_w))]
            + [whole((width, 128))] * len(gains),
            [to_cols] * 3
            + [
                whole((width, 3 * PAIR)),
                whole((width, 3 * PAIR)),
                whole((16, half_w)),
                whole((width, 128)),
            ],
            [sds((2, th, 2 * PAIR), BF)] * 3
            + [
                sds((width, 3 * PAIR), BF),
                sds((width, 3 * PAIR), BF),
                small,
                sds((width, 128), F32),
            ],
            scratch=[
                pltpu.VMEM((2, strip_len, 128), F32),
                pltpu.VMEM((2, la, la), BF),
                pltpu.VMEM((2, lb, lb), BF),
                pltpu.VMEM((2, tokens, 3 * PAIR), BF),
            ],
            free=(8, 9, 10, 11, 12, 13, 14),
            vmem=40,
        flops=score_macs * 256 * 8 // 3 + dense * width,
            nbytes=2 * score_macs // 3,
            after=hold,
        )(meta, q, k, v, d_attn, attn, pa, pb, normed, *([w_query, w_key, w_value] * 2), hot, gain1, small_sum, *gains)
        dqs.append((dq, dk, dv))
        gains = [gain]
        groups.append((keep, send))

    if paired:
        last = Piece([second, pair_sum(*groups[2])], every_bit, carrier=True)
        smalls = [small_sum, swap(small_sum, "seq", 1)]
        _, _, hold = shuttle(meta, half_w, [(back, (2,)), (inner, (0,)), (first, (1,))], none, [dqs[2][0]])
        hold += [groups[2][1], small_sum]

    def token_grads(part):
        of_part = lambda w: pl.BlockSpec((1, tile, w), lambda i, m: (part, i, 0))
        own = [of_core(shape_a), of_core(shape_b)]
        return call(
            tokens_kernel,
            (per,),
            [of_part(2 * PAIR)] * 9
            + [whole((width, width))] * 3
            + [of_part(width), of_part(width), whole((1, width))],
            [pl.BlockSpec((tile, width), lambda i, m: (i, 0))] if part else own,
            [sds((th, width), BF)] if part else [sds(all_a, BF), sds(all_b, BF)],
            vmem=28,
            free=(10, 11, 12),
            flops=3 * dense * width // 2,
            nbytes=7 * tokens * width,
            after=hold,
        )(meta, *(d[i] for i in range(3) for d in dqs), w_query, w_key, w_value, x, d_hidden, gain1)

    (grads1,) = token_grads(1)
    if paired:
        _, small_state, hold = shuttle(
            meta,
            half_w,
            [(back, (3,)), (inner, (3,)), (first, (2,)), (last, low_bits)],
            none,
            [grads1],
            (smalls, ()),
        )
        hold.append(grads1)
    out_rows = lambda w: pl.BlockSpec((1, tile, w), lambda i, m: (1 - i // per, i % per, 0))
    outs1, out_a, out_b = call(
        out_kernel,
        row_grid,
        [out_rows(ff), whole((ff, width)), out_rows(width)],
        [pl.BlockSpec((tile, width), lambda i, m: (jnp.minimum(i, per - 1), 0)), of_core(shape_a), of_core(shape_b)],
        [sds((th, width), BF), sds(all_a, BF), sds(all_b, BF)],
        vmem=34,
        free=(2,),
        flops=dense * ff,
        nbytes=2 * tokens * ff,
        after=hold,
    )(meta, low, w_back, hidden)
    if paired:
        r = width // nrows
        in_back = [(0, 0, ff // nrows, 0, half_w)]
        in_in = [(1, r * j, r, 0, half_w) for j in range(half_f // half_w)]
        (g_back, g_in), small_state, hold = shuttle(
            meta,
            half_w,
            [(first, (3,)), (last, high_bits)],
            ([back, inner], [in_back, in_in]),
            [],
            small_state,
            [grads1, outs1],
        )
        grads1_got, outs1_got = (swap(y, "seq", 1) for y in hold[-2:])
    grad_a, grad_b = token_grads(0)

    if paired:
        def of(col):
            at = [(0, r), (1, 0), (1, r)]
            return [(piece, row, r, PAIR * col, PAIR) for piece, row in at]

        (g_out, g_q, g_k, g_v), ((small_all,), _), _ = shuttle(
            meta,
            half_w,
            [],
            ([first, last], [[(0, 0, r, 0, half_w)], of(0), of(1), of(2)]),
            [grad_a],
            small_state,
        )
        out_a, out_b, grad_a, grad_b = call(
            functools.partial(place_kernel, dims=dims),
            (1,),
            [in_vmem] * 2 + [anywhere] * 4,
            [anywhere] * 4,
            [sds(all_a, BF), sds(all_b, BF)] * 2,
            scratch=copies,
            vmem=8,
            free=(1, 2),
            aliases={3: 0, 4: 1, 5: 2, 6: 3},
        )(meta, outs1_got, grads1_got, out_a, out_b, grad_a, grad_b)
    else:
        out_a, out_b = ungroup(out_a, out_b, outs1)
        grad_a, grad_b = ungroup(grad_a, grad_b, grads1)
        small_all = lax.psum(small_sum, ("rows", "seq"))

        def reduce(x):
            x = lax.psum_scatter(x.astype(F32), "rows", scatter_dimension=0, tiled=True)
            return lax.psum_scatter(x.astype(BF), "seq", scatter_dimension=1, tiled=True).astype(F32)

        def both(keep, send):
            return reduce(jnp.concatenate([keep, send], axis=1))

        g_back, g_in, g_out = both(back_keep, back_send), both(in_keep, in_send), both(out_keep, out_send)
        g_q, g_k, g_v = (
            reduce(
                jnp.concatenate([part[s][:, PAIR * i : PAIR * i + PAIR] for s in range(2) for part in groups], axis=1)
            )
            for i in range(3)
        )
    gain_one, gain_two = small_all[0:2].reshape(width), small_all[2:4].reshape(width)
    table_sum = small_all[4 : 4 + head_count, :buckets].T
    return (
        out_a, out_b, grad_a, grad_b, gain_one, g_q, g_k, g_v, g_out, table_sum, gain_two, g_in, g_back,
    )


def solution(mesh):
    split = P("rows", "seq", None)
    placed = (split, P("rows"), split, split, P("rows"), split) + (P(),) * 9
    shard = P("rows", "seq")
    return jax.shard_map(
        body,
        mesh=mesh,
        in_specs=placed,
        out_specs=(split, split, split, split, P(), shard, shard, shard, shard, P(), P(), shard, shard),
        check_vma=False,
    )
```

```python
import functools

import jax
import jax.numpy as jnp
from jax import lax
from jax.experimental import pallas as pl
from jax.experimental.pallas import tpu as pltpu
from jax.sharding import PartitionSpec as P

EPS = 1e-06
EDGES = (12, 16, 23, 32, 46, 64, 91)
MASKED = -1e30
C1 = 0.7978845608
C3 = 0.044715
BF = jnp.bfloat16
F32 = jnp.float32
HEAD = 64
PAIR = 2 * HEAD
MIB = 1 << 20


def dot(a, b, ca, cb):
    return lax.dot_general(a, b, (((ca,), (cb,)), ((), ())), preferred_element_type=F32)


def exact(a, b):
    return lax.dot_general(
        a, b, (((1,), (0,)), ((), ())), precision=lax.Precision.HIGHEST, preferred_element_type=F32
    )


def sds(shape, dtype):
    return jax.ShapeDtypeStruct(shape, dtype)


def call(kernel, grid, in_specs, out_specs, out_shape, scratch=(), flops=0, nbytes=0, vmem=60, after=(), free=(), aliases=None):
    count, extra = len(in_specs), len(after)

    def run(meta, *refs):
        kernel(meta, *refs[:count], *refs[count + extra :])

    def large(x):
        return x.size * x.dtype.itemsize >= MIB

    def put(x):
        return pltpu.HBM(x.shape, x.dtype) if large(x) else x

    in_specs = list(in_specs) + [pl.BlockSpec(memory_space=pl.ANY)] * extra
    made = pl.pallas_call(
        run,
        grid_spec=pltpu.PrefetchScalarGridSpec(
            num_scalar_prefetch=1,
            grid=grid,
            in_specs=in_specs,
            out_specs=out_specs,
            scratch_shapes=list(scratch),
        ),
        out_shape=[put(x) for x in out_shape] if isinstance(out_shape, list) else put(out_shape),
        input_output_aliases=aliases or {},
        compiler_params=pltpu.CompilerParams(vmem_limit_bytes=vmem * MIB),
        cost_estimate=pl.CostEstimate(flops=int(flops), bytes_accessed=int(nbytes), transcendentals=0),
    )

    def place(i, x):
        return pltpu.with_memory_space_constraint(x, pltpu.HBM) if large(x) and i not in free else x

    return lambda *args: made(*(place(i, x) for i, x in enumerate((*args, *after))))


def whole(shape):
    return pl.BlockSpec(shape, lambda *_: (0,) * len(shape))


def bucket_of(rel, buckets):
    n = jnp.abs(rel)
    far = jnp.full(rel.shape, 8, jnp.int32)
    for edge in EDGES:
        far = far + (n >= edge).astype(jnp.int32)
    return jnp.where(n < 8, n, far) + jnp.where(rel > 0, buckets // 2, 0)


def strip_kernel(meta, table, hot, strip, *, base, buckets):
    near0, near1 = base - 96, base + 224
    heads = strip.shape[0]
    lines = lax.dot_general(
        table[0], hot[...], (((1,), (1,)), ((), ())), precision=lax.Precision.HIGHEST, preferred_element_type=F32
    )
    shape = (near1 - near0, 128)
    rel = near0 - base + lax.broadcasted_iota(jnp.int32, shape, 0) - lax.broadcasted_iota(jnp.int32, shape, 1)
    for h in range(heads):
        wide = jnp.broadcast_to(lines[h : h + 1], (near1 - near0, 256))
        near = pltpu.roll(wide, 0, 1, stride=1, stride_axis=0)[:, :128]
        minus = table[0, h : h + 1, buckets // 2 - 1 : buckets // 2]
        plus = table[0, h : h + 1, buckets - 1 : buckets]
        strip[h, near0:near1, :] = jnp.where(rel >= EDGES[-1], plus, jnp.where(rel <= -EDGES[-1], minus, near))
        strip[h, :near0, :] = jnp.broadcast_to(minus, (near0, 128))
        strip[h, near1:, :] = jnp.broadcast_to(plus, (strip.shape[1] - near1, 128))


def moved(copies, sems):
    started = [pltpu.make_async_copy(src, dst, sems.at[i]) for i, (src, dst) in enumerate(copies)]
    for one in started:
        one.start()
    for one in started:
        one.wait()


def moved_on(copies, held, arrive, leave):
    first = [pltpu.make_async_copy(src, held.at[at], arrive.at[i]) for i, (src, at, _) in enumerate(copies)]
    then = [pltpu.make_async_copy(held.at[at], dst, leave.at[i]) for i, (_, at, dst) in enumerate(copies)]
    for one in first:
        one.start()
    for one, two in zip(first, then):
        one.wait()
        two.start()
    for two in then:
        two.wait()


def flat_rows(dims):
    na, la, nb, lb = dims
    first = [(0, s, pl.ds(s * la // 2, la // 2)) for s in range(na)]
    return first + [(1, s, pl.ds(na * la // 2 + s * lb // 2, lb // 2)) for s in range(nb)]


def pick_kernel(meta, ta, tb, ca, cb, out_x, out_g, held, arrive, leave, *, dims):
    first = [(1 - meta[1]) * n for n in (dims[0], dims[2])]
    moved_on(
        [
            (pair[kind].at[first[kind] + s], (i, rows), out.at[rows])
            for i, (pair, out) in enumerate((((ta, tb), out_x), ((ca, cb), out_g)))
            for kind, s, rows in flat_rows(dims)
        ],
        held,
        arrive,
        leave,
    )


def place_kernel(meta, out_got, grad_got, a0, b0, a1, b1, out_a, out_b, grad_a, grad_b, sems, *, dims):
    first = [(1 - meta[1]) * n for n in (dims[0], dims[2])]
    moved(
        [
            (got.at[rows], pair[kind].at[first[kind] + s])
            for got, pair in ((out_got, (out_a, out_b)), (grad_got, (grad_a, grad_b)))
            for kind, s, rows in flat_rows(dims)
        ],
        sems,
    )


def gathered(i, a, b, rest, out):
    @pl.when(i == 0)
    def _():
        out[...] = flat(a)

    @pl.when(i == 1)
    def _():
        out[...] = flat(b)

    @pl.when(i > 1)
    def _():
        out[...] = rest[...]


def qkv_kernel(meta, xa, xb, xr, gain, wq, wk, wv, x_ref, normed, q, k, v):
    gathered(pl.program_id(0), xa, xb, xr, x_ref.at[0])
    x = x_ref[0].astype(F32)
    r = lax.rsqrt(jnp.mean(x * x, axis=-1, keepdims=True) + EPS)
    n = (x * r * gain[...]).astype(BF)
    normed[0] = n
    q[0] = dot(n, wq[...], 1, 0).astype(BF)
    k[0] = dot(n, wk[...], 1, 0).astype(BF)
    v[0] = dot(n, wv[...], 1, 0).astype(BF)


def units_of(na, la, nb, lb):
    out = [(0, s, la, s * la // 2) for s in range(na)]
    return out + [(1, s, lb, na * la // 2 + s * lb // 2) for s in range(nb)]


def joined(ref, off, half):
    return jnp.concatenate([ref[0, off : off + half, :], ref[1, off : off + half, :]], axis=0)


def strip_rows(flip, base, size, cb, kh):
    half = size // 2
    plain = base - 128 * cb + half * kh
    if flip is None:
        return plain
    moved = (128 * cb + half) % size
    return pl.multiple_of(jnp.where(flip == 0, plain, base - moved + half * (1 - kh)), 128)


def lanes_of(shape, high):
    lane = lax.broadcasted_iota(jnp.int32, shape, len(shape) - 1)
    return (lane >= HEAD) == high


def half_mask(high):
    return jnp.where(lanes_of((1, PAIR), high), 1.0, 0.0).astype(BF)


def attn_kernel(meta, q, k, v, strip, pa, pb, attn, linv, kaug, *, dims, base, seqs_a):
    na, la, nb, lb = dims
    flip = meta[0]

    @pl.when(pl.program_id(0) == 0)
    def _():
        for kind, s, size, off in units_of(*dims):
            half = size // 2
            for kh in range(2):
                row = lax.broadcasted_iota(jnp.int32, (half, 128), 0)
                start = jnp.where(flip == 0, half * kh, half * (1 - kh))
                length = meta[4 + (meta[3] * na if kind == 0 else seqs_a + meta[3] * nb) + s]
                lane = lax.broadcasted_iota(jnp.int32, (half, 128), 1)
                gone = jnp.logical_and(row + start >= length, lane == 0)
                kaug[kh, off : off + half, :] = jnp.where(gone, MASKED, 0.0).astype(BF)

    low_lanes = lax.broadcasted_iota(jnp.int32, (1, PAIR), 1) < HEAD
    for kind, s, size, off in units_of(*dims):
        half = size // 2
        pref = pa if kind == 0 else pb
        q2, k2, v2 = joined(q, off, half), joined(k, off, half), joined(v, off, half)
        first = jnp.where(lax.broadcasted_iota(jnp.int32, (size, 128), 1) == 0, 1.0, 0.0).astype(BF)
        ones = jnp.ones((size, 128), BF)
        qa = jnp.concatenate([q2, first], axis=1)
        ka = joined(kaug, off, half)
        mixed, inverse = [], []
        for h in range(2):
            kk = jnp.concatenate([k2 * half_mask(h == 1), ka], axis=1)
            for c2 in range(size // 256):
                scores = dot(kk, qa[256 * c2 : 256 * c2 + 256], 1, 1)
                for sub in range(2):
                    cb = 2 * c2 + sub
                    bias = jnp.concatenate(
                        [strip[h, pl.ds(strip_rows(flip, base, size, cb, kh), half), :] for kh in range(2)], axis=0
                    )
                    one = scores[:, 128 * sub : 128 * sub + 128] + bias
                    e = jnp.exp(one - jnp.max(one, axis=0, keepdims=True))
                    pref[h, s, :, 128 * cb : 128 * cb + 128] = e.astype(BF)
            va = jnp.concatenate([v2 * half_mask(h == 1), ones], axis=1)
            both = dot(pref[h, s], va, 0, 0)
            inv = 1.0 / both[:, PAIR:]
            mixed.append(both[:, :PAIR] * inv)
            inverse.append(inv)
        o = (mixed[0] + mixed[1]).astype(BF)
        inv = jnp.where(low_lanes, inverse[0], inverse[1]).astype(BF)
        attn[0, off : off + half, :] = o[:half]
        attn[1, off : off + half, :] = o[half:]
        linv[0, off : off + half, :] = inv[:half]
        linv[1, off : off + half, :] = inv[half:]


def ffn_kernel(
    meta, attn, x, w_out, gain, ga, gb, gr, w_in, w_back,
    hidden, g_out, low, back_send, back_keep, in_send, in_keep, d_normed, normed, d_inner, acc, g, *, mixes, chunk,
):
    i = pl.program_id(0)
    th, tile = g.shape[1], x.shape[1]
    per = th // tile

    @pl.when(i < mixes)
    def _():
        h = x[0].astype(F32) + dot(attn[0], w_out[...], 1, 0)
        r = lax.rsqrt(jnp.mean(h * h, axis=-1, keepdims=True) + EPS)
        hidden[0] = h.astype(BF)
        at = pl.ds(pl.multiple_of((i % per) * tile, tile), tile)
        normed[i // per, at, :] = (h * r * gain[...]).astype(BF)
        gathered(i, ga, gb, gr, g_out.at[0])
        g[i // per, at, :] = g_out[0]

    @pl.when(i == mixes)
    def _():
        acc[...] = jnp.zeros_like(acc)

    @pl.when(i >= mixes)
    def _():
        for part in range(2):
            for lo in range(0, th, chunk):
                rows = slice(lo, lo + chunk)
                v = dot(normed[part, rows, :], w_in[...], 1, 0)
                gw = dot(g[part, rows, :], w_back[...], 1, 1)
                u = v * v
                up = 0.5 + 0.5 * jnp.tanh(v * (C1 + (C1 * C3) * u))
                low[part, rows, :] = (v * up).astype(BF)
                slope = up + up * ((1.0 - up) * (v * (2.0 * C1 + (6.0 * C1 * C3) * u)))
                inner = (gw * slope).astype(BF)
                d_inner[part, rows, :] = inner
                acc[part, rows, :] += dot(inner, w_in[...], 1, 1)
        split_columns(meta, dot(flat(low), flat(g), 0, 0), back_send, back_keep)
        value = dot(flat(normed), flat(d_inner), 0, 0).astype(BF)
        sending = i < mixes + (pl.num_programs(0) - mixes) // 2

        @pl.when(sending)
        def _():
            in_send[...] = value

        @pl.when(jnp.logical_not(sending))
        def _():
            in_keep[...] = value

    @pl.when(i == pl.num_programs(0) - 1)
    def _():
        d_normed[...] = acc[...].astype(BF)


def flat(ref):
    a = ref[...]
    return a.reshape(a.shape[0] * a.shape[1], a.shape[2])


def split_columns(meta, value, send, keep):
    half = value.shape[1] // 2
    lo, hi = value[:, :half].astype(BF), value[:, half:].astype(BF)
    first = meta[1] == 0

    @pl.when(first)
    def _():
        keep[...] = lo
        send[...] = hi

    @pl.when(jnp.logical_not(first))
    def _():
        keep[...] = hi
        send[...] = lo


def rows8(value):
    return jnp.sum(value.reshape(value.shape[0] // 8, 8, value.shape[1]), axis=0)


def hidden_kernel(meta, d_normed, hidden, g, gain, w_out, attn, linv, d_hidden, d_attn, small, send, keep, acc, gains):
    i, last = pl.program_id(0), pl.num_programs(0) - 1
    dn = d_normed[0].astype(F32)
    h = hidden[0].astype(F32)
    r = lax.rsqrt(jnp.mean(h * h, axis=-1, keepdims=True) + EPS)
    gained = dn * gain[...]
    mean = jnp.mean(gained * h, axis=-1, keepdims=True)
    dh = (g[0].astype(F32) + r * gained - h * (r * r * r * mean)).astype(BF)
    d_hidden[0] = dh
    d_attn[0] = (dot(dh, w_out[...], 1, 1) * linv[0].astype(F32)).astype(BF)
    part = rows8(dn * h * r)
    product = dot(attn[0], dh, 0, 0)

    @pl.when(i == 0)
    def _():
        gains[...] = part
        acc[...] = product

    @pl.when(i > 0)
    def _():
        gains[...] += part
        acc[...] += product

    @pl.when(i == last)
    def _():
        split_columns(meta, acc[...], send, keep)
        line = jnp.sum(gains[...], axis=0, keepdims=True)
        half = small.shape[1]
        small[...] = jnp.zeros_like(small)
        small[2:3, :] = line[:, :half]
        small[3:4, :] = line[:, half:]


def table_sums(strip, hot, base, buckets):
    near0, near1 = base - 96, base + 224
    lines, ends = [], []
    for h in range(strip.shape[0]):
        near = strip[h, near0:near1, :]
        rel = (
            near0 - base + lax.broadcasted_iota(jnp.int32, near.shape, 0) - lax.broadcasted_iota(jnp.int32, near.shape, 1)
        )
        plus = rows8(strip[h, near1:, :]) + rows8(jnp.where(rel >= 128, near, 0.0))
        minus = rows8(strip[h, :near0, :]) + rows8(jnp.where(rel <= -128, near, 0.0))
        wide = jnp.where(jnp.abs(rel) < 128, near, 0.0)
        wide = jnp.concatenate([wide, jnp.zeros_like(wide)], axis=1)
        line = jnp.zeros((8, 256), F32)
        for r in range(0, near1 - near0, 8):
            line = line + pltpu.roll(wide[r : r + 8], -r % 256, 1)
        one = jnp.zeros((8, 256), F32)
        row = lax.broadcasted_iota(jnp.int32, (8, 256), 0)
        for r in range(8):
            one = one + pltpu.roll(jnp.where(row == r, line, 0.0), -r % 256, 1)
        lines.append(jnp.sum(one, axis=0, keepdims=True))
        ends.append((jnp.sum(plus, keepdims=True), jnp.sum(minus, keepdims=True)))
    fill = [jnp.zeros((8 - len(lines), 256), F32)]
    sums = exact(jnp.concatenate(lines + fill, axis=0), hot[...])
    lane = lax.broadcasted_iota(jnp.int32, (8, 128), 1)
    row = lax.broadcasted_iota(jnp.int32, (8, 128), 0)
    for h, (plus, minus) in enumerate(ends):
        here = row == h
        sums = sums + jnp.where(jnp.logical_and(here, lane == buckets - 1), plus, 0.0)
        sums = sums + jnp.where(jnp.logical_and(here, lane == buckets // 2 - 1), minus, 0.0)
    return sums


def attn_back_kernel(
    meta, q, k, v, do, at_ref, pa, pb, normed, wqs, wks, wvs, wqk, wkk, wvk, hot, gain_attn, small_in, *rest, dims, base, buckets, pair_at, place
):
    before = [] if place[0] else [rest[0]]
    dq, dk, dv, send, keep, small, gain, strip, dsa, dsb, cat = rest[len(before) :]
    flip = meta[0]
    step = pl.program_id(0)
    th = normed.shape[1]
    strip[...] = jnp.zeros_like(strip)
    lane = lax.broadcasted_iota(jnp.int32, (1, PAIR), 1)
    minus = jnp.where(lane < 2, -1.0, 0.0).astype(BF)
    for kind, s, size, off in units_of(*dims):
        half = size // 2
        pref = pa if kind == 0 else pb
        ds_ref = dsa if kind == 0 else dsb
        q2, k2, v2, o2, a2 = (joined(ref, off, half) for ref in (q, k, v, do, at_ref))
        prod = o2.astype(F32) * a2.astype(F32)
        dvs, dks, dqs = [], [], []
        for h in range(2):
            mask = half_mask(h == 1)
            delta = jnp.sum(jnp.where((lane >= HEAD) == (h == 1), prod, 0.0), axis=1, keepdims=True)
            high = delta.astype(BF).astype(F32)
            cols = jnp.where(lane == 0, high, jnp.where(lane == 1, delta - high, 0.0)).astype(BF)
            va = jnp.concatenate([v2 * mask, jnp.broadcast_to(minus, (size, PAIR))], axis=1)
            oa = jnp.concatenate([o2, cols], axis=1)
            for c2 in range(size // 256):
                dp = dot(va, oa[256 * c2 : 256 * c2 + 256], 1, 1)
                for sub in range(2):
                    cb = 2 * c2 + sub
                    cs = slice(128 * cb, 128 * cb + 128)
                    ds = pref[h, s, :, cs].astype(F32) * dp[:, 128 * sub : 128 * sub + 128]
                    for kh in range(2):
                        at = pl.ds(strip_rows(flip, base, size, cb, kh), half)
                        strip[h, at, :] += ds[half * kh : half * kh + half]
                    ds_ref[h, :, cs] = ds.astype(BF)
            dvs.append(dot(pref[h, s], o2 * mask, 1, 0))
            dks.append(dot(ds_ref[h], q2 * mask, 1, 0))
            dqs.append(dot(ds_ref[h], k2 * mask, 0, 0))
        d_v = (dvs[0] + dvs[1]).astype(BF)
        d_k = (dks[0] + dks[1]).astype(BF)
        d_q = (dqs[0] + dqs[1]).astype(BF)
        for part in range(2):
            rows = slice(off, off + half)
            got = slice(part * half, part * half + half)
            dq[part, rows, :] = d_q[got]
            dk[part, rows, :] = d_k[got]
            dv[part, rows, :] = d_v[got]
            at = slice(part * th + off, part * th + off + half)
            cat[step, at, 0:128] = d_q[got]
            cat[step, at, 128:256] = d_k[got]
            cat[step, at, 256:384] = d_v[got]
    @pl.when(step == 0)
    def _():
        small[...] = small_in[...]

    sums = table_sums(strip, hot, base, buckets)
    row = lax.broadcasted_iota(jnp.int32, (small.shape[0], 128), 0) - (4 + 2 * pair_at(step, meta))
    small[:, 0:128] += jnp.where(row == 0, sums[0:1], jnp.where(row == 1, sums[1:2], 0.0))

    @pl.when(step == 1)
    def _():
        both = jnp.concatenate([cat[0], cat[1]], axis=1)
        value = dot(flat(normed), both, 0, 0)
        send[...] = value[:, :384].astype(BF)
        keep[...] = value[:, 384:].astype(BF)
        part = sum(
            value[:, 128 * i : 128 * i + 128] * w[...].astype(F32) for i, w in enumerate((wqs, wks, wvs, wqk, wkk, wvk))
        )
        for ref in before:
            part = part + ref[...]
        gain[...] = part
        if place[1]:
            high = part.astype(BF)
            low = (part - high.astype(F32)).astype(BF)
            ones = jnp.ones((16, 128), BF)
            line = (dot(ones, high, 1, 1) + dot(ones, low, 1, 1))[:1] / gain_attn[...]
            half = small.shape[1]
            small[0:1, :] += line[:, :half]
            small[1:2, :] += line[:, half:]


def spread(i, value, first, second):
    @pl.when(i == 0)
    def _():
        first[...] = value.reshape(first.shape)

    @pl.when(i == 1)
    def _():
        second[...] = value.reshape(second.shape)


def out_kernel(meta, low, w_back, hidden, give, out_a, out_b):
    i = pl.program_id(0)
    value = (hidden[0].astype(F32) + dot(low[0], w_back[...], 1, 0)).astype(BF)

    @pl.when(i < 2)
    def _():
        give[...] = value

    spread(i - 2, value, out_a, out_b)


def tokens_kernel(meta, *refs):
    wq, wk, wv, x_ref, d_hidden, gain = refs[9:15]
    outs = refs[15:]

    def columns(of):
        return jnp.concatenate([r[0, :, :PAIR] for r in of] + [r[0, :, PAIR:] for r in of], axis=1)

    dq, dk, dv = columns(refs[0:3]), columns(refs[3:6]), columns(refs[6:9])
    dn = dot(dq, wq[...], 1, 1) + dot(dk, wk[...], 1, 1) + dot(dv, wv[...], 1, 1)
    x = x_ref[0].astype(F32)
    r = lax.rsqrt(jnp.mean(x * x, axis=-1, keepdims=True) + EPS)
    gained = dn * gain[...]
    mean = jnp.mean(gained * x, axis=-1, keepdims=True)
    value = (d_hidden[0].astype(F32) + r * gained - x * (r * r * r * mean)).astype(BF)
    if len(outs) == 1:
        outs[0][...] = value
    else:
        spread(pl.program_id(0), value, *outs)


def swap(x, axis, bit):
    n = lax.axis_size(axis)
    return lax.ppermute(x, axis, [(i, i ^ bit) for i in range(n)])


TAIL = 32


class Piece:
    def __init__(self, parts, bits_left, carrier=False):
        self.parts, self.left, self.carrier, self.flat = parts, bits_left, carrier, 0

    def rows(self, cols):
        return self.flat or sum(t[0].shape[-2] * t[0].shape[-1] // cols for t in self.parts)

    def count(self, bits):
        return 1 << (len(self.left) - len(bits))


def blocks(x, bits):
    return x.reshape((2,) * bits + (x.shape[0] >> bits, x.shape[1]))


def masks_of(bits):
    return [tuple((m >> i) & 1 for i in range(len(bits))) for m in range(1 << len(bits))]


def shuttle(meta, cols, work, finals, after, small=((), ()), through=()):
    pieces, results = finals
    ins = []

    def slot(x):
        for i, y in enumerate(ins):
            if y is x:
                return i
        ins.append(x)
        return len(ins) - 1

    every = [piece for piece, _ in work] + pieces
    slots = []
    received = set()
    for piece in every:
        for terms in piece.parts:
            received |= {1 + slot(t[0] if piece.flat else t) for t in terms[1:]}
        slots.append([[(slot(t[0]), t[1]) if piece.flat else (slot(t), 0) for t in terms] for terms in piece.parts])
    small_at, tail_at = [slot(x) for x in small[0]], [slot(x) for x in small[1]]
    messages = {}
    for number, (piece, bits) in enumerate(work):
        for mask in masks_of(bits):
            wide = sum(flip << b for flip, b in zip(mask, bits))
            entry = messages.setdefault(wide, [0, False, []])
            entry[2].append((number, mask, entry[0]))
            entry[0] += piece.count(bits) * piece.rows(cols)
            entry[1] |= piece.carrier and wide > 0
    outs = [sds((rows + (TAIL if tail else 0), cols), BF) for rows, tail, _ in messages.values()]
    outs += [sds((spans[0][2], sum(s[4] for s in spans)), F32) for spans in results]
    if small_at:
        outs.append(sds(small[0][0].shape, F32))

    def kernel(meta, *refs):
        got, put = refs[: len(ins)], list(refs[len(ins) + len(through) : len(ins) + len(through) + len(outs)])
        row = meta[2]
        if small_at:
            total = sum(got[i][...] for i in small_at)
            for i in tail_at:
                end = got[i].shape[0]
                tail = got[i][end - TAIL : end, :].astype(F32)
                total = total + tail[: TAIL // 2] + tail[TAIL // 2 :]
            put[-1][...] = total
            high = total.astype(BF).astype(F32)
            tail = jnp.concatenate([high, total - high], axis=0).astype(BF)

        def take(piece, terms, index):
            if not piece.flat:
                return sum(got[i][index].astype(F32) for i, _ in terms)
            at = 0
            for bit in index:
                at = 2 * at + bit
            value = 0.0
            for i, low in terms:
                start = low + at * piece.flat
                value = value + got[i][pl.ds(pl.multiple_of(start, 16) if index else start, piece.flat), :].astype(F32)
            return value

        for (rows, tailed, entries), out in zip(messages.values(), put):
            for number, mask, low in entries:
                piece, bits = work[number]
                rest = [b for b in piece.left if b not in bits]
                for m in range(1 << len(rest)):
                    chosen = {b: (m >> i) & 1 for i, b in enumerate(rest)}
                    for b, flip in zip(bits, mask):
                        chosen[b] = ((row >> b) & 1) ^ flip
                    index = tuple(chosen[b] for b in reversed(piece.left))
                    for terms in slots[number]:
                        value = take(piece, terms, index).astype(BF)
                        high = value.shape[0]
                        for c in range(0, value.shape[1], cols):
                            out[low : low + high, :] = value[:, c : c + cols]
                            low += high
            if tailed:
                out[rows : rows + TAIL, :] = tail
        sums = [take(piece, slots[len(work) + i][0], ()) for i, piece in enumerate(pieces)]
        for spans, out in zip(results, put[len(messages) :]):
            low = 0
            for piece, r0, r, c0, c in spans:
                out[:, low : low + c] = sums[piece][r0 : r0 + r, c0 : c0 + c]
                low += c

    made = call(
        kernel,
        (1,),
        [whole(x.shape) for x in ins] + [pl.BlockSpec(memory_space=pl.ANY)] * len(through),
        [whole(x.shape) for x in outs] + [pl.BlockSpec(memory_space=pl.ANY)] * len(through),
        outs + [sds(x.shape, x.dtype) for x in through],
        nbytes=sum(x.size * 2 for x in ins),
        vmem=30,
        free=tuple(range(1, 1 + len(ins))),
        after=after,
        aliases={1 + len(ins) + i: len(outs) + i for i in range(len(through))},
    )(meta, *ins, *through)
    made, passed = list(made[: len(outs)]), made[len(outs) :]
    got = {wide: swap(x, "rows", wide) if wide else x for wide, x in zip(messages, made)}
    tails = []
    for number, (piece, bits) in enumerate(work):
        rows = piece.rows(cols)
        terms = []
        for wide, (_, tailed, entries) in messages.items():
            for other, _, low in entries:
                if other == number:
                    terms.append((got[wide], low))
                    if piece.carrier and tailed:
                        tails.append(got[wide])
        piece.parts, piece.flat = [terms], rows
        piece.left = tuple(b for b in piece.left if b not in bits)
    ends = len(messages) + len(results)
    return made[len(messages) : ends], (made[ends:], tails), [*made[: len(messages)], *passed]


def body(
    tokens_a, lengths_a, cotangent_a, tokens_b, lengths_b, cotangent_b,
    gain_attn, w_query, w_key, w_value, w_out, relative_bias_table, gain_ffn, w_in, w_back,
):
    nseq, nrows = lax.axis_size("seq"), lax.axis_size("rows")
    c = lax.axis_index("seq")
    width = tokens_a.shape[2]
    ff = w_in.shape[1]
    buckets, head_count = relative_bias_table.shape
    la, lb = tokens_a.shape[1] * nseq, tokens_b.shape[1] * nseq
    na, nb = tokens_a.shape[0] // nseq, tokens_b.shape[0] // nseq
    dims = (na, la, nb, lb)
    th = (na * la + nb * lb) // 2
    tokens = 2 * th
    base = la - 128
    strip_len = 2 * la - 128
    pairs = head_count // 2
    paired = nseq == 2 and nrows == 16

    me = c if paired else jnp.int32(0)
    flip = me
    meta = jnp.concatenate(
        [jnp.stack([flip, me, lax.axis_index("rows"), c]).astype(jnp.int32), lengths_a, lengths_b]
    )
    gain1, gain2 = gain_attn[None], gain_ffn[None]

    tile = th // 2
    per = 2
    row_grid = (2 * per,)
    by_row = lambda w: pl.BlockSpec((1, tile, w), lambda i, m: (i // per, i % per, 0))
    dense = 2 * tokens * width
    shape_a, shape_b = (na, la // 2, width), (nb, lb // 2, width)
    of_core = lambda shape: pl.BlockSpec(shape, lambda i, m: (m[1], 0, 0))
    of_other = lambda shape: pl.BlockSpec(shape, lambda i, m: (1 - m[1], 0, 0))
    cores = 2 if paired else 1
    all_a, all_b = (cores * na,) + shape_a[1:], (cores * nb,) + shape_b[1:]
    cut = na * la // 2

    def regroup(a, b):
        def one(x):
            got = lax.all_to_all(x, "seq", 0, 1, tiled=True)
            n, size, _ = got.shape
            return got.reshape(n, 2, size // 2, width).transpose(1, 0, 2, 3)

        whole_a, whole_b = one(a), one(b)
        rest = jnp.concatenate([whole_a[1].reshape(-1, width), whole_b[1].reshape(-1, width)], axis=0)
        return whole_a[0], whole_b[0], rest

    def ungroup(own_a, own_b, rest):
        def one(own, other, n, size):
            y = jnp.stack([own, other.reshape(own.shape)], axis=1).reshape(n, size, width)
            return lax.all_to_all(y, "seq", 1, 0, tiled=True)

        return one(own_a, rest[:cut], na, la), one(own_b, rest[cut:], nb, lb)

    received = pl.BlockSpec((tile, width), lambda i, m: (jnp.clip(i - per, 0, per - 1), 0))
    anywhere = pl.BlockSpec(memory_space=pl.ANY)
    copies = [pltpu.SemaphoreType.DMA((2 * (na + nb),))]
    in_vmem = pl.BlockSpec(memory_space=pltpu.VMEM)
    if paired:
        give = call(
            functools.partial(pick_kernel, dims=dims),
            (1,),
            [anywhere] * 4,
            [anywhere] * 2,
            [sds((th, width), BF)] * 2,
            scratch=[pltpu.VMEM((2, th, width), BF)] + copies * 2,
            nbytes=8 * th * width,
            vmem=8,
        )(meta, tokens_a, tokens_b, cotangent_a, cotangent_b)
        x_in = (tokens_a, tokens_b, swap(give[0], "seq", 1))
        g_in3 = (cotangent_a, cotangent_b, swap(give[1], "seq", 1))
    else:
        x_in = regroup(tokens_a, tokens_b)
        g_in3 = regroup(cotangent_a, cotangent_b)
    lane = jnp.arange(256, dtype=jnp.int32)
    back_rel = ((-96 - lane + 128 + 512) & 255) - 128
    hot = jnp.logical_and(
        bucket_of(back_rel, buckets)[:, None] == jnp.arange(128, dtype=jnp.int32)[None], back_rel[:, None] > -128
    ).astype(F32)

    at_once = 4
    rows_of_table = jnp.pad(
        relative_bias_table.T.reshape(head_count // at_once, at_once, buckets), ((0, 0), (0, 4), (0, 128 - buckets))
    )
    strip = call(
        functools.partial(strip_kernel, base=base, buckets=buckets),
        (head_count // at_once,),
        [pl.BlockSpec((1, 8, 128), lambda h, m: (h, 0, 0)), whole((256, 128))],
        pl.BlockSpec((at_once, strip_len, 128), lambda h, m: (h, 0, 0)),
        sds((head_count, strip_len, 128), F32),
        vmem=16,
        nbytes=4 * head_count * strip_len * 128,
    )(meta, rows_of_table, hot)

    tok = sds((2, th, width), BF)
    x, normed, q, k, v = call(
        qkv_kernel,
        row_grid,
        [of_core(shape_a), of_core(shape_b), received, whole((1, width))] + [whole((width, width))] * 3,
        [by_row(width)] * 5,
        [tok] * 5,
        vmem=30,
        free=(3, 5, 6, 7),
        flops=3 * dense * width,
        nbytes=10 * tokens * width,
        after=[strip],
    )(meta, *x_in, gain1, w_query, w_key, w_value)

    by_pair = pl.BlockSpec((2, th, PAIR), lambda p, m: (0, 0, p))
    pa_shape, pb_shape = (head_count, na, la, la), (head_count, nb, lb, lb)
    score_macs = head_count * (na * la * la + nb * lb * lb)
    pa, pb, attn, linv = call(
        functools.partial(attn_kernel, dims=dims, base=base, seqs_a=tokens_a.shape[0]),
        (pairs,),
        [by_pair] * 3 + [pl.BlockSpec((2, strip_len, 128), lambda p, m: (p, 0, 0))],
        [
            pl.BlockSpec((2, na, la, la), lambda p, m: (p, 0, 0, 0)),
            pl.BlockSpec((2, nb, lb, lb), lambda p, m: (p, 0, 0, 0)),
            by_pair,
            by_pair,
        ],
        [sds(pa_shape, BF), sds(pb_shape, BF), tok, tok],
        scratch=[pltpu.VMEM((2, th, 128), BF)],
        vmem=34,
        flops=score_macs * 256 * 4,
        nbytes=2 * score_macs,
    )(meta, q, k, v, strip)

    all_tok = whole((2, th, width))
    fb = 512
    half_w, half_f, nf, mixes = width // 2, ff // 2, ff // fb, 2 * per

    def unit_at(i, m):
        return (jnp.maximum(i - mixes, 0) + (1 - m[1]) * (nf // 2)) % nf

    def mix_at(i):
        return jnp.minimum(i, mixes - 1)

    mix_rows = pl.BlockSpec((1, tile, width), lambda i, m: (mix_at(i) // per, mix_at(i) % per, 0))
    unit_rows = pl.BlockSpec((fb, half_w), lambda i, m: (unit_at(i, m), 0))
    hidden, g, low, back_send, back_keep, in_send, in_keep, d_normed2 = call(
        functools.partial(ffn_kernel, mixes=mixes, chunk=th),
        (mixes + nf,),
        [
            mix_rows,
            mix_rows,
            whole((width, width)),
            whole((1, width)),
            of_core(shape_a),
            of_core(shape_b),
            received,
            pl.BlockSpec((width, fb), lambda i, m: (0, unit_at(i, m))),
            pl.BlockSpec((fb, width), lambda i, m: (unit_at(i, m), 0)),
        ],
        [
            mix_rows,
            mix_rows,
            pl.BlockSpec((2, th, fb), lambda i, m: (0, 0, unit_at(i, m))),
            unit_rows,
            unit_rows,
            pl.BlockSpec((width, fb), lambda i, m: (0, jnp.clip(i - mixes, 0, nf // 2 - 1))),
            pl.BlockSpec((width, fb), lambda i, m: (0, jnp.maximum(i - mixes - nf // 2, 0))),
            all_tok,
        ],
        [tok, tok, sds((2, th, ff), BF)]
        + [sds((ff, half_w), BF)] * 2
        + [sds((width, half_f), BF)] * 2
        + [tok],
        scratch=[
            pltpu.VMEM((2, th, width), BF),
            pltpu.VMEM((2, th, fb), BF),
            pltpu.VMEM((2, th, width), F32),
            pltpu.VMEM((2, th, width), BF),
        ],
        flops=dense * (5 * ff + width),
        nbytes=2 * tokens * ff,
        vmem=52,
        free=(3, 7, 8, 9),
    )(meta, attn, x, w_out, gain2, *g_in3, w_in, w_back)

    bit_count = nrows.bit_length() - 1
    low_bits, high_bits = (0, 1), tuple(range(2, bit_count))
    every_bit = tuple(range(bit_count))

    def pair_sum(keep, send):
        return [blocks(keep, bit_count), blocks(swap(send, "seq", 1), bit_count)]

    hold = []
    if paired:
        back = Piece([pair_sum(back_keep, back_send)], every_bit)
        inner = Piece([pair_sum(in_keep, in_send)], every_bit)
        hold = [back_send, in_send]

    small = sds((16, half_w), F32)
    none = ([], [])
    d_hidden, d_attn, small_sum, out_send, out_keep = call(
        hidden_kernel,
        row_grid,
        [
            by_row(width),
            by_row(width),
            by_row(width),
            whole((1, width)),
            whole((width, width)),
            by_row(width),
            by_row(width),
        ],
        [by_row(width), by_row(width), whole((16, half_w)), whole((width, half_w)), whole((width, half_w))],
        [tok, tok, small, sds((width, half_w), BF), sds((width, half_w), BF)],
        scratch=[pltpu.VMEM((width, width), F32), pltpu.VMEM((8, width), F32)],
        free=(5,),
        vmem=34,
        flops=dense * (ff + 2 * width),
        nbytes=2 * tokens * ff,
        after=hold,
    )(meta, d_normed2, hidden, g, gain2, w_out, attn, linv)

    group_count = pairs // 2
    groups, dqs, gains = [], [], []
    for gi in range(group_count):
        if paired:
            if gi == 0:
                out_sum = pair_sum(out_keep, out_send)
                _, _, hold = shuttle(meta, half_w, [(back, (0,)), (inner, (1,))], none, [d_attn])
                hold.append(out_send)
            elif gi == 1:
                first = [out_sum, pair_sum(*groups[0])]
                hold = [groups[0][1]]
            else:
                first = Piece(first, every_bit)
                _, _, hold = shuttle(
                    meta, half_w, [(back, (1,)), (inner, (2,)), (first, (0,))], none, [dqs[1][0]]
                )
                second = pair_sum(*groups[1])
                hold.append(groups[1][1])

        def pair_at(s, m, gi=gi):
            return jnp.where(s == 0, 1 - m[1], m[1]) * group_count + gi

        def half_at(s, m):
            return jnp.where(s == 0, 1 - m[1], m[1])

        by_cols = pl.BlockSpec((2, th, PAIR), lambda s, m, f=pair_at: (0, 0, f(s, m)))
        to_cols = pl.BlockSpec((2, th, PAIR), lambda s, m: (0, 0, half_at(s, m)))
        weight_cols = [
            pl.BlockSpec((width, PAIR), lambda s, m, f=pair_at, at=at: (0, f(at, m))) for at in (0, 0, 0, 1, 1, 1)
        ]
        dq, dk, dv, send, keep, small_sum, gain = call(
            functools.partial(
                attn_back_kernel, dims=dims, base=base, buckets=buckets, pair_at=pair_at,
                place=(gi == 0, gi == group_count - 1),
            ),
            (2,),
            [by_cols] * 5
            + [
                pl.BlockSpec((2, na, la, la), lambda s, m, f=pair_at: (f(s, m), 0, 0, 0)),
                pl.BlockSpec((2, nb, lb, lb), lambda s, m, f=pair_at: (f(s, m), 0, 0, 0)),
                all_tok,
            ]
            + weight_cols
            + [whole((256, 128)), whole((1, width)), whole((16, half_w))]
            + [whole((width, 128))] * len(gains),
            [to_cols] * 3
            + [
                whole((width, 3 * PAIR)),
                whole((width, 3 * PAIR)),
                whole((16, half_w)),
                whole((width, 128)),
            ],
            [sds((2, th, 2 * PAIR), BF)] * 3
            + [
                sds((width, 3 * PAIR), BF),
                sds((width, 3 * PAIR), BF),
                small,
                sds((width, 128), F32),
            ],
            scratch=[
                pltpu.VMEM((2, strip_len, 128), F32),
                pltpu.VMEM((2, la, la), BF),
                pltpu.VMEM((2, lb, lb), BF),
                pltpu.VMEM((2, tokens, 3 * PAIR), BF),
            ],
            free=(8, 9, 10, 11, 12, 13, 14),
            vmem=40,
        flops=score_macs * 256 * 8 // 3 + dense * width,
            nbytes=2 * score_macs // 3,
            after=hold,
        )(meta, q, k, v, d_attn, attn, pa, pb, normed, *([w_query, w_key, w_value] * 2), hot, gain1, small_sum, *gains)
        dqs.append((dq, dk, dv))
        gains = [gain]
        groups.append((keep, send))

    if paired:
        last = Piece([second, pair_sum(*groups[2])], every_bit, carrier=True)
        smalls = [small_sum, swap(small_sum, "seq", 1)]
        _, _, hold = shuttle(meta, half_w, [(back, (2,)), (inner, (0,)), (first, (1,))], none, [dqs[2][0]])
        hold += [groups[2][1], small_sum]

    def token_grads(part):
        of_part = lambda w: pl.BlockSpec((1, tile, w), lambda i, m: (part, i, 0))
        own = [of_core(shape_a), of_core(shape_b)]
        return call(
            tokens_kernel,
            (per,),
            [of_part(2 * PAIR)] * 9
            + [whole((width, width))] * 3
            + [of_part(width), of_part(width), whole((1, width))],
            [pl.BlockSpec((tile, width), lambda i, m: (i, 0))] if part else own,
            [sds((th, width), BF)] if part else [sds(all_a, BF), sds(all_b, BF)],
            vmem=24,
            free=(10, 11, 12),
            flops=3 * dense * width // 2,
            nbytes=7 * tokens * width,
            after=hold,
        )(meta, *(d[i] for i in range(3) for d in dqs), w_query, w_key, w_value, x, d_hidden, gain1)

    (grads1,) = token_grads(1)
    if paired:
        _, small_state, hold = shuttle(
            meta,
            half_w,
            [(back, (3,)), (inner, (3,)), (first, (2,)), (last, low_bits)],
            none,
            [grads1],
            (smalls, ()),
        )
        hold.append(grads1)
    out_rows = lambda w: pl.BlockSpec((1, tile, w), lambda i, m: (1 - i // per, i % per, 0))
    outs1, out_a, out_b = call(
        out_kernel,
        row_grid,
        [out_rows(ff), whole((ff, width)), out_rows(width)],
        [pl.BlockSpec((tile, width), lambda i, m: (jnp.minimum(i, per - 1), 0)), of_core(shape_a), of_core(shape_b)],
        [sds((th, width), BF), sds(all_a, BF), sds(all_b, BF)],
        vmem=30,
        free=(2,),
        flops=dense * ff,
        nbytes=2 * tokens * ff,
        after=hold,
    )(meta, low, w_back, hidden)
    if paired:
        r = width // nrows
        in_back = [(0, 0, ff // nrows, 0, half_w)]
        in_in = [(1, r * j, r, 0, half_w) for j in range(half_f // half_w)]
        (g_back, g_in), small_state, hold = shuttle(
            meta,
            half_w,
            [(first, (3,)), (last, high_bits)],
            ([back, inner], [in_back, in_in]),
            [],
            small_state,
            [grads1, outs1],
        )
        grads1_got, outs1_got = (swap(y, "seq", 1) for y in hold[-2:])
    grad_a, grad_b = token_grads(0)

    if paired:
        def of(col):
            at = [(0, r), (1, 0), (1, r)]
            return [(piece, row, r, PAIR * col, PAIR) for piece, row in at]

        (g_out, g_q, g_k, g_v), ((small_all,), _), _ = shuttle(
            meta,
            half_w,
            [],
            ([first, last], [[(0, 0, r, 0, half_w)], of(0), of(1), of(2)]),
            [grad_a],
            small_state,
        )
        out_a, out_b, grad_a, grad_b = call(
            functools.partial(place_kernel, dims=dims),
            (1,),
            [in_vmem] * 2 + [anywhere] * 4,
            [anywhere] * 4,
            [sds(all_a, BF), sds(all_b, BF)] * 2,
            scratch=copies,
            vmem=8,
            free=(1, 2),
            aliases={3: 0, 4: 1, 5: 2, 6: 3},
        )(meta, outs1_got, grads1_got, out_a, out_b, grad_a, grad_b)
    else:
        out_a, out_b = ungroup(out_a, out_b, outs1)
        grad_a, grad_b = ungroup(grad_a, grad_b, grads1)
        small_all = lax.psum(small_sum, ("rows", "seq"))

        def reduce(x):
            x = lax.psum_scatter(x.astype(F32), "rows", scatter_dimension=0, tiled=True)
            return lax.psum_scatter(x.astype(BF), "seq", scatter_dimension=1, tiled=True).astype(F32)

        def both(keep, send):
            return reduce(jnp.concatenate([keep, send], axis=1))

        g_back, g_in, g_out = both(back_keep, back_send), both(in_keep, in_send), both(out_keep, out_send)
        g_q, g_k, g_v = (
            reduce(
                jnp.concatenate([part[s][:, PAIR * i : PAIR * i + PAIR] for s in range(2) for part in groups], axis=1)
            )
            for i in range(3)
        )
    gain_one, gain_two = small_all[0:2].reshape(width), small_all[2:4].reshape(width)
    table_sum = small_all[4 : 4 + head_count, :buckets].T
    return (
        out_a, out_b, grad_a, grad_b, gain_one, g_q, g_k, g_v, g_out, table_sum, gain_two, g_in, g_back,
    )


def solution(mesh):
    split = P("rows", "seq", None)
    placed = (split, P("rows"), split, split, P("rows"), split) + (P(),) * 9
    shard = P("rows", "seq")
    return jax.shard_map(
        body,
        mesh=mesh,
        in_specs=placed,
        out_specs=(split, split, split, split, P(), shard, shard, shard, shard, P(), P(), shard, shard),
        check_vma=False,
    )
```

```python
import functools

import jax
import jax.numpy as jnp
from jax import lax
from jax.experimental import pallas as pl
from jax.experimental.pallas import tpu as pltpu
from jax.sharding import PartitionSpec as P

EPS = 1e-06
EDGES = (12, 16, 23, 32, 46, 64, 91)
MASKED = -1e30
C1 = 0.7978845608
C3 = 0.044715
BF = jnp.bfloat16
F32 = jnp.float32
HEAD = 64
PAIR = 2 * HEAD
MIB = 1 << 20


def dot(a, b, ca, cb):
    return lax.dot_general(a, b, (((ca,), (cb,)), ((), ())), preferred_element_type=F32)


def exact(a, b):
    return lax.dot_general(
        a, b, (((1,), (0,)), ((), ())), precision=lax.Precision.HIGHEST, preferred_element_type=F32
    )


def sds(shape, dtype):
    return jax.ShapeDtypeStruct(shape, dtype)


def call(kernel, grid, in_specs, out_specs, out_shape, scratch=(), flops=0, nbytes=0, vmem=60, after=(), free=(), aliases=None):
    count, extra = len(in_specs), len(after)

    def run(meta, *refs):
        kernel(meta, *refs[:count], *refs[count + extra :])

    def large(x):
        return x.size * x.dtype.itemsize >= MIB

    def put(x):
        return pltpu.HBM(x.shape, x.dtype) if large(x) else x

    in_specs = list(in_specs) + [pl.BlockSpec(memory_space=pl.ANY)] * extra
    made = pl.pallas_call(
        run,
        grid_spec=pltpu.PrefetchScalarGridSpec(
            num_scalar_prefetch=1,
            grid=grid,
            in_specs=in_specs,
            out_specs=out_specs,
            scratch_shapes=list(scratch),
        ),
        out_shape=[put(x) for x in out_shape] if isinstance(out_shape, list) else put(out_shape),
        input_output_aliases=aliases or {},
        compiler_params=pltpu.CompilerParams(vmem_limit_bytes=vmem * MIB),
        cost_estimate=pl.CostEstimate(flops=int(flops), bytes_accessed=int(nbytes), transcendentals=0),
    )

    def place(i, x):
        return pltpu.with_memory_space_constraint(x, pltpu.HBM) if large(x) and i not in free else x

    return lambda *args: made(*(place(i, x) for i, x in enumerate((*args, *after))))


def whole(shape):
    return pl.BlockSpec(shape, lambda *_: (0,) * len(shape))


def bucket_of(rel, buckets):
    n = jnp.abs(rel)
    far = jnp.full(rel.shape, 8, jnp.int32)
    for edge in EDGES:
        far = far + (n >= edge).astype(jnp.int32)
    return jnp.where(n < 8, n, far) + jnp.where(rel > 0, buckets // 2, 0)


def strip_kernel(meta, table, hot, strip, *, base, buckets):
    near0, near1 = base - 96, base + 224
    heads = strip.shape[0]
    lines = lax.dot_general(
        table[0], hot[...], (((1,), (1,)), ((), ())), precision=lax.Precision.HIGHEST, preferred_element_type=F32
    )
    shape = (near1 - near0, 128)
    rel = near0 - base + lax.broadcasted_iota(jnp.int32, shape, 0) - lax.broadcasted_iota(jnp.int32, shape, 1)
    for h in range(heads):
        wide = jnp.broadcast_to(lines[h : h + 1], (near1 - near0, 256))
        near = pltpu.roll(wide, 0, 1, stride=1, stride_axis=0)[:, :128]
        minus = table[0, h : h + 1, buckets // 2 - 1 : buckets // 2]
        plus = table[0, h : h + 1, buckets - 1 : buckets]
        strip[h, near0:near1, :] = jnp.where(rel >= EDGES[-1], plus, jnp.where(rel <= -EDGES[-1], minus, near))
        strip[h, :near0, :] = jnp.broadcast_to(minus, (near0, 128))
        strip[h, near1:, :] = jnp.broadcast_to(plus, (strip.shape[1] - near1, 128))


def moved(copies, sems):
    started = [pltpu.make_async_copy(src, dst, sems.at[i]) for i, (src, dst) in enumerate(copies)]
    for one in started:
        one.start()
    for one in started:
        one.wait()


def moved_on(copies, held, arrive, leave):
    first = [pltpu.make_async_copy(src, held.at[at], arrive.at[i]) for i, (src, at, _) in enumerate(copies)]
    then = [pltpu.make_async_copy(held.at[at], dst, leave.at[i]) for i, (_, at, dst) in enumerate(copies)]
    for one in first:
        one.start()
    for one, two in zip(first, then):
        one.wait()
        two.start()
    for two in then:
        two.wait()


def flat_rows(dims):
    na, la, nb, lb = dims
    first = [(0, s, pl.ds(s * la // 2, la // 2)) for s in range(na)]
    return first + [(1, s, pl.ds(na * la // 2 + s * lb // 2, lb // 2)) for s in range(nb)]


def pick_kernel(meta, ta, tb, ca, cb, out_x, out_g, held, arrive, leave, *, dims):
    first = [(1 - meta[1]) * n for n in (dims[0], dims[2])]
    moved_on(
        [
            (pair[kind].at[first[kind] + s], (i, rows), out.at[rows])
            for i, (pair, out) in enumerate((((ta, tb), out_x), ((ca, cb), out_g)))
            for kind, s, rows in flat_rows(dims)
        ],
        held,
        arrive,
        leave,
    )


def place_kernel(meta, out_got, grad_got, a0, b0, a1, b1, out_a, out_b, grad_a, grad_b, sems, *, dims):
    first = [(1 - meta[1]) * n for n in (dims[0], dims[2])]
    moved(
        [
            (got.at[rows], pair[kind].at[first[kind] + s])
            for got, pair in ((out_got, (out_a, out_b)), (grad_got, (grad_a, grad_b)))
            for kind, s, rows in flat_rows(dims)
        ],
        sems,
    )


def gathered(i, a, b, rest, out):
    @pl.when(i == 0)
    def _():
        out[...] = flat(a)

    @pl.when(i == 1)
    def _():
        out[...] = flat(b)

    @pl.when(i > 1)
    def _():
        out[...] = rest[...]


def qkv_kernel(meta, xa, xb, xr, gain, wq, wk, wv, x_ref, normed, q, k, v):
    gathered(pl.program_id(0), xa, xb, xr, x_ref.at[0])
    x = x_ref[0].astype(F32)
    r = lax.rsqrt(jnp.mean(x * x, axis=-1, keepdims=True) + EPS)
    n = (x * r * gain[...]).astype(BF)
    normed[0] = n
    q[0] = dot(n, wq[...], 1, 0).astype(BF)
    k[0] = dot(n, wk[...], 1, 0).astype(BF)
    v[0] = dot(n, wv[...], 1, 0).astype(BF)


def units_of(na, la, nb, lb):
    out = [(0, s, la, s * la // 2) for s in range(na)]
    return out + [(1, s, lb, na * la // 2 + s * lb // 2) for s in range(nb)]


def joined(ref, off, half):
    return jnp.concatenate([ref[0, off : off + half, :], ref[1, off : off + half, :]], axis=0)


def strip_rows(flip, base, size, cb, kh):
    half = size // 2
    plain = base - 128 * cb + half * kh
    if flip is None:
        return plain
    moved = (128 * cb + half) % size
    return pl.multiple_of(jnp.where(flip == 0, plain, base - moved + half * (1 - kh)), 128)


def lanes_of(shape, high):
    lane = lax.broadcasted_iota(jnp.int32, shape, len(shape) - 1)
    return (lane >= HEAD) == high


def half_mask(high):
    return jnp.where(lanes_of((1, PAIR), high), 1.0, 0.0).astype(BF)


def attn_kernel(meta, q, k, v, strip, pa, pb, attn, linv, kaug, *, dims, base, seqs_a):
    na, la, nb, lb = dims
    flip = meta[0]

    @pl.when(pl.program_id(0) == 0)
    def _():
        for kind, s, size, off in units_of(*dims):
            half = size // 2
            for kh in range(2):
                row = lax.broadcasted_iota(jnp.int32, (half, 128), 0)
                start = jnp.where(flip == 0, half * kh, half * (1 - kh))
                length = meta[4 + (meta[3] * na if kind == 0 else seqs_a + meta[3] * nb) + s]
                lane = lax.broadcasted_iota(jnp.int32, (half, 128), 1)
                gone = jnp.logical_and(row + start >= length, lane == 0)
                kaug[kh, off : off + half, :] = jnp.where(gone, MASKED, 0.0).astype(BF)

    low_lanes = lax.broadcasted_iota(jnp.int32, (1, PAIR), 1) < HEAD
    for kind, s, size, off in units_of(*dims):
        half = size // 2
        pref = pa if kind == 0 else pb
        q2, k2, v2 = joined(q, off, half), joined(k, off, half), joined(v, off, half)
        first = jnp.where(lax.broadcasted_iota(jnp.int32, (size, 128), 1) == 0, 1.0, 0.0).astype(BF)
        ones = jnp.ones((size, 128), BF)
        qa = jnp.concatenate([q2, first], axis=1)
        ka = joined(kaug, off, half)
        mixed, inverse = [], []
        for h in range(2):
            kk = jnp.concatenate([k2 * half_mask(h == 1), ka], axis=1)
            for c2 in range(size // 256):
                scores = dot(kk, qa[256 * c2 : 256 * c2 + 256], 1, 1)
                for sub in range(2):
                    cb = 2 * c2 + sub
                    bias = jnp.concatenate(
                        [strip[h, pl.ds(strip_rows(flip, base, size, cb, kh), half), :] for kh in range(2)], axis=0
                    )
                    one = scores[:, 128 * sub : 128 * sub + 128] + bias
                    e = jnp.exp(one - jnp.max(one, axis=0, keepdims=True))
                    pref[h, s, :, 128 * cb : 128 * cb + 128] = e.astype(BF)
            va = jnp.concatenate([v2 * half_mask(h == 1), ones], axis=1)
            both = dot(pref[h, s], va, 0, 0)
            inv = 1.0 / both[:, PAIR:]
            mixed.append(both[:, :PAIR] * inv)
            inverse.append(inv)
        o = (mixed[0] + mixed[1]).astype(BF)
        inv = jnp.where(low_lanes, inverse[0], inverse[1]).astype(BF)
        attn[0, off : off + half, :] = o[:half]
        attn[1, off : off + half, :] = o[half:]
        linv[0, off : off + half, :] = inv[:half]
        linv[1, off : off + half, :] = inv[half:]


def ffn_kernel(
    meta, attn, x, w_out, gain, ga, gb, gr, w_in, w_back,
    hidden, g_out, low, back_send, back_keep, in_send, in_keep, d_normed, normed, d_inner, acc, g, *, mixes, chunk,
):
    i = pl.program_id(0)
    th, tile = g.shape[1], x.shape[1]
    per = th // tile

    @pl.when(i < mixes)
    def _():
        h = x[0].astype(F32) + dot(attn[0], w_out[...], 1, 0)
        r = lax.rsqrt(jnp.mean(h * h, axis=-1, keepdims=True) + EPS)
        hidden[0] = h.astype(BF)
        at = pl.ds(pl.multiple_of((i % per) * tile, tile), tile)
        normed[i // per, at, :] = (h * r * gain[...]).astype(BF)
        gathered(i, ga, gb, gr, g_out.at[0])
        g[i // per, at, :] = g_out[0]

    @pl.when(i == mixes)
    def _():
        acc[...] = jnp.zeros_like(acc)

    @pl.when(i >= mixes)
    def _():
        for part in range(2):
            for lo in range(0, th, chunk):
                rows = slice(lo, lo + chunk)
                v = dot(normed[part, rows, :], w_in[...], 1, 0)
                gw = dot(g[part, rows, :], w_back[...], 1, 1)
                u = v * v
                up = 0.5 + 0.5 * jnp.tanh(v * (C1 + (C1 * C3) * u))
                low[part, rows, :] = (v * up).astype(BF)
                slope = up + up * ((1.0 - up) * (v * (2.0 * C1 + (6.0 * C1 * C3) * u)))
                inner = (gw * slope).astype(BF)
                d_inner[part, rows, :] = inner
                acc[part, rows, :] += dot(inner, w_in[...], 1, 1)
        split_columns(meta, dot(flat(low), flat(g), 0, 0), back_send, back_keep)
        value = dot(flat(normed), flat(d_inner), 0, 0).astype(BF)
        sending = i < mixes + (pl.num_programs(0) - mixes) // 2

        @pl.when(sending)
        def _():
            in_send[...] = value

        @pl.when(jnp.logical_not(sending))
        def _():
            in_keep[...] = value

    @pl.when(i == pl.num_programs(0) - 1)
    def _():
        d_normed[...] = acc[...].astype(BF)


def flat(ref):
    a = ref[...]
    return a.reshape(a.shape[0] * a.shape[1], a.shape[2])


def split_columns(meta, value, send, keep):
    half = value.shape[1] // 2
    lo, hi = value[:, :half].astype(BF), value[:, half:].astype(BF)
    first = meta[1] == 0

    @pl.when(first)
    def _():
        keep[...] = lo
        send[...] = hi

    @pl.when(jnp.logical_not(first))
    def _():
        keep[...] = hi
        send[...] = lo


def rows8(value):
    return jnp.sum(value.reshape(value.shape[0] // 8, 8, value.shape[1]), axis=0)


def hidden_kernel(meta, d_normed, hidden, g, gain, w_out, attn, linv, d_hidden, d_attn, small, send, keep, acc, gains):
    i, last = pl.program_id(0), pl.num_programs(0) - 1
    dn = d_normed[0].astype(F32)
    h = hidden[0].astype(F32)
    r = lax.rsqrt(jnp.mean(h * h, axis=-1, keepdims=True) + EPS)
    gained = dn * gain[...]
    mean = jnp.mean(gained * h, axis=-1, keepdims=True)
    dh = (g[0].astype(F32) + r * gained - h * (r * r * r * mean)).astype(BF)
    d_hidden[0] = dh
    d_attn[0] = (dot(dh, w_out[...], 1, 1) * linv[0].astype(F32)).astype(BF)
    part = rows8(dn * h * r)
    product = dot(attn[0], dh, 0, 0)

    @pl.when(i == 0)
    def _():
        gains[...] = part
        acc[...] = product

    @pl.when(i > 0)
    def _():
        gains[...] += part
        acc[...] += product

    @pl.when(i == last)
    def _():
        split_columns(meta, acc[...], send, keep)
        line = jnp.sum(gains[...], axis=0, keepdims=True)
        half = small.shape[1]
        small[...] = jnp.zeros_like(small)
        small[2:3, :] = line[:, :half]
        small[3:4, :] = line[:, half:]


def table_sums(strip, hot, base, buckets):
    near0, near1 = base - 96, base + 224
    lines, ends = [], []
    for h in range(strip.shape[0]):
        near = strip[h, near0:near1, :]
        rel = (
            near0 - base + lax.broadcasted_iota(jnp.int32, near.shape, 0) - lax.broadcasted_iota(jnp.int32, near.shape, 1)
        )
        plus = rows8(strip[h, near1:, :]) + rows8(jnp.where(rel >= 128, near, 0.0))
        minus = rows8(strip[h, :near0, :]) + rows8(jnp.where(rel <= -128, near, 0.0))
        wide = jnp.where(jnp.abs(rel) < 128, near, 0.0)
        wide = jnp.concatenate([wide, jnp.zeros_like(wide)], axis=1)
        line = jnp.zeros((8, 256), F32)
        for r in range(0, near1 - near0, 8):
            line = line + pltpu.roll(wide[r : r + 8], -r % 256, 1)
        one = jnp.zeros((8, 256), F32)
        row = lax.broadcasted_iota(jnp.int32, (8, 256), 0)
        for r in range(8):
            one = one + pltpu.roll(jnp.where(row == r, line, 0.0), -r % 256, 1)
        lines.append(jnp.sum(one, axis=0, keepdims=True))
        ends.append((jnp.sum(plus, keepdims=True), jnp.sum(minus, keepdims=True)))
    fill = [jnp.zeros((8 - len(lines), 256), F32)]
    sums = exact(jnp.concatenate(lines + fill, axis=0), hot[...])
    lane = lax.broadcasted_iota(jnp.int32, (8, 128), 1)
    row = lax.broadcasted_iota(jnp.int32, (8, 128), 0)
    for h, (plus, minus) in enumerate(ends):
        here = row == h
        sums = sums + jnp.where(jnp.logical_and(here, lane == buckets - 1), plus, 0.0)
        sums = sums + jnp.where(jnp.logical_and(here, lane == buckets // 2 - 1), minus, 0.0)
    return sums


def attn_back_kernel(
    meta, q, k, v, do, at_ref, pa, pb, normed, wqs, wks, wvs, wqk, wkk, wvk, hot, gain_attn, small_in, *rest, dims, base, buckets, pair_at, place
):
    before = [] if place[0] else [rest[0]]
    dq, dk, dv, send, keep, small, gain, strip, dsa, dsb, cat = rest[len(before) :]
    flip = meta[0]
    step = pl.program_id(0)
    th = normed.shape[1]
    strip[...] = jnp.zeros_like(strip)
    lane = lax.broadcasted_iota(jnp.int32, (1, PAIR), 1)
    minus = jnp.where(lane < 2, -1.0, 0.0).astype(BF)
    for kind, s, size, off in units_of(*dims):
        half = size // 2
        pref = pa if kind == 0 else pb
        ds_ref = dsa if kind == 0 else dsb
        q2, k2, v2, o2, a2 = (joined(ref, off, half) for ref in (q, k, v, do, at_ref))
        prod = o2.astype(F32) * a2.astype(F32)
        dvs, dks, dqs = [], [], []
        for h in range(2):
            mask = half_mask(h == 1)
            delta = jnp.sum(jnp.where((lane >= HEAD) == (h == 1), prod, 0.0), axis=1, keepdims=True)
            high = delta.astype(BF).astype(F32)
            cols = jnp.where(lane == 0, high, jnp.where(lane == 1, delta - high, 0.0)).astype(BF)
            va = jnp.concatenate([v2 * mask, jnp.broadcast_to(minus, (size, PAIR))], axis=1)
            oa = jnp.concatenate([o2, cols], axis=1)
            for c2 in range(size // 256):
                dp = dot(va, oa[256 * c2 : 256 * c2 + 256], 1, 1)
                for sub in range(2):
                    cb = 2 * c2 + sub
                    cs = slice(128 * cb, 128 * cb + 128)
                    ds = pref[h, s, :, cs].astype(F32) * dp[:, 128 * sub : 128 * sub + 128]
                    for kh in range(2):
                        at = pl.ds(strip_rows(flip, base, size, cb, kh), half)
                        strip[h, at, :] += ds[half * kh : half * kh + half]
                    ds_ref[h, :, cs] = ds.astype(BF)
            dvs.append(dot(pref[h, s], o2 * mask, 1, 0))
            dks.append(dot(ds_ref[h], q2 * mask, 1, 0))
            dqs.append(dot(ds_ref[h], k2 * mask, 0, 0))
        d_v = (dvs[0] + dvs[1]).astype(BF)
        d_k = (dks[0] + dks[1]).astype(BF)
        d_q = (dqs[0] + dqs[1]).astype(BF)
        for part in range(2):
            rows = slice(off, off + half)
            got = slice(part * half, part * half + half)
            dq[part, rows, :] = d_q[got]
            dk[part, rows, :] = d_k[got]
            dv[part, rows, :] = d_v[got]
            at = slice(part * th + off, part * th + off + half)
            cat[step, at, 0:128] = d_q[got]
            cat[step, at, 128:256] = d_k[got]
            cat[step, at, 256:384] = d_v[got]
    @pl.when(step == 0)
    def _():
        small[...] = small_in[...]

    sums = table_sums(strip, hot, base, buckets)
    row = lax.broadcasted_iota(jnp.int32, (small.shape[0], 128), 0) - (4 + 2 * pair_at(step, meta))
    small[:, 0:128] += jnp.where(row == 0, sums[0:1], jnp.where(row == 1, sums[1:2], 0.0))

    @pl.when(step == 1)
    def _():
        both = jnp.concatenate([cat[0], cat[1]], axis=1)
        value = dot(flat(normed), both, 0, 0)
        send[...] = value[:, :384].astype(BF)
        keep[...] = value[:, 384:].astype(BF)
        part = sum(
            value[:, 128 * i : 128 * i + 128] * w[...].astype(F32) for i, w in enumerate((wqs, wks, wvs, wqk, wkk, wvk))
        )
        for ref in before:
            part = part + ref[...]
        gain[...] = part
        if place[1]:
            high = part.astype(BF)
            low = (part - high.astype(F32)).astype(BF)
            ones = jnp.ones((16, 128), BF)
            line = (dot(ones, high, 1, 1) + dot(ones, low, 1, 1))[:1] / gain_attn[...]
            half = small.shape[1]
            small[0:1, :] += line[:, :half]
            small[1:2, :] += line[:, half:]


def spread(i, value, first, second):
    @pl.when(i == 0)
    def _():
        first[...] = value.reshape(first.shape)

    @pl.when(i == 1)
    def _():
        second[...] = value.reshape(second.shape)


def out_kernel(meta, low, w_back, hidden, give, out_a, out_b):
    i = pl.program_id(0)
    value = (hidden[0].astype(F32) + dot(low[0], w_back[...], 1, 0)).astype(BF)

    @pl.when(i < 2)
    def _():
        give[...] = value

    spread(i - 2, value, out_a, out_b)


def tokens_kernel(meta, *refs):
    wq, wk, wv, x_ref, d_hidden, gain = refs[9:15]
    outs = refs[15:]

    def columns(of):
        return jnp.concatenate([r[0, :, :PAIR] for r in of] + [r[0, :, PAIR:] for r in of], axis=1)

    dq, dk, dv = columns(refs[0:3]), columns(refs[3:6]), columns(refs[6:9])
    dn = dot(dq, wq[...], 1, 1) + dot(dk, wk[...], 1, 1) + dot(dv, wv[...], 1, 1)
    x = x_ref[0].astype(F32)
    r = lax.rsqrt(jnp.mean(x * x, axis=-1, keepdims=True) + EPS)
    gained = dn * gain[...]
    mean = jnp.mean(gained * x, axis=-1, keepdims=True)
    value = (d_hidden[0].astype(F32) + r * gained - x * (r * r * r * mean)).astype(BF)
    if len(outs) == 1:
        outs[0][...] = value
    else:
        spread(pl.program_id(0), value, *outs)


def swap(x, axis, bit):
    n = lax.axis_size(axis)
    return lax.ppermute(x, axis, [(i, i ^ bit) for i in range(n)])


TAIL = 32


class Piece:
    def __init__(self, parts, bits_left, carrier=False):
        self.parts, self.left, self.carrier, self.flat = parts, bits_left, carrier, 0

    def rows(self, cols):
        return self.flat or sum(t[0].shape[-2] * t[0].shape[-1] // cols for t in self.parts)

    def count(self, bits):
        return 1 << (len(self.left) - len(bits))


def blocks(x, bits):
    return x.reshape((2,) * bits + (x.shape[0] >> bits, x.shape[1]))


def masks_of(bits):
    return [tuple((m >> i) & 1 for i in range(len(bits))) for m in range(1 << len(bits))]


def shuttle(meta, cols, work, finals, after, small=((), ()), through=()):
    pieces, results = finals
    ins = []

    def slot(x):
        for i, y in enumerate(ins):
            if y is x:
                return i
        ins.append(x)
        return len(ins) - 1

    every = [piece for piece, _ in work] + pieces
    slots = []
    received = set()
    for piece in every:
        for terms in piece.parts:
            received |= {1 + slot(t[0] if piece.flat else t) for t in terms[1:]}
        slots.append([[(slot(t[0]), t[1]) if piece.flat else (slot(t), 0) for t in terms] for terms in piece.parts])
    small_at, tail_at = [slot(x) for x in small[0]], [slot(x) for x in small[1]]
    messages = {}
    for number, (piece, bits) in enumerate(work):
        for mask in masks_of(bits):
            wide = sum(flip << b for flip, b in zip(mask, bits))
            entry = messages.setdefault(wide, [0, False, []])
            entry[2].append((number, mask, entry[0]))
            entry[0] += piece.count(bits) * piece.rows(cols)
            entry[1] |= piece.carrier and wide > 0
    outs = [sds((rows + (TAIL if tail else 0), cols), BF) for rows, tail, _ in messages.values()]
    outs += [sds((spans[0][2], sum(s[4] for s in spans)), F32) for spans in results]
    if small_at:
        outs.append(sds(small[0][0].shape, F32))

    def kernel(meta, *refs):
        got, put = refs[: len(ins)], list(refs[len(ins) + len(through) : len(ins) + len(through) + len(outs)])
        row = meta[2]
        if small_at:
            total = sum(got[i][...] for i in small_at)
            for i in tail_at:
                end = got[i].shape[0]
                tail = got[i][end - TAIL : end, :].astype(F32)
                total = total + tail[: TAIL // 2] + tail[TAIL // 2 :]
            put[-1][...] = total
            high = total.astype(BF).astype(F32)
            tail = jnp.concatenate([high, total - high], axis=0).astype(BF)

        def take(piece, terms, index):
            if not piece.flat:
                return sum(got[i][index].astype(F32) for i, _ in terms)
            at = 0
            for bit in index:
                at = 2 * at + bit
            value = 0.0
            for i, low in terms:
                start = low + at * piece.flat
                value = value + got[i][pl.ds(pl.multiple_of(start, 16) if index else start, piece.flat), :].astype(F32)
            return value

        for (rows, tailed, entries), out in zip(messages.values(), put):
            for number, mask, low in entries:
                piece, bits = work[number]
                rest = [b for b in piece.left if b not in bits]
                for m in range(1 << len(rest)):
                    chosen = {b: (m >> i) & 1 for i, b in enumerate(rest)}
                    for b, flip in zip(bits, mask):
                        chosen[b] = ((row >> b) & 1) ^ flip
                    index = tuple(chosen[b] for b in reversed(piece.left))
                    for terms in slots[number]:
                        value = take(piece, terms, index).astype(BF)
                        high = value.shape[0]
                        for c in range(0, value.shape[1], cols):
                            out[low : low + high, :] = value[:, c : c + cols]
                            low += high
            if tailed:
                out[rows : rows + TAIL, :] = tail
        sums = [take(piece, slots[len(work) + i][0], ()) for i, piece in enumerate(pieces)]
        for spans, out in zip(results, put[len(messages) :]):
            low = 0
            for piece, r0, r, c0, c in spans:
                out[:, low : low + c] = sums[piece][r0 : r0 + r, c0 : c0 + c]
                low += c

    made = call(
        kernel,
        (1,),
        [whole(x.shape) for x in ins] + [pl.BlockSpec(memory_space=pl.ANY)] * len(through),
        [whole(x.shape) for x in outs] + [pl.BlockSpec(memory_space=pl.ANY)] * len(through),
        outs + [sds(x.shape, x.dtype) for x in through],
        nbytes=sum(x.size * 2 for x in ins),
        vmem=30,
        free=tuple(range(1, 1 + len(ins))),
        after=after,
        aliases={1 + len(ins) + i: len(outs) + i for i in range(len(through))},
    )(meta, *ins, *through)
    made, passed = list(made[: len(outs)]), made[len(outs) :]
    got = {wide: swap(x, "rows", wide) if wide else x for wide, x in zip(messages, made)}
    tails = []
    for number, (piece, bits) in enumerate(work):
        rows = piece.rows(cols)
        terms = []
        for wide, (_, tailed, entries) in messages.items():
            for other, _, low in entries:
                if other == number:
                    terms.append((got[wide], low))
                    if piece.carrier and tailed:
                        tails.append(got[wide])
        piece.parts, piece.flat = [terms], rows
        piece.left = tuple(b for b in piece.left if b not in bits)
    ends = len(messages) + len(results)
    return made[len(messages) : ends], (made[ends:], tails), [*made[: len(messages)], *passed]


def body(
    tokens_a, lengths_a, cotangent_a, tokens_b, lengths_b, cotangent_b,
    gain_attn, w_query, w_key, w_value, w_out, relative_bias_table, gain_ffn, w_in, w_back,
):
    nseq, nrows = lax.axis_size("seq"), lax.axis_size("rows")
    c = lax.axis_index("seq")
    width = tokens_a.shape[2]
    ff = w_in.shape[1]
    buckets, head_count = relative_bias_table.shape
    la, lb = tokens_a.shape[1] * nseq, tokens_b.shape[1] * nseq
    na, nb = tokens_a.shape[0] // nseq, tokens_b.shape[0] // nseq
    dims = (na, la, nb, lb)
    th = (na * la + nb * lb) // 2
    tokens = 2 * th
    base = la - 128
    strip_len = 2 * la - 128
    pairs = head_count // 2
    paired = nseq == 2 and nrows == 16

    me = c if paired else jnp.int32(0)
    flip = me
    meta = jnp.concatenate(
        [jnp.stack([flip, me, lax.axis_index("rows"), c]).astype(jnp.int32), lengths_a, lengths_b]
    )
    gain1, gain2 = gain_attn[None], gain_ffn[None]

    tile = th // 2
    per = 2
    row_grid = (2 * per,)
    by_row = lambda w: pl.BlockSpec((1, tile, w), lambda i, m: (i // per, i % per, 0))
    dense = 2 * tokens * width
    shape_a, shape_b = (na, la // 2, width), (nb, lb // 2, width)
    of_core = lambda shape: pl.BlockSpec(shape, lambda i, m: (m[1], 0, 0))
    of_other = lambda shape: pl.BlockSpec(shape, lambda i, m: (1 - m[1], 0, 0))
    cores = 2 if paired else 1
    all_a, all_b = (cores * na,) + shape_a[1:], (cores * nb,) + shape_b[1:]
    cut = na * la // 2

    def regroup(a, b):
        def one(x):
            got = lax.all_to_all(x, "seq", 0, 1, tiled=True)
            n, size, _ = got.shape
            return got.reshape(n, 2, size // 2, width).transpose(1, 0, 2, 3)

        whole_a, whole_b = one(a), one(b)
        rest = jnp.concatenate([whole_a[1].reshape(-1, width), whole_b[1].reshape(-1, width)], axis=0)
        return whole_a[0], whole_b[0], rest

    def ungroup(own_a, own_b, rest):
        def one(own, other, n, size):
            y = jnp.stack([own, other.reshape(own.shape)], axis=1).reshape(n, size, width)
            return lax.all_to_all(y, "seq", 1, 0, tiled=True)

        return one(own_a, rest[:cut], na, la), one(own_b, rest[cut:], nb, lb)

    received = pl.BlockSpec((tile, width), lambda i, m: (jnp.clip(i - per, 0, per - 1), 0))
    anywhere = pl.BlockSpec(memory_space=pl.ANY)
    copies = [pltpu.SemaphoreType.DMA((2 * (na + nb),))]
    in_vmem = pl.BlockSpec(memory_space=pltpu.VMEM)
    if paired:
        give = call(
            functools.partial(pick_kernel, dims=dims),
            (1,),
            [anywhere] * 4,
            [anywhere] * 2,
            [sds((th, width), BF)] * 2,
            scratch=[pltpu.VMEM((2, th, width), BF)] + copies * 2,
            nbytes=8 * th * width,
            vmem=8,
        )(meta, tokens_a, tokens_b, cotangent_a, cotangent_b)
        x_in = (tokens_a, tokens_b, swap(give[0], "seq", 1))
        g_in3 = (cotangent_a, cotangent_b, swap(give[1], "seq", 1))
    else:
        x_in = regroup(tokens_a, tokens_b)
        g_in3 = regroup(cotangent_a, cotangent_b)
    lane = jnp.arange(256, dtype=jnp.int32)
    back_rel = ((-96 - lane + 128 + 512) & 255) - 128
    hot = jnp.logical_and(
        bucket_of(back_rel, buckets)[:, None] == jnp.arange(128, dtype=jnp.int32)[None], back_rel[:, None] > -128
    ).astype(F32)

    at_once = 4
    rows_of_table = jnp.pad(
        relative_bias_table.T.reshape(head_count // at_once, at_once, buckets), ((0, 0), (0, 4), (0, 128 - buckets))
    )
    strip = call(
        functools.partial(strip_kernel, base=base, buckets=buckets),
        (head_count // at_once,),
        [pl.BlockSpec((1, 8, 128), lambda h, m: (h, 0, 0)), whole((256, 128))],
        pl.BlockSpec((at_once, strip_len, 128), lambda h, m: (h, 0, 0)),
        sds((head_count, strip_len, 128), F32),
        vmem=16,
        nbytes=4 * head_count * strip_len * 128,
    )(meta, rows_of_table, hot)

    tok = sds((2, th, width), BF)
    x, normed, q, k, v = call(
        qkv_kernel,
        row_grid,
        [of_core(shape_a), of_core(shape_b), received, whole((1, width))] + [whole((width, width))] * 3,
        [by_row(width)] * 5,
        [tok] * 5,
        vmem=30,
        free=(3, 5, 6, 7),
        flops=3 * dense * width,
        nbytes=10 * tokens * width,
        after=[strip],
    )(meta, *x_in, gain1, w_query, w_key, w_value)

    by_pair = pl.BlockSpec((2, th, PAIR), lambda p, m: (0, 0, p))
    pa_shape, pb_shape = (head_count, na, la, la), (head_count, nb, lb, lb)
    score_macs = head_count * (na * la * la + nb * lb * lb)
    pa, pb, attn, linv = call(
        functools.partial(attn_kernel, dims=dims, base=base, seqs_a=tokens_a.shape[0]),
        (pairs,),
        [by_pair] * 3 + [pl.BlockSpec((2, strip_len, 128), lambda p, m: (p, 0, 0))],
        [
            pl.BlockSpec((2, na, la, la), lambda p, m: (p, 0, 0, 0)),
            pl.BlockSpec((2, nb, lb, lb), lambda p, m: (p, 0, 0, 0)),
            by_pair,
            by_pair,
        ],
        [sds(pa_shape, BF), sds(pb_shape, BF), tok, tok],
        scratch=[pltpu.VMEM((2, th, 128), BF)],
        vmem=34,
        flops=score_macs * 256 * 4,
        nbytes=2 * score_macs,
    )(meta, q, k, v, strip)

    all_tok = whole((2, th, width))
    fb = 512
    half_w, half_f, nf, mixes = width // 2, ff // 2, ff // fb, 2 * per

    def unit_at(i, m):
        return (jnp.maximum(i - mixes, 0) + (1 - m[1]) * (nf // 2)) % nf

    def mix_at(i):
        return jnp.minimum(i, mixes - 1)

    mix_rows = pl.BlockSpec((1, tile, width), lambda i, m: (mix_at(i) // per, mix_at(i) % per, 0))
    unit_rows = pl.BlockSpec((fb, half_w), lambda i, m: (unit_at(i, m), 0))
    hidden, g, low, back_send, back_keep, in_send, in_keep, d_normed2 = call(
        functools.partial(ffn_kernel, mixes=mixes, chunk=th),
        (mixes + nf,),
        [
            mix_rows,
            mix_rows,
            whole((width, width)),
            whole((1, width)),
            of_core(shape_a),
            of_core(shape_b),
            received,
            pl.BlockSpec((width, fb), lambda i, m: (0, unit_at(i, m))),
            pl.BlockSpec((fb, width), lambda i, m: (unit_at(i, m), 0)),
        ],
        [
            mix_rows,
            mix_rows,
            pl.BlockSpec((2, th, fb), lambda i, m: (0, 0, unit_at(i, m))),
            unit_rows,
            unit_rows,
            pl.BlockSpec((width, fb), lambda i, m: (0, jnp.clip(i - mixes, 0, nf // 2 - 1))),
            pl.BlockSpec((width, fb), lambda i, m: (0, jnp.maximum(i - mixes - nf // 2, 0))),
            all_tok,
        ],
        [tok, tok, sds((2, th, ff), BF)]
        + [sds((ff, half_w), BF)] * 2
        + [sds((width, half_f), BF)] * 2
        + [tok],
        scratch=[
            pltpu.VMEM((2, th, width), BF),
            pltpu.VMEM((2, th, fb), BF),
            pltpu.VMEM((2, th, width), F32),
            pltpu.VMEM((2, th, width), BF),
        ],
        flops=dense * (5 * ff + width),
        nbytes=2 * tokens * ff,
        vmem=52,
        free=(3, 7, 8, 9),
    )(meta, attn, x, w_out, gain2, *g_in3, w_in, w_back)

    bit_count = nrows.bit_length() - 1
    low_bits, high_bits = (0, 1), tuple(range(2, bit_count))
    every_bit = tuple(range(bit_count))

    def pair_sum(keep, send):
        return [blocks(keep, bit_count), blocks(swap(send, "seq", 1), bit_count)]

    hold = []
    if paired:
        back = Piece([pair_sum(back_keep, back_send)], every_bit)
        inner = Piece([pair_sum(in_keep, in_send)], every_bit)
        hold = [back_send, in_send]

    small = sds((16, half_w), F32)
    none = ([], [])
    d_hidden, d_attn, small_sum, out_send, out_keep = call(
        hidden_kernel,
        row_grid,
        [
            by_row(width),
            by_row(width),
            by_row(width),
            whole((1, width)),
            whole((width, width)),
            by_row(width),
            by_row(width),
        ],
        [by_row(width), by_row(width), whole((16, half_w)), whole((width, half_w)), whole((width, half_w))],
        [tok, tok, small, sds((width, half_w), BF), sds((width, half_w), BF)],
        scratch=[pltpu.VMEM((width, width), F32), pltpu.VMEM((8, width), F32)],
        free=(5,),
        vmem=34,
        flops=dense * (ff + 2 * width),
        nbytes=2 * tokens * ff,
        after=hold,
    )(meta, d_normed2, hidden, g, gain2, w_out, attn, linv)

    group_count = pairs // 2
    groups, dqs, gains = [], [], []
    for gi in range(group_count):
        if paired:
            if gi == 0:
                out_sum = pair_sum(out_keep, out_send)
                _, _, hold = shuttle(meta, half_w, [(back, (0,)), (inner, (1,))], none, [d_attn])
                hold.append(out_send)
            elif gi == 1:
                first = [out_sum, pair_sum(*groups[0])]
                hold = [groups[0][1]]
            else:
                first = Piece(first, every_bit)
                _, _, hold = shuttle(
                    meta, half_w, [(back, (1,)), (inner, (2,)), (first, (0,))], none, [dqs[1][0]]
                )
                second = pair_sum(*groups[1])
                hold.append(groups[1][1])

        def pair_at(s, m, gi=gi):
            return jnp.where(s == 0, 1 - m[1], m[1]) * group_count + gi

        def half_at(s, m):
            return jnp.where(s == 0, 1 - m[1], m[1])

        by_cols = pl.BlockSpec((2, th, PAIR), lambda s, m, f=pair_at: (0, 0, f(s, m)))
        to_cols = pl.BlockSpec((2, th, PAIR), lambda s, m: (0, 0, half_at(s, m)))
        weight_cols = [
            pl.BlockSpec((width, PAIR), lambda s, m, f=pair_at, at=at: (0, f(at, m))) for at in (0, 0, 0, 1, 1, 1)
        ]
        dq, dk, dv, send, keep, small_sum, gain = call(
            functools.partial(
                attn_back_kernel, dims=dims, base=base, buckets=buckets, pair_at=pair_at,
                place=(gi == 0, gi == group_count - 1),
            ),
            (2,),
            [by_cols] * 5
            + [
                pl.BlockSpec((2, na, la, la), lambda s, m, f=pair_at: (f(s, m), 0, 0, 0)),
                pl.BlockSpec((2, nb, lb, lb), lambda s, m, f=pair_at: (f(s, m), 0, 0, 0)),
                all_tok,
            ]
            + weight_cols
            + [whole((256, 128)), whole((1, width)), whole((16, half_w))]
            + [whole((width, 128))] * len(gains),
            [to_cols] * 3
            + [
                whole((width, 3 * PAIR)),
                whole((width, 3 * PAIR)),
                whole((16, half_w)),
                whole((width, 128)),
            ],
            [sds((2, th, 2 * PAIR), BF)] * 3
            + [
                sds((width, 3 * PAIR), BF),
                sds((width, 3 * PAIR), BF),
                small,
                sds((width, 128), F32),
            ],
            scratch=[
                pltpu.VMEM((2, strip_len, 128), F32),
                pltpu.VMEM((2, la, la), BF),
                pltpu.VMEM((2, lb, lb), BF),
                pltpu.VMEM((2, tokens, 3 * PAIR), BF),
            ],
            free=(8, 9, 10, 11, 12, 13, 14),
            vmem=40,
        flops=score_macs * 256 * 8 // 3 + dense * width,
            nbytes=2 * score_macs // 3,
            after=hold,
        )(meta, q, k, v, d_attn, attn, pa, pb, normed, *([w_query, w_key, w_value] * 2), hot, gain1, small_sum, *gains)
        dqs.append((dq, dk, dv))
        gains = [gain]
        groups.append((keep, send))

    if paired:
        last = Piece([second, pair_sum(*groups[2])], every_bit, carrier=True)
        smalls = [small_sum, swap(small_sum, "seq", 1)]
        _, _, hold = shuttle(meta, half_w, [(back, (2,)), (inner, (0,)), (first, (1,))], none, [dqs[2][0]])
        hold += [groups[2][1], small_sum]

    def token_grads(part):
        of_part = lambda w: pl.BlockSpec((1, tile, w), lambda i, m: (part, i, 0))
        own = [of_core(shape_a), of_core(shape_b)]
        return call(
            tokens_kernel,
            (per,),
            [of_part(2 * PAIR)] * 9
            + [whole((width, width))] * 3
            + [of_part(width), of_part(width), whole((1, width))],
            [pl.BlockSpec((tile, width), lambda i, m: (i, 0))] if part else own,
            [sds((th, width), BF)] if part else [sds(all_a, BF), sds(all_b, BF)],
            vmem=24,
            free=(10, 11, 12),
            flops=3 * dense * width // 2,
            nbytes=7 * tokens * width,
            after=hold,
        )(meta, *(d[i] for i in range(3) for d in dqs), w_query, w_key, w_value, x, d_hidden, gain1)

    (grads1,) = token_grads(1)
    if paired:
        _, small_state, hold = shuttle(
            meta,
            half_w,
            [(back, (3,)), (inner, (3,)), (first, (2,)), (last, low_bits)],
            none,
            [grads1],
            (smalls, ()),
        )
        hold.append(grads1)
    out_rows = lambda w: pl.BlockSpec((1, tile, w), lambda i, m: (1 - i // per, i % per, 0))
    outs1, out_a, out_b = call(
        out_kernel,
        row_grid,
        [out_rows(ff), whole((ff, width)), out_rows(width)],
        [pl.BlockSpec((tile, width), lambda i, m: (jnp.minimum(i, per - 1), 0)), of_core(shape_a), of_core(shape_b)],
        [sds((th, width), BF), sds(all_a, BF), sds(all_b, BF)],
        vmem=30,
        flops=dense * ff,
        nbytes=2 * tokens * ff,
        after=hold,
    )(meta, low, w_back, hidden)
    if paired:
        r = width // nrows
        in_back = [(0, 0, ff // nrows, 0, half_w)]
        in_in = [(1, r * j, r, 0, half_w) for j in range(half_f // half_w)]
        (g_back, g_in), small_state, hold = shuttle(
            meta,
            half_w,
            [(first, (3,)), (last, high_bits)],
            ([back, inner], [in_back, in_in]),
            [],
            small_state,
            [grads1, outs1],
        )
        grads1_got, outs1_got = (swap(y, "seq", 1) for y in hold[-2:])
    grad_a, grad_b = token_grads(0)

    if paired:
        def of(col):
            at = [(0, r), (1, 0), (1, r)]
            return [(piece, row, r, PAIR * col, PAIR) for piece, row in at]

        (g_out, g_q, g_k, g_v), ((small_all,), _), _ = shuttle(
            meta,
            half_w,
            [],
            ([first, last], [[(0, 0, r, 0, half_w)], of(0), of(1), of(2)]),
            [grad_a],
            small_state,
        )
        out_a, out_b, grad_a, grad_b = call(
            functools.partial(place_kernel, dims=dims),
            (1,),
            [in_vmem] * 2 + [anywhere] * 4,
            [anywhere] * 4,
            [sds(all_a, BF), sds(all_b, BF)] * 2,
            scratch=copies,
            vmem=8,
            free=(1, 2),
            aliases={3: 0, 4: 1, 5: 2, 6: 3},
        )(meta, outs1_got, grads1_got, out_a, out_b, grad_a, grad_b)
    else:
        out_a, out_b = ungroup(out_a, out_b, outs1)
        grad_a, grad_b = ungroup(grad_a, grad_b, grads1)
        small_all = lax.psum(small_sum, ("rows", "seq"))

        def reduce(x):
            x = lax.psum_scatter(x.astype(F32), "rows", scatter_dimension=0, tiled=True)
            return lax.psum_scatter(x.astype(BF), "seq", scatter_dimension=1, tiled=True).astype(F32)

        def both(keep, send):
            return reduce(jnp.concatenate([keep, send], axis=1))

        g_back, g_in, g_out = both(back_keep, back_send), both(in_keep, in_send), both(out_keep, out_send)
        g_q, g_k, g_v = (
            reduce(
                jnp.concatenate([part[s][:, PAIR * i : PAIR * i + PAIR] for s in range(2) for part in groups], axis=1)
            )
            for i in range(3)
        )
    gain_one, gain_two = small_all[0:2].reshape(width), small_all[2:4].reshape(width)
    table_sum = small_all[4 : 4 + head_count, :buckets].T
    return (
        out_a, out_b, grad_a, grad_b, gain_one, g_q, g_k, g_v, g_out, table_sum, gain_two, g_in, g_back,
    )


def solution(mesh):
    split = P("rows", "seq", None)
    placed = (split, P("rows"), split, split, P("rows"), split) + (P(),) * 9
    shard = P("rows", "seq")
    return jax.shard_map(
        body,
        mesh=mesh,
        in_specs=placed,
        out_specs=(split, split, split, split, P(), shard, shard, shard, shard, P(), P(), shard, shard),
        check_vma=False,
    )
```
